32 devices in a mesh: section: 2 (over x), head: 4 (over y, core), dp: 4 (over z).
Axes of the slice: x: 2, y: 2, z: 4, core: 2. Of those that a mesh axis runs over, the one named last changes fastest.
Arguments:
- inputs: bfloat16 [8, 1024, 1024], P('dp', 'head'), may hold values from -6 to 6
- memory: bfloat16 [2, 8, 256, 1024], P('section', 'dp', 'head'), may hold values from -6 to 6
- value_routes: int32 [2, 8, 1280, 4, 2], P('section', 'dp', None, 'head'), may hold values from 0 to 4, all different within a row
- out_routes: int32 [2, 8, 1024, 4, 2], P('section', 'dp', None, 'head'), may hold values from 0 to 4, all different within a row
- ln1_gain: float32 [2, 1024], P('section'), may hold values from 0.5 to 1.5
- ln1_bias: float32 [2, 1024], P('section'), may hold values from -1 to 1
- query_weight: bfloat16 [2, 4, 1024, 112], P('section', 'head'), may hold values from -0.1875 to 0.1875
- key_weight: bfloat16 [2, 4, 1024, 112], P('section', 'head'), may hold values from -0.1875 to 0.1875
- value_weight: bfloat16 [2, 4, 1024, 560], P('section', 'head'), may hold values from -0.1875 to 0.1875
- value_router: bfloat16 [2, 4, 1024, 5], P('section', 'head'), may hold values from -0.125 to 0.125
- out_router: bfloat16 [2, 4, 1024, 5], P('section', 'head'), may hold values from -0.125 to 0.125
- output_weight: bfloat16 [2, 4, 560, 1024], P('section', 'head'), may hold values from -6 to 6
- ln2_gain: float32 [2, 1024], P('section'), may hold values from 0.5 to 1.5
- ln2_bias: float32 [2, 1024], P('section'), may hold values from -1 to 1
- up_weight: bfloat16 [2, 1024, 4096], P('section', None, 'head'), may hold values from -0.1875 to 0.1875
- up_bias: float32 [2, 4096], P('section', 'head'), may hold values from -1.5 to 1.5
- down_weight: bfloat16 [2, 4096, 1024], P('section', 'head'), may hold values from -0.09375 to 0.09375
- down_bias: float32 [2, 1024], P('section'), may hold values from -1 to 1
- out_cot: bfloat16 [8, 1024, 1024], P('dp', 'head'), may hold values from -6 to 6
Outputs:
- layer_out: bfloat16 [2, 8, 1024, 1024], P('section', 'dp', 'head')
- input_grad: bfloat16 [2, 8, 1024, 1024], P('section', 'dp', 'head')
- ln1_gain_grad: float32 [2, 1024], P('section')
- ln1_bias_grad: float32 [2, 1024], P('section')
- query_grad: float32 [2, 4, 1024, 112], P('section', 'head')
- key_grad: float32 [2, 4, 1024, 112], P('section', 'head')
- value_grad: float32 [2, 4, 1024, 560], P('section', 'head')
- value_router_grad: float32 [2, 4, 1024, 5], P('section', 'head')
- out_router_grad: float32 [2, 4, 1024, 5], P('section', 'head')
- output_grad: float32 [2, 4, 560, 1024], P('section', 'head')
- ln2_gain_grad: float32 [2, 1024], P('section')
- ln2_bias_grad: float32 [2, 1024], P('section')
- up_grad: float32 [2, 1024, 4096], P('section', None, 'head')
- up_bias_grad: float32 [2, 4096], P('section', 'head')
- down_grad: float32 [2, 4096, 1024], P('section', 'head')
- down_bias_grad: float32 [2, 1024], P('section')
The draws below stay inside these ranges and needn't reach their ends.
Inputs may be any that keep to these rules, and one draw needn't show every extreme that they name: `value_routes`: the 2 experts of a token and head are distinct, and every expert is named somewhere. `out_routes`: the 2 experts of a token and head are distinct, and every expert is named somewhere.
All inputs are finite; a program needn't handle non-finite values.
Results may differ from the reference program's by a relative error of at most 0.03.
Values may be sent and summed in bfloat16 or wider, within the bound.
No kernel may reach another device: no remote copies, remote signals or barrier semaphores. Data moves between devices by JAX's collectives and lax.ppermute only.
A program may use at most 320 MiB of HBM per device.

```python
import jax
import jax.numpy as jnp
from jax import lax

D = 1024
HEADS = 4
HD = 112
EXPERTS = 5
FF = 4096
TOPK = 2
SEQ_LEN = 1024
MEM = 256
LAYERS = 2
SEQS = 8


def block_levels(key, dims, pieces, smallest, high):
    loudness, own = 1.0, jax.random.fold_in(key, 6)
    for position, parts in pieces:
        steps = jnp.exp(jax.random.uniform(jax.random.fold_in(own, position), (parts,), jnp.float32, smallest / len(pieces), high / len(pieces)))
        loudness = loudness * jnp.repeat(steps, dims[position] // parts).reshape([-1 if axis == position else 1 for axis in range(len(dims))])
    return loudness


def choose_distinct(own_key, rows, number_of, top, lift):
    order = jax.random.permutation(jax.random.fold_in(own_key, 1), number_of)
    boost = order
    for power in range(3):
        boost = boost * boost // number_of
    boost = boost * lift // number_of
    chance = jax.random.randint(jax.random.fold_in(own_key, 2), (rows, number_of), 0, 4096) + boost
    holders = jax.random.permutation(jax.random.fold_in(own_key, 3), rows)[jnp.arange(number_of) % rows]
    chance = jnp.where(jnp.arange(rows)[:, None] == holders[None, :], 1 << 14, chance)
    merit = chance * number_of + jnp.arange(number_of)
    return lax.top_k(merit.astype(jnp.int32), top)[1].astype(jnp.int32)


def gaussian(rng, extent, scale, bound, cuts=(), held_as=jnp.bfloat16):
    array = scale * jax.random.normal(rng, extent, jnp.float32)
    if cuts:
        array = array * block_levels(rng, extent, cuts, -0.22, 0.18)
    return jnp.clip(array, -bound, bound).astype(held_as)


def setup_inputs(seed: int = 0) -> dict:
    splits = jax.random.split(jax.random.key(seed), 20)
    inputs = gaussian(splits[0], (SEQS, SEQ_LEN, D), 1.0, 6.0, ((0, 4), (1, 4)))
    memory = gaussian(splits[1], (LAYERS, SEQS, MEM, D), 1.0, 6.0, ((0, 2), (1, 4), (2, 4)))
    value_routes = choose_distinct(splits[2], LAYERS * SEQS * (MEM + SEQ_LEN) * HEADS, EXPERTS, TOPK, 0).reshape((LAYERS, SEQS, MEM + SEQ_LEN, HEADS, TOPK))
    out_routes = choose_distinct(splits[3], LAYERS * SEQS * SEQ_LEN * HEADS, EXPERTS, TOPK, 0).reshape((LAYERS, SEQS, SEQ_LEN, HEADS, TOPK))
    ln1_gain = jnp.clip(1.0 + 0.1 * jax.random.normal(splits[4], (LAYERS, D), jnp.float32), 0.5, 1.5)
    ln1_bias = gaussian(splits[5], (LAYERS, D), 0.2, 1.0, ((0, 2),), jnp.float32)
    query_weight = gaussian(splits[6], (LAYERS, HEADS, D, HD), D ** -0.5, 0.1875, ((0, 2), (1, 4)))
    key_weight = gaussian(splits[7], (LAYERS, HEADS, D, HD), D ** -0.5, 0.1875, ((0, 2), (1, 4)))
    value_weight = gaussian(splits[8], (LAYERS, HEADS, D, EXPERTS * HD), D ** -0.5, 0.1875, ((0, 2), (1, 4)))
    value_router = gaussian(splits[9], (LAYERS, HEADS, D, EXPERTS), (2 * D) ** -0.5, 0.125, ((0, 2), (1, 4)))
    out_router = gaussian(splits[10], (LAYERS, HEADS, D, EXPERTS), (2 * D) ** -0.5, 0.125, ((0, 2), (1, 4)))
    output_weight = gaussian(splits[11], (LAYERS, HEADS, EXPERTS * HD, D), 1 ** -0.5, 6.0, ((0, 2), (1, 4)))
    ln2_gain = jnp.clip(1.0 + 0.1 * jax.random.normal(splits[12], (LAYERS, D), jnp.float32), 0.5, 1.5)
    ln2_bias = gaussian(splits[13], (LAYERS, D), 0.2, 1.0, ((0, 2),), jnp.float32)
    up_weight = gaussian(splits[14], (LAYERS, D, FF), D ** -0.5, 0.1875, ((0, 2), (2, 4)))
    up_bias = gaussian(splits[15], (LAYERS, FF), 0.3, 1.5, ((0, 2), (1, 4)), jnp.float32)
    down_weight = gaussian(splits[16], (LAYERS, FF, D), FF ** -0.5, 0.09375, ((0, 2), (1, 4)))
    down_bias = gaussian(splits[17], (LAYERS, D), 0.2, 1.0, ((0, 2),), jnp.float32)
    out_cot = gaussian(splits[18], (SEQS, SEQ_LEN, D), 1.0, 6.0, ((0, 4), (1, 4)))
    return dict(inputs=inputs, memory=memory, value_routes=value_routes, out_routes=out_routes, ln1_gain=ln1_gain, ln1_bias=ln1_bias, query_weight=query_weight, key_weight=key_weight, value_weight=value_weight, value_router=value_router, out_router=out_router, output_weight=output_weight, ln2_gain=ln2_gain, ln2_bias=ln2_bias, up_weight=up_weight, up_bias=up_bias, down_weight=down_weight, down_bias=down_bias, out_cot=out_cot)


@jax.custom_vjp
def low(v):
    return lax.optimization_barrier(v.astype(jnp.bfloat16)).astype(jnp.float32)

@jax.custom_vjp
def low_back(v):
    return v

def low_keep(v):
    return (low(v), None)

def low_pass(kept, grad):
    return (grad,)

def back_keep(v):
    return (v, None)

def back_low(kept, grad):
    return (low(grad),)
low.defvjp(low_keep, low_pass)
low_back.defvjp(back_keep, back_low)
norm_eps = 1e-05
precise = lax.Precision.HIGHEST
masked_score = -1e+30

def normalize(row_data, gain_vec, shift_vec):
    average = lax.optimization_barrier(jnp.mean(row_data, axis=-1, keepdims=True))
    centred = row_data - average
    variance = lax.optimization_barrier(jnp.mean(centred * centred, axis=-1, keepdims=True))
    return centred * lax.rsqrt(variance + norm_eps) * gain_vec + shift_vec

def choose(route_ids):
    expert_ids = jnp.arange(EXPERTS, dtype=jnp.int32)
    picked = lax.optimization_barrier(jnp.sum((route_ids[..., None] == expert_ids).astype(jnp.float32), axis=2))
    return jnp.transpose(picked, (1, 0, 2))

def sequence_layer(weights, layer_in, memory_rows, value_ids, out_ids):
    norm1_gain, norm1_shift, query_w, key_w, value_w, vroute_w, oroute_w, output_w, norm2_gain, norm2_shift, up_w, up_shift, down_w, down_shift = weights
    whole = jnp.concatenate([memory_rows, layer_in], axis=0)
    normed = low(normalize(whole, norm1_gain, norm1_shift))
    query_rows = normed[MEM:]
    query_low = low(low_back(jnp.einsum('td,hde->hte', query_rows, query_w, precision=precise)))
    key_low = low(low_back(jnp.einsum('td,hde->hte', normed, key_w, precision=precise)))
    expert_vals = low_back(jnp.einsum('td,hdf->htf', normed, value_w, precision=precise))
    expert_vals = expert_vals.reshape(HEADS, MEM + SEQ_LEN, EXPERTS, HD)
    value_gate = jax.nn.sigmoid(low_back(jnp.einsum('td,hde->hte', normed, vroute_w, precision=precise))) * choose(value_ids)
    value_low = low(low_back(lax.optimization_barrier(jnp.sum(expert_vals * value_gate[..., None], axis=2))))
    scores = low_back(jnp.einsum('hqe,hke->hqk', query_low, key_low, precision=precise) * HD ** (-0.5))
    query_pos = MEM + jnp.arange(SEQ_LEN, dtype=jnp.int32)[:, None]
    key_pos = jnp.arange(MEM + SEQ_LEN, dtype=jnp.int32)[None, :]
    scores = jnp.where(key_pos <= query_pos, scores, masked_score)
    row_top = lax.optimization_barrier(jnp.max(scores, axis=-1, keepdims=True))
    exponent = jnp.exp(scores - row_top)
    chance = low(low_back(exponent / lax.optimization_barrier(jnp.sum(exponent, axis=-1, keepdims=True))))
    attended = low_back(jnp.einsum('hqk,hke->hqe', chance, value_low, precision=precise))
    out_gate = jax.nn.sigmoid(low_back(jnp.einsum('td,hde->hte', query_rows, oroute_w, precision=precise))) * choose(out_ids)
    mixed = low(low_back((attended[:, :, None, :] * out_gate[..., None]).reshape(HEADS, SEQ_LEN, EXPERTS * HD)))
    attn_out = low_back(jnp.einsum('htf,hfd->td', mixed, output_w, precision=precise))
    hidden = layer_in + attn_out
    normed2 = low(normalize(hidden, norm2_gain, norm2_shift))
    upper = low_back(jnp.dot(normed2, up_w, precision=precise) + up_shift)
    active = low(low_back(jax.nn.gelu(upper)))
    ffn_out = low_back(jnp.dot(active, down_w, precision=precise))
    return low(hidden + ffn_out + down_shift)

def run_layer(weights, layer_in, memory_rows, value_ids, out_ids):
    checked = jax.checkpoint(sequence_layer)
    return lax.map(lambda bundle: checked(weights, bundle[0], bundle[1], bundle[2], bundle[3]), (layer_in, memory_rows, value_ids, out_ids))

def reference(inputs, memory, value_routes, out_routes, ln1_gain, ln1_bias, query_weight, key_weight, value_weight, value_router, out_router, output_weight, ln2_gain, ln2_bias, up_weight, up_bias, down_weight, down_bias, out_cot):
    stacked = (ln1_gain, ln1_bias, query_weight, key_weight, value_weight, value_router, out_router, output_weight, ln2_gain, ln2_bias, up_weight, up_bias, down_weight, down_bias)
    floats = tuple((member.astype(jnp.float32) for member in stacked))
    first_w = tuple((member[0] for member in floats))
    second_w = tuple((member[1] for member in floats))
    memory_f = memory.astype(jnp.float32)
    first_out, first_back = jax.vjp(lambda params, rows_in: run_layer(params, rows_in, memory_f[0], value_routes[0], out_routes[0]), first_w, inputs.astype(jnp.float32))
    second_out, second_back = jax.vjp(lambda params, rows_in: run_layer(params, rows_in, memory_f[1], value_routes[1], out_routes[1]), second_w, first_out)
    second_grads, middle_grad = second_back(out_cot.astype(jnp.float32))
    middle_grad = low(middle_grad)
    first_grads, first_grad = first_back(middle_grad)
    grads = tuple((jnp.stack([one_grad, two_grad]) for one_grad, two_grad in zip(first_grads, second_grads)))
    layer_out = jnp.stack([first_out, second_out]).astype(jnp.bfloat16)
    input_grad = jnp.stack([first_grad, middle_grad]).astype(jnp.bfloat16)
    return (layer_out, input_grad, grads[0], grads[1], grads[2], grads[3], grads[4], grads[5], grads[6], grads[7], grads[8], grads[9], grads[10], grads[11], grads[12], grads[13])
```

```python
import functools

import jax
import jax.numpy as jnp
from jax import lax
from jax.experimental import pallas as pl
from jax.experimental.pallas import tpu as pltpu
from jax.sharding import PartitionSpec as P

norm_eps = 1e-05
masked_score = -1e30
lanes = 128
bf16 = jnp.bfloat16
f32 = jnp.float32
gelu_c = 0.7978845608028654
gelu_a = 0.044715

core_pairs = [(0, 1), (1, 0), (2, 3), (3, 2)]
chip_pairs = [(0, 2), (2, 0), (1, 3), (3, 1)]
vmem_bytes = 50 * 1024 * 1024


def dot(a, b):
    return lax.dot_general(a, b, (((1,), (0,)), ((), ())), preferred_element_type=f32)


def dot_t(a, b):
    return lax.dot_general(a, b, (((1,), (1,)), ((), ())), preferred_element_type=f32)


def t_dot(a, b):
    return lax.dot_general(a, b, (((0,), (0,)), ((), ())), preferred_element_type=f32)


def params(**more):
    return pltpu.CompilerParams(vmem_limit_bytes=vmem_bytes, **more)


def whole_spec(shape):
    return pl.BlockSpec(shape, lambda *_: (0,) * len(shape))


def cost(flops, nbytes, trans=0):
    return pl.CostEstimate(flops=int(flops), bytes_accessed=int(nbytes), transcendentals=int(trans))


def to_core(a):
    return lax.ppermute(a, "head", core_pairs)


def to_chip(a):
    return lax.ppermute(a, "head", chip_pairs)


def swap_section(a):
    return lax.ppermute(a, "section", [(0, 1), (1, 0)])


def gather_slots(own):
    from_chip = to_chip(own)
    from_core = to_core(own)
    from_both = to_core(from_chip)
    return [own, from_core, from_chip, from_both]


def scatter_slots(parts):
    from_core_far = to_core(parts[3])
    from_core = to_core(parts[1])
    far = (parts[2].astype(f32) + from_core_far.astype(f32)).astype(bf16)
    return parts[0], from_core, to_chip(far)


def norm_rows(x, gain, shift):
    average = jnp.mean(x, axis=-1, keepdims=True)
    centred = x - average
    variance = jnp.mean(centred * centred, axis=-1, keepdims=True)
    return centred * lax.rsqrt(variance + norm_eps) * gain + shift


def norm_kernel(x_ref, gain_ref, shift_ref, out_ref):
    out_ref[...] = norm_rows(x_ref[...].astype(f32), gain_ref[...], shift_ref[...]).astype(bf16)


def norm_only(x, gain, shift):
    return pl.pallas_call(
        norm_kernel,
        out_shape=jax.ShapeDtypeStruct(x.shape, bf16),
        compiler_params=params(),
        cost_estimate=cost(x.size * 8, x.size * 4),
        name="norm_only",
    )(x, gain, shift)


def add_norm_kernel(x_ref, a_ref, b_ref, c_ref, add_ref, gain_ref, shift_ref, sum_ref, out_ref):
    total = x_ref[...].astype(f32) + (a_ref[...].astype(f32) + b_ref[...].astype(f32) + c_ref[...].astype(f32))
    total = total + add_ref[...]
    sum_ref[...] = total.astype(sum_ref.dtype)
    total = sum_ref[...].astype(f32)
    out_ref[...] = norm_rows(total, gain_ref[...], shift_ref[...]).astype(bf16)


def add_norm(x, terms, add, gain, shift, sum_type):
    return pl.pallas_call(
        add_norm_kernel,
        out_shape=(jax.ShapeDtypeStruct(x.shape, sum_type), jax.ShapeDtypeStruct(x.shape, bf16)),
        compiler_params=params(),
        cost_estimate=cost(x.size * 12, x.size * 14),
        name="add_norm",
    )(x, *terms, add, gain, shift)


def norm_back_kernel(x_ref, a_ref, b_ref, c_ref, gain_ref, more_ref, dx_ref, low_ref, small_ref):
    x = x_ref[...].astype(f32)
    grad = a_ref[...].astype(f32) + b_ref[...].astype(f32) + c_ref[...].astype(f32)
    average = jnp.mean(x, axis=-1, keepdims=True)
    centred = x - average
    variance = jnp.mean(centred * centred, axis=-1, keepdims=True)
    scale = lax.rsqrt(variance + norm_eps)
    unit = centred * scale
    wide = grad * gain_ref[...]
    mean_wide = jnp.mean(wide, axis=-1, keepdims=True)
    mean_unit = jnp.mean(wide * unit, axis=-1, keepdims=True)
    more = more_ref[...].astype(f32)
    dx = more + scale * (wide - mean_wide - unit * mean_unit)
    dx_ref[...] = dx
    low_ref[...] = dx.astype(bf16)
    small_ref[0:1, :] = jnp.sum(grad * unit, axis=0, keepdims=True)
    small_ref[1:2, :] = jnp.sum(grad, axis=0, keepdims=True)
    small_ref[2:3, :] = jnp.sum(more, axis=0, keepdims=True)
    small_ref[3:8, :] = jnp.zeros((5, x.shape[1]), f32)


def norm_back(x, terms, gain, more):
    return pl.pallas_call(
        norm_back_kernel,
        out_shape=(
            jax.ShapeDtypeStruct(x.shape, f32),
            jax.ShapeDtypeStruct(x.shape, bf16),
            jax.ShapeDtypeStruct((8, x.shape[1]), f32),
        ),
        compiler_params=params(),
        cost_estimate=cost(x.size * 20, x.size * 20),
        name="norm_back",
    )(x, *terms, gain, more)


def norm_back_small_kernel(x_ref, a_ref, b_ref, c_ref, small_ref):
    x = x_ref[...].astype(f32)
    grad = a_ref[...].astype(f32) + b_ref[...].astype(f32) + c_ref[...].astype(f32)
    average = jnp.mean(x, axis=-1, keepdims=True)
    centred = x - average
    variance = jnp.mean(centred * centred, axis=-1, keepdims=True)
    unit = centred * lax.rsqrt(variance + norm_eps)
    small_ref[0:1, :] = jnp.sum(grad * unit, axis=0, keepdims=True)
    small_ref[1:2, :] = jnp.sum(grad, axis=0, keepdims=True)
    small_ref[2:8, :] = jnp.zeros((6, x.shape[1]), f32)


def norm_back_small(x, terms):
    return pl.pallas_call(
        norm_back_small_kernel,
        out_shape=jax.ShapeDtypeStruct((8, x.shape[1]), f32),
        compiler_params=params(),
        cost_estimate=cost(x.size * 10, x.size * 8),
        name="norm_back_small",
    )(x, *terms)


def pick_slot(slot, refs, target):
    for number, ref in enumerate(refs):

        @pl.when(slot == number)
        def _(ref=ref):
            target[...] = ref[...]


def attn_fwd_kernel(
    experts,
    head_width,
    me_ref,
    mem_ref,
    p0_ref,
    p1_ref,
    p2_ref,
    p3_ref,
    w_ref,
    wo_ref,
    mask_ref,
    out_ref,
    normed_ref,
    q_ref,
    k_ref,
    v_ref,
    ev_ref,
    gate_ref,
    att_ref,
    mixed_ref,
    rows_s,
    k_s,
    v_s,
    mask_s,
):
    step = pl.program_id(0)
    me = me_ref[0]
    block = rows_s.shape[0]
    wide = experts * lanes
    quarter = block // 4

    @pl.when(step == 0)
    def _():
        rows_s[...] = mem_ref[...]
        for slot in range(4):
            start = pl.multiple_of((me ^ slot) * quarter, quarter)
            mask_s[slot * quarter : (slot + 1) * quarter, :] = mask_ref[pl.ds(start, quarter), :]

    @pl.when(step > 0)
    def _():
        pick_slot((step - 1) ^ me, (p0_ref, p1_ref, p2_ref, p3_ref), rows_s)
        mask_s[...] = mask_ref[pl.ds(pl.multiple_of(step * block, block), block), :]

    x = rows_s[...]
    normed_ref[...] = x
    proj = dot(x, w_ref[...])
    gate = jax.nn.sigmoid(proj[:, wide : wide + lanes]) * mask_s[...]
    value = jnp.zeros((block, lanes), f32)
    for j in range(experts):
        value = value + gate[:, j : j + 1] * proj[:, j * lanes : (j + 1) * lanes]
    start = pl.multiple_of(step * block, block)
    keys = proj[:, wide + lanes : wide + 2 * lanes].astype(bf16)
    value = value.astype(bf16)
    k_s[pl.ds(start, block), :] = keys
    v_s[pl.ds(start, block), :] = value
    k_ref[...] = keys
    v_ref[...] = value
    ev_ref[...] = proj[:, :wide].astype(bf16)
    queries = proj[:, wide + 2 * lanes :].astype(bf16)
    q_ref[...] = queries

    @pl.when(step == 0)
    def _():
        gate_ref[...] = gate

    scale = head_width ** (-0.5)
    for count in range(1, 5):

        @pl.when(step == count)
        def _(count=count):
            span = (count + 1) * block
            scores = dot_t(queries, k_s[0:span, :]) * scale
            row = lax.broadcasted_iota(jnp.int32, (block, block), 0)
            col = lax.broadcasted_iota(jnp.int32, (block, block), 1)
            last = jnp.where(col <= row, scores[:, span - block :], masked_score)
            scores = jnp.concatenate([scores[:, : span - block], last], axis=1)
            top = jnp.max(scores, axis=-1, keepdims=True)
            exponent = jnp.exp(scores - top)
            total = jnp.sum(exponent, axis=-1, keepdims=True)
            probs = (exponent * (1.0 / total)).astype(bf16)
            attended = dot(probs, v_s[0:span, :])
            att_ref[...] = attended
            lane = lax.broadcasted_iota(jnp.int32, (block, lanes), 1)
            gate_ref[...] = jnp.where(lane == 2 * experts, top + jnp.log(total), gate)
            mixed = jnp.concatenate(
                [(gate[:, experts + j : experts + j + 1] * attended).astype(bf16) for j in range(experts)], axis=1
            )
            mixed_ref[...] = mixed
            out_ref[0] = dot(mixed, wo_ref[...]).astype(bf16)


def attn_fwd(me, mem, slots, w, wo, mask, experts, head_width):
    block, width = slots[0].shape
    total = 5 * block
    wide = experts * lanes
    later = lambda i, me_ref: (jnp.maximum(i - 1, 0), 0)
    every = lambda i, me_ref: (i, 0)
    shapes = lambda rows, cols, kind: jax.ShapeDtypeStruct((rows, cols), kind)
    grid_spec = pltpu.PrefetchScalarGridSpec(
        num_scalar_prefetch=1,
        grid=(5,),
        in_specs=[whole_spec((block, width))] * 5
        + [whole_spec(w.shape), whole_spec(wo.shape), whole_spec(mask.shape)],
        out_specs=[
            pl.BlockSpec((1, block, width), lambda i, me_ref: (jnp.maximum(i - 1, 0) ^ me_ref[0], 0, 0)),
            pl.BlockSpec((block, width), every),
            pl.BlockSpec((block, lanes), every),
            pl.BlockSpec((block, lanes), every),
            pl.BlockSpec((block, lanes), every),
            pl.BlockSpec((block, wide), every),
            pl.BlockSpec((block, lanes), every),
            pl.BlockSpec((block, lanes), later),
            pl.BlockSpec((block, wide), later),
        ],
        scratch_shapes=[
            pltpu.VMEM((block, width), bf16),
            pltpu.VMEM((total, lanes), bf16),
            pltpu.VMEM((total, lanes), bf16),
            pltpu.VMEM((block, lanes), f32),
        ],
    )
    return pl.pallas_call(
        functools.partial(attn_fwd_kernel, experts, head_width),
        grid_spec=grid_spec,
        out_shape=(
            jax.ShapeDtypeStruct((4, block, width), bf16),
            shapes(total, width, bf16),
            shapes(total, lanes, bf16),
            shapes(total, lanes, bf16),
            shapes(total, lanes, bf16),
            shapes(total, wide, bf16),
            shapes(total, lanes, f32),
            shapes(4 * block, lanes, f32),
            shapes(4 * block, wide, bf16),
        ),
        compiler_params=params(dimension_semantics=("arbitrary",)),
        cost_estimate=cost(2 * total * width * w.shape[1] + 2 * 4 * block * wide * width, 20 * 1024 * 1024, total * total),
        name="attn_fwd",
    )(me, mem, *slots, w, wo, mask)


def attn_bwd_kernel(
    experts,
    head_width,
    me_ref,
    d0_ref,
    d1_ref,
    d2_ref,
    d3_ref,
    w_ref,
    wo_ref,
    q_ref,
    k_ref,
    v_ref,
    ev_ref,
    gate_ref,
    att_ref,
    ngs_ref,
    ngm_ref,
    dproj_ref,
    da_ref,
    rows_s,
    dk_s,
    dv_s,
    dq_s,
    dlog_s,
):
    step = pl.program_id(0)
    me = me_ref[0]
    here = 4 - step
    block = rows_s.shape[0]
    wide = experts * lanes
    scale = head_width ** (-0.5)
    gate = gate_ref[...]
    lane = lax.broadcasted_iota(jnp.int32, (block, lanes), 1)

    @pl.when(step == 0)
    def _():
        dk_s[...] = jnp.zeros_like(dk_s)
        dv_s[...] = jnp.zeros_like(dv_s)

    @pl.when(here == 0)
    def _():
        dq_s[...] = jnp.zeros_like(dq_s)
        dlog_s[...] = jnp.zeros_like(dlog_s)

    for count in range(1, 5):

        @pl.when(here == count)
        def _(count=count):
            pick_slot((count - 1) ^ me, (d0_ref, d1_ref, d2_ref, d3_ref), rows_s)
            rows = rows_s[...]
            da_ref[...] = rows
            mixed_grad = dot_t(rows, wo_ref[...])
            attended = att_ref[...]
            att_grad = jnp.zeros((block, lanes), f32)
            logit_grad = jnp.zeros((block, lanes), f32)
            for j in range(experts):
                part = mixed_grad[:, j * lanes : (j + 1) * lanes]
                att_grad = att_grad + gate[:, experts + j : experts + j + 1] * part
                inner = jnp.sum(part * attended, axis=-1, keepdims=True)
                logit_grad = jnp.where(lane == experts + j, inner, logit_grad)
            dlog_s[...] = logit_grad
            grad_low = att_grad.astype(bf16)
            row_sum = jnp.sum(att_grad * attended, axis=-1, keepdims=True)
            log_total = gate[:, 2 * experts : 2 * experts + 1]
            span = (count + 1) * block
            queries = q_ref[...]
            keys = k_ref[0:span, :]
            scores = dot_t(queries, keys) * scale
            row = lax.broadcasted_iota(jnp.int32, (block, block), 0)
            col = lax.broadcasted_iota(jnp.int32, (block, block), 1)
            last = jnp.where(col <= row, scores[:, span - block :], masked_score)
            scores = jnp.concatenate([scores[:, : span - block], last], axis=1)
            probs = jnp.exp(scores - log_total)
            probs_grad = dot_t(grad_low, v_ref[0:span, :])
            score_grad = (probs * (probs_grad - row_sum)).astype(bf16)
            dq_s[...] = dot(score_grad, keys) * scale
            dk_s[0:span, :] += t_dot(score_grad, queries)
            dv_s[0:span, :] += t_dot(probs.astype(bf16), grad_low)

    start = pl.multiple_of(here * block, block)
    value_grad = dv_s[pl.ds(start, block), :].astype(bf16).astype(f32)
    parts = []
    logit_grad = dlog_s[...]
    for j in range(experts):
        parts.append((gate[:, j : j + 1] * value_grad).astype(bf16))
        inner = jnp.sum(value_grad * ev_ref[:, j * lanes : (j + 1) * lanes].astype(f32), axis=-1, keepdims=True)
        logit_grad = jnp.where(lane == j, inner, logit_grad)
    slope = jnp.where(lane < 2 * experts, gate * (1.0 - gate), 0.0)
    parts.append((logit_grad * slope).astype(bf16))
    parts.append((dk_s[pl.ds(start, block), :] * scale).astype(bf16))
    parts.append(dq_s[...].astype(bf16))
    dproj = jnp.concatenate(parts, axis=1)
    dproj_ref[...] = dproj
    normed_grad = dot_t(dproj, w_ref[...]).astype(bf16)

    @pl.when(here > 0)
    def _():
        ngs_ref[0] = normed_grad

    @pl.when(here == 0)
    def _():
        ngm_ref[...] = normed_grad


def attn_bwd(me, slots, w, wo, saved, experts, head_width):
    q, k, v, ev, gate, att = saved
    block, width = slots[0].shape
    total = 5 * block
    wide = experts * lanes
    back = lambda i, me_ref: (4 - i, 0)
    later = lambda i, me_ref: (jnp.maximum(3 - i, 0), 0)
    grid_spec = pltpu.PrefetchScalarGridSpec(
        num_scalar_prefetch=1,
        grid=(5,),
        in_specs=[whole_spec((block, width))] * 4
        + [
            whole_spec(w.shape),
            whole_spec(wo.shape),
            pl.BlockSpec((block, lanes), back),
            whole_spec(k.shape),
            whole_spec(v.shape),
            pl.BlockSpec((block, wide), back),
            pl.BlockSpec((block, lanes), back),
            pl.BlockSpec((block, lanes), later),
        ],
        out_specs=[
            pl.BlockSpec((1, block, width), lambda i, me_ref: (jnp.maximum(3 - i, 0) ^ me_ref[0], 0, 0)),
            whole_spec((block, width)),
            pl.BlockSpec((block, w.shape[1]), back),
            pl.BlockSpec((block, width), later),
        ],
        scratch_shapes=[
            pltpu.VMEM((block, width), bf16),
            pltpu.VMEM((total, lanes), f32),
            pltpu.VMEM((total, lanes), f32),
            pltpu.VMEM((block, lanes), f32),
            pltpu.VMEM((block, lanes), f32),
        ],
    )
    return pl.pallas_call(
        functools.partial(attn_bwd_kernel, experts, head_width),
        grid_spec=grid_spec,
        out_shape=(
            jax.ShapeDtypeStruct((4, block, width), bf16),
            jax.ShapeDtypeStruct((block, width), bf16),
            jax.ShapeDtypeStruct((total, w.shape[1]), bf16),
            jax.ShapeDtypeStruct((4 * block, width), bf16),
        ),
        compiler_params=params(dimension_semantics=("arbitrary",)),
        cost_estimate=cost(2 * total * width * w.shape[1] + 2 * 4 * block * wide * width, 20 * 1024 * 1024, total * total),
        name="attn_bwd",
    )(me, *slots, w, wo, q, k, v, ev, gate, att)


def ffn_fwd_kernel(p0_ref, p1_ref, p2_ref, p3_ref, wu_ref, bu_ref, wd_ref, out_ref, rows_ref, upper_ref, active_ref, rows_s):
    pick_slot(pl.program_id(0), (p0_ref, p1_ref, p2_ref, p3_ref), rows_s)
    x = rows_s[...]
    rows_ref[...] = x
    upper = dot(x, wu_ref[...]) + bu_ref[...]
    upper_ref[...] = upper.astype(bf16)
    active = jax.nn.gelu(upper).astype(bf16)
    active_ref[...] = active
    out_ref[0] = dot(active, wd_ref[...]).astype(bf16)


def ffn_fwd(slots, wu, bu, wd):
    block, width = slots[0].shape
    hidden = wu.shape[1]
    rows = lambda i: (i, 0)
    return pl.pallas_call(
        ffn_fwd_kernel,
        grid=(4,),
        in_specs=[whole_spec((block, width))] * 4 + [whole_spec(wu.shape), whole_spec(bu.shape), whole_spec(wd.shape)],
        out_specs=[
            pl.BlockSpec((1, block, width), lambda i: (i, 0, 0)),
            pl.BlockSpec((block, width), rows),
            pl.BlockSpec((block, hidden), rows),
            pl.BlockSpec((block, hidden), rows),
        ],
        out_shape=(
            jax.ShapeDtypeStruct((4, block, width), bf16),
            jax.ShapeDtypeStruct((4 * block, width), bf16),
            jax.ShapeDtypeStruct((4 * block, hidden), bf16),
            jax.ShapeDtypeStruct((4 * block, hidden), bf16),
        ),
        scratch_shapes=[pltpu.VMEM((block, width), bf16)],
        compiler_params=params(dimension_semantics=("arbitrary",)),
        cost_estimate=cost(16 * block * width * hidden, 14 * 1024 * 1024, 4 * block * hidden),
        name="ffn_fwd",
    )(*slots, wu, bu, wd)


def ffn_bwd_kernel(
    g0_ref, g1_ref, g2_ref, g3_ref, upper_ref, wd_ref, wu_ref, out_ref, rows_ref, ug_ref, bias_ref, rows_s
):
    step = pl.program_id(0)
    pick_slot(step, (g0_ref, g1_ref, g2_ref, g3_ref), rows_s)
    g = rows_s[...]
    rows_ref[...] = g
    active_grad = dot_t(g, wd_ref[...])
    u = upper_ref[...].astype(f32)
    square = u * u
    t = jnp.tanh(gelu_c * u * (1.0 + gelu_a * square))
    slope = 0.5 * (1.0 + t) + 0.5 * gelu_c * u * (1.0 - t * t) * (1.0 + 3.0 * gelu_a * square)
    upper_grad = (active_grad * slope).astype(bf16)
    ug_ref[...] = upper_grad
    sums = jnp.sum(upper_grad.astype(f32), axis=0, keepdims=True)

    @pl.when(step == 0)
    def _():
        bias_ref[...] = sums

    @pl.when(step > 0)
    def _():
        bias_ref[...] += sums

    out_ref[0] = dot_t(upper_grad, wu_ref[...]).astype(bf16)


def ffn_bwd(slots, upper, wd, wu):
    block, width = slots[0].shape
    hidden = wu.shape[1]
    rows = lambda i: (i, 0)
    return pl.pallas_call(
        ffn_bwd_kernel,
        grid=(4,),
        in_specs=[whole_spec((block, width))] * 4
        + [pl.BlockSpec((block, hidden), rows), whole_spec(wd.shape), whole_spec(wu.shape)],
        out_specs=[
            pl.BlockSpec((1, block, width), lambda i: (i, 0, 0)),
            pl.BlockSpec((block, width), rows),
            pl.BlockSpec((block, hidden), rows),
            whole_spec((1, hidden)),
        ],
        out_shape=(
            jax.ShapeDtypeStruct((4, block, width), bf16),
            jax.ShapeDtypeStruct((4 * block, width), bf16),
            jax.ShapeDtypeStruct((4 * block, hidden), bf16),
            jax.ShapeDtypeStruct((1, hidden), f32),
        ),
        scratch_shapes=[pltpu.VMEM((block, width), bf16)],
        compiler_params=params(dimension_semantics=("arbitrary",)),
        cost_estimate=cost(16 * block * width * hidden, 14 * 1024 * 1024, 4 * block * hidden),
        name="ffn_bwd",
    )(*slots, upper, wd, wu)


def sum_dp(part):
    if lax.axis_size("dp") != 4:
        return lax.psum(part, "dp").astype(f32)
    kind = part.dtype
    place = lax.axis_index("dp")
    inward = lax.ppermute(part, "dp", [(0, 1), (3, 2)])
    half = (part.astype(f32) + inward.astype(f32)).astype(kind)
    other = lax.ppermute(half, "dp", [(1, 2), (2, 1)])
    full = (half.astype(f32) + other.astype(f32)).astype(kind)
    outward = lax.ppermute(full, "dp", [(1, 0), (2, 3)])
    return jnp.where((place == 1) | (place == 2), full, outward).astype(f32)


def cut(a, pieces):
    rows = a.shape[0] // pieces
    return [a[i * rows : (i + 1) * rows] for i in range(pieces)]


def pad_lanes(a, axis, count, width):
    shape = a.shape[:axis] + (count, width) + a.shape[axis + 1 :]
    pads = [(0, 0)] * len(shape)
    pads[axis + 1] = (0, lanes - width)
    padded = jnp.pad(a.reshape(shape), pads)
    return padded.reshape(a.shape[:axis] + (count * lanes,) + a.shape[axis + 1 :])


def spread(pack, experts, width):
    ev = experts * width
    routers = jnp.pad(pack[:, ev + 2 * width :], ((0, 0), (0, lanes - 2 * experts)))
    key = jnp.pad(pack[:, ev : ev + width], ((0, 0), (0, lanes - width)))
    query = jnp.pad(pack[:, ev + width : ev + 2 * width], ((0, 0), (0, lanes - width)))
    return jnp.concatenate([pad_lanes(pack[:, :ev], 1, experts, width), routers, key, query], axis=1)


def squeeze(wide, experts, width):
    base = experts * lanes
    parts = [wide[:, j * lanes : j * lanes + width] for j in range(experts)]
    parts.append(wide[:, base + lanes : base + lanes + width])
    parts.append(wide[:, base + 2 * lanes : base + 2 * lanes + width])
    parts.append(wide[:, base : base + 2 * experts])
    return jnp.concatenate(parts, axis=1)


def route_mask(value_ids, out_ids, experts, memory_len):
    lane = jnp.arange(lanes, dtype=jnp.int32)[None, :]
    out_full = jnp.pad(out_ids, ((0, 0), (memory_len, 0)), constant_values=-1)
    hit = jnp.zeros((value_ids.shape[1], lanes), jnp.bool_)
    for k in range(value_ids.shape[0]):
        hit = hit | (lane == value_ids[k][:, None])
        hit = hit | ((lane == out_full[k][:, None] + experts) & (out_full[k][:, None] >= 0))
    return hit.astype(f32)


def on_device(
    inputs,
    memory,
    value_routes,
    out_routes,
    ln1_gain,
    ln1_bias,
    query_weight,
    key_weight,
    value_weight,
    value_router,
    out_router,
    output_weight,
    ln2_gain,
    ln2_bias,
    up_weight,
    up_bias,
    down_weight,
    down_bias,
    out_cot,
):
    experts = value_router.shape[-1]
    head_width = query_weight.shape[-1]
    sec = lax.axis_index("section")
    head = lax.axis_index("head")
    me = head.astype(jnp.int32).reshape(1)
    first = sec == 0
    pick = lambda a, index: lax.dynamic_index_in_dim(a, index, 0, keepdims=False)
    memory_len = memory.shape[2] * lax.axis_size("head")

    pack = jnp.concatenate([value_weight[0, 0], key_weight[0, 0], query_weight[0, 0], value_router[0, 0], out_router[0, 0]], axis=1)
    small = jnp.concatenate([ln1_gain, ln1_bias, ln2_gain, ln2_bias, up_bias, down_bias, jnp.zeros_like(jnp.tile(ln1_gain, (2, 1)))], axis=0)
    route_rows = jnp.concatenate(
        [
            jnp.transpose(value_routes[0, :, :, 0, :], (0, 2, 1)),
            jnp.pad(jnp.transpose(out_routes[0, :, :, 0, :], (0, 2, 1)), ((0, 0), (0, 0), (memory_len, 0)), constant_values=-1),
        ],
        axis=1,
    )

    def both_layers(own, sent):
        got = swap_section(sent)
        return jnp.where(first, own, got), jnp.where(first, got, own)

    smalls = both_layers(small, small)
    route_sets = both_layers(pick(route_rows, sec), pick(route_rows, 1 - sec))
    memories = both_layers(pick(memory[0], sec), pick(memory[0], 1 - sec))
    packs = both_layers(pack, pack)
    outs_w = both_layers(output_weight[0, 0], output_weight[0, 0])
    ups = both_layers(up_weight[0], up_weight[0])
    downs = both_layers(down_weight[0], down_weight[0])

    x = pick(inputs, sec)
    cot = pick(out_cot, sec)
    topk = value_routes.shape[-1]

    layers = []
    for number in range(2):
        vec = smalls[number]
        routes = route_sets[number]
        layers.append(
            dict(
                gain1=vec[0:1],
                shift1=vec[1:2],
                gain2=vec[2:3],
                shift2=vec[3:4],
                up_b=vec[4:5],
                down_b=vec[5:6],
                w=spread(packs[number], experts, head_width),
                wo=pad_lanes(outs_w[number], 0, experts, head_width),
                wu=ups[number],
                wd=downs[number],
                mask=route_mask(routes[:topk], routes[topk:, memory_len:], experts, memory_len),
                mem=memories[number],
            )
        )
    no_add = jnp.zeros_like(layers[0]["gain1"])

    own_norm = norm_only(x, layers[0]["gain1"], layers[0]["shift1"])
    slots = gather_slots(own_norm)
    for layer in layers:
        layer["mem_all"] = jnp.concatenate(gather_slots(norm_only(layer["mem"], layer["gain1"], layer["shift1"])), axis=0)
    cot_slots = gather_slots(cot)

    saves = []
    rows_in = x
    layer_outs = []
    for number, layer in enumerate(layers):
        out, normed, q, k, v, ev, gate, att, mixed = attn_fwd(
            me, layer["mem_all"], slots, layer["w"], layer["wo"], layer["mask"], experts, head_width
        )
        terms = scatter_slots([out[s] for s in range(4)])
        hidden, own_norm2 = add_norm(rows_in, terms, no_add, layer["gain2"], layer["shift2"], f32)
        n2_slots = gather_slots(own_norm2)
        ffn, n2, upper, active = ffn_fwd(n2_slots, layer["wu"], layer["up_b"], layer["wd"])
        terms = scatter_slots([ffn[s] for s in range(4)])
        next_layer = layers[min(number + 1, 1)]
        result, own_norm = add_norm(hidden, terms, layer["down_b"], next_layer["gain1"], next_layer["shift1"], bf16)
        layer_outs.append(result)
        saves.append(
            dict(rows=rows_in, normed=normed, attn=(q, k, v, ev, gate, att), mixed=mixed, hidden=hidden, n2=n2, upper=upper, active=active)
        )
        if number == 0:
            rows_in = result
            slots = gather_slots(own_norm)

    input_grads = [None, None]
    grads = [None, None]
    g_rows = cot
    g_slots = cot_slots
    for number in (1, 0):
        layer, saved = layers[number], saves[number]
        ffn, g_all, upper_grad, up_bias_grad = ffn_bwd(g_slots, saved["upper"], layer["wd"], layer["wu"])
        terms = scatter_slots([ffn[s] for s in range(4)])
        down_grad = t_dot(saved["active"], g_all).astype(bf16)
        up_grad = t_dot(saved["n2"], upper_grad).astype(bf16)
        hidden_grad, hidden_low, small2 = norm_back(saved["hidden"], terms, layer["gain2"], g_rows)
        a_slots = gather_slots(hidden_low)
        ngs, ngm, dproj, a_all = attn_bwd(me, a_slots, layer["w"], layer["wo"], saved["attn"], experts, head_width)
        seq_terms = scatter_slots([ngs[s] for s in range(4)])
        mem_terms = scatter_slots(cut(ngm, 4))
        out_grad = t_dot(saved["mixed"], a_all).astype(bf16)
        out_grad = out_grad.reshape(experts, lanes, -1)[:, :head_width].reshape(experts * head_width, -1)
        pack_grad = squeeze(t_dot(saved["normed"], dproj).astype(bf16), experts, head_width)
        _, input_low, small1 = norm_back(saved["rows"], seq_terms, layer["gain1"], hidden_grad)
        small_mem = norm_back_small(layer["mem"], mem_terms)
        input_grads[number] = input_low
        over_head = jnp.concatenate([(small1 + small_mem)[0:2], small2[0:3], jnp.zeros_like(small2[0:3])], axis=0)
        grads[number] = dict(
            arrays=cut(down_grad, 2) + cut(up_grad, 2) + cut(out_grad, 1) + cut(pack_grad, 2),
            over_head=over_head,
            up_bias=up_bias_grad,
        )
        if number == 1:
            g_rows = input_low
            g_slots = gather_slots(input_low)

    def combine(one, two):
        kind = one.dtype
        from_first = lax.ppermute(two, "section", [(0, 1)])
        from_second = lax.ppermute(one, "section", [(1, 0)])
        at_second = (two.astype(f32) + from_first.astype(f32)).astype(kind)
        at_first = (one.astype(f32) + from_second.astype(f32)).astype(kind)
        return jnp.where(first, at_first, at_second)

    sums = [sum_dp(combine(one, two)) for one, two in zip(grads[0]["arrays"], grads[1]["arrays"])]
    vecs = []
    for grad in grads:
        vec = grad["over_head"]
        vec = vec + to_core(vec)
        vec = vec + to_chip(vec)
        vecs.append(jnp.concatenate([vec[0:5], grad["up_bias"], vec[6:8]], axis=0))
    vec = sum_dp(combine(*vecs))

    down_sum = jnp.concatenate(sums[0:2], axis=0)
    up_sum = jnp.concatenate(sums[2:4], axis=0)
    out_sum = sums[4]
    pack_sum = jnp.concatenate(sums[5:7], axis=0)
    ev = experts * head_width
    value_sum, key_sum = pack_sum[:, :ev], pack_sum[:, ev : ev + head_width]
    query_sum = pack_sum[:, ev + head_width : ev + 2 * head_width]
    vroute_sum = pack_sum[:, ev + 2 * head_width : ev + 2 * head_width + experts]
    oroute_sum = pack_sum[:, ev + 2 * head_width + experts :]

    def by_layer(one, two):
        kept = jnp.where(first, one, two)
        got = swap_section(jnp.where(first, two, one))
        return jnp.stack([jnp.where(first, kept, got), jnp.where(first, got, kept)])[None]

    return (
        by_layer(*layer_outs),
        by_layer(*input_grads),
        vec[0:1],
        vec[1:2],
        query_sum[None, None],
        key_sum[None, None],
        value_sum[None, None],
        vroute_sum[None, None],
        oroute_sum[None, None],
        out_sum[None, None],
        vec[2:3],
        vec[3:4],
        up_sum[None],
        vec[5:6],
        down_sum[None],
        vec[4:5],
    )


def solution(mesh):
    placed = (
        P("dp", "head", None),
        P("section", "dp", "head", None),
        P("section", "dp", None, "head", None),
        P("section", "dp", None, "head", None),
        P("section", None),
        P("section", None),
        P("section", "head", None, None),
        P("section", "head", None, None),
        P("section", "head", None, None),
        P("section", "head", None, None),
        P("section", "head", None, None),
        P("section", "head", None, None),
        P("section", None),
        P("section", None),
        P("section", None, "head"),
        P("section", "head"),
        P("section", "head", None),
        P("section", None),
        P("dp", "head", None),
    )
    return jax.shard_map(
        on_device,
        mesh=mesh,
        in_specs=placed,
        out_specs=(
            P("section", "dp", "head", None),
            P("section", "dp", "head", None),
            P("section", None),
            P("section", None),
            P("section", "head", None, None),
            P("section", "head", None, None),
            P("section", "head", None, None),
            P("section", "head", None, None),
            P("section", "head", None, None),
            P("section", "head", None, None),
            P("section", None),
            P("section", None),
            P("section", None, "head"),
            P("section", "head"),
            P("section", "head", None),
            P("section", None),
        ),
        check_vma=False,
    )
```

```python
import functools

import jax
import jax.numpy as jnp
from jax import lax
from jax.experimental import pallas as pl
from jax.experimental.pallas import tpu as pltpu
from jax.sharding import PartitionSpec as P

norm_eps = 1e-05
masked_score = -1e30
lanes = 128
out_lane = 8
log_lane = 16
bf16 = jnp.bfloat16
f32 = jnp.float32
gelu_c = 0.7978845608028654
gelu_a = 0.044715

core_pairs = [(0, 1), (1, 0), (2, 3), (3, 2)]
chip_pairs = [(0, 2), (2, 0), (1, 3), (3, 1)]
vmem_bytes = 50 * 1024 * 1024


def dot(a, b):
    return lax.dot_general(a, b, (((1,), (0,)), ((), ())), preferred_element_type=f32)


def dot_t(a, b):
    return lax.dot_general(a, b, (((1,), (1,)), ((), ())), preferred_element_type=f32)


def t_dot(a, b):
    return lax.dot_general(a, b, (((0,), (0,)), ((), ())), preferred_element_type=f32)


def params(**more):
    return pltpu.CompilerParams(vmem_limit_bytes=vmem_bytes, **more)


def whole_spec(shape):
    return pl.BlockSpec(shape, lambda *_: (0,) * len(shape))


def cost(flops, nbytes, trans=0):
    return pl.CostEstimate(flops=int(flops), bytes_accessed=int(nbytes), transcendentals=int(trans))


def to_core(a):
    return lax.ppermute(a, "head", core_pairs)


def to_chip(a):
    return lax.ppermute(a, "head", chip_pairs)


def swap_section(a):
    return lax.ppermute(a, "section", [(0, 1), (1, 0)])


def gather_slots(own):
    from_chip = to_chip(own)
    from_core = to_core(own)
    from_both = to_core(from_chip)
    return [own, from_core, from_chip, from_both]


def scatter_slots(parts, beside=None):
    from_core_far = to_core(parts[3])
    from_core = to_core(parts[1])
    far = (parts[2].astype(f32) + from_core_far.astype(f32)).astype(bf16)
    from_chip = to_chip(far)
    if beside is None:
        return parts[0], from_core, from_chip
    from_chip, beside = lax.optimization_barrier((from_chip, beside))
    return (parts[0], from_core, from_chip), beside


def norm_rows(x, gain, shift):
    average = jnp.mean(x, axis=-1, keepdims=True)
    centred = x - average
    variance = jnp.mean(centred * centred, axis=-1, keepdims=True)
    return centred * lax.rsqrt(variance + norm_eps) * gain + shift


def norm_kernel(x_ref, gain_ref, shift_ref, out_ref):
    out_ref[...] = norm_rows(x_ref[...].astype(f32), gain_ref[...], shift_ref[...]).astype(bf16)


def norm_only(x, gain, shift):
    return pl.pallas_call(
        norm_kernel,
        out_shape=jax.ShapeDtypeStruct(x.shape, bf16),
        compiler_params=params(),
        cost_estimate=cost(x.size * 8, x.size * 4),
        name="norm_only",
    )(x, gain, shift)


def add_norm_kernel(x_ref, a_ref, b_ref, c_ref, add_ref, gain_ref, shift_ref, sum_ref, out_ref):
    total = x_ref[...].astype(f32) + (a_ref[...].astype(f32) + b_ref[...].astype(f32) + c_ref[...].astype(f32))
    total = total + add_ref[...]
    sum_ref[...] = total.astype(sum_ref.dtype)
    total = sum_ref[...].astype(f32)
    out_ref[...] = norm_rows(total, gain_ref[...], shift_ref[...]).astype(bf16)


def add_norm(x, terms, add, gain, shift, sum_type):
    return pl.pallas_call(
        add_norm_kernel,
        out_shape=(jax.ShapeDtypeStruct(x.shape, sum_type), jax.ShapeDtypeStruct(x.shape, bf16)),
        compiler_params=params(),
        cost_estimate=cost(x.size * 12, x.size * 14),
        name="add_norm",
    )(x, *terms, add, gain, shift)


def norm_back_kernel(x_ref, a_ref, b_ref, c_ref, gain_ref, more_ref, dx_ref, low_ref, small_ref):
    x = x_ref[...].astype(f32)
    grad = a_ref[...].astype(f32) + b_ref[...].astype(f32) + c_ref[...].astype(f32)
    average = jnp.mean(x, axis=-1, keepdims=True)
    centred = x - average
    variance = jnp.mean(centred * centred, axis=-1, keepdims=True)
    scale = lax.rsqrt(variance + norm_eps)
    unit = centred * scale
    wide = grad * gain_ref[...]
    mean_wide = jnp.mean(wide, axis=-1, keepdims=True)
    mean_unit = jnp.mean(wide * unit, axis=-1, keepdims=True)
    more = more_ref[...].astype(f32)
    dx = more + scale * (wide - mean_wide - unit * mean_unit)
    dx_ref[...] = dx
    low_ref[...] = dx.astype(bf16)
    small_ref[0:1, :] = jnp.sum(grad * unit, axis=0, keepdims=True)
    small_ref[1:2, :] = jnp.sum(grad, axis=0, keepdims=True)
    small_ref[2:3, :] = jnp.sum(more, axis=0, keepdims=True)
    small_ref[3:8, :] = jnp.zeros((5, x.shape[1]), f32)


def norm_back(x, terms, gain, more):
    return pl.pallas_call(
        norm_back_kernel,
        out_shape=(
            jax.ShapeDtypeStruct(x.shape, f32),
            jax.ShapeDtypeStruct(x.shape, bf16),
            jax.ShapeDtypeStruct((8, x.shape[1]), f32),
        ),
        compiler_params=params(),
        cost_estimate=cost(x.size * 20, x.size * 20),
        name="norm_back",
    )(x, *terms, gain, more)


def norm_back_small_kernel(x_ref, a_ref, b_ref, c_ref, small_ref):
    x = x_ref[...].astype(f32)
    grad = a_ref[...].astype(f32) + b_ref[...].astype(f32) + c_ref[...].astype(f32)
    average = jnp.mean(x, axis=-1, keepdims=True)
    centred = x - average
    variance = jnp.mean(centred * centred, axis=-1, keepdims=True)
    unit = centred * lax.rsqrt(variance + norm_eps)
    small_ref[0:1, :] = jnp.sum(grad * unit, axis=0, keepdims=True)
    small_ref[1:2, :] = jnp.sum(grad, axis=0, keepdims=True)
    small_ref[2:8, :] = jnp.zeros((6, x.shape[1]), f32)


def norm_back_small(x, terms):
    return pl.pallas_call(
        norm_back_small_kernel,
        out_shape=jax.ShapeDtypeStruct((8, x.shape[1]), f32),
        compiler_params=params(),
        cost_estimate=cost(x.size * 10, x.size * 8),
        name="norm_back_small",
    )(x, *terms)


def pick_slot(slot, refs, target):
    for number, ref in enumerate(refs):

        @pl.when(slot == number)
        def _(ref=ref):
            target[...] = ref[...]


def store_slot(slot, refs, block):
    for number, ref in enumerate(refs):

        @pl.when(slot == number)
        def _(ref=ref):
            ref[...] = block


def fill_experts(target, source, experts, width):
    for j in range(experts):
        target[j * lanes : j * lanes + width, :] = source[j * width : (j + 1) * width, :]
        target[j * lanes + width : (j + 1) * lanes, :] = jnp.zeros((lanes - width, target.shape[1]), bf16)


def fill_weights(w_s, wo_s, wv_ref, wk_ref, wo_ref, experts, width):
    fill_experts(w_s, wv_ref, experts, width)
    fill_experts(wo_s, wo_ref, experts, width)
    start = 0
    for place, rows in ((experts + 1, width), (experts + 2, width), (experts, 2 * out_lane)):
        w_s[place * lanes : place * lanes + rows, :] = wk_ref[start : start + rows, :]
        w_s[place * lanes + rows : (place + 1) * lanes, :] = jnp.zeros((lanes - rows, w_s.shape[1]), bf16)
        start += rows


def attn_fwd_kernel(
    experts,
    head_width,
    me_ref,
    m0_ref,
    m1_ref,
    m2_ref,
    m3_ref,
    p0_ref,
    p1_ref,
    p2_ref,
    p3_ref,
    wv_ref,
    wk_ref,
    wo_ref,
    mask_ref,
    o0_ref,
    o1_ref,
    o2_ref,
    o3_ref,
    normed_ref,
    q_ref,
    k_ref,
    v_ref,
    ev_ref,
    gate_ref,
    att_ref,
    mixed_ref,
    rows_s,
    k_s,
    v_s,
    mask_s,
    w_s,
    wo_s,
):
    step = pl.program_id(0)
    me = me_ref[0]
    block = rows_s.shape[0]
    wide = experts * lanes
    quarter = block // 4

    @pl.when(step == 0)
    def _():
        fill_weights(w_s, wo_s, wv_ref, wk_ref, wo_ref, experts, head_width)
        for slot, mem_ref in enumerate((m0_ref, m1_ref, m2_ref, m3_ref)):
            rows_s[slot * quarter : (slot + 1) * quarter, :] = mem_ref[...]
            start = pl.multiple_of((me ^ slot) * quarter, quarter)
            mask_s[slot * quarter : (slot + 1) * quarter, :] = mask_ref[pl.ds(start, quarter), :]

    @pl.when(step > 0)
    def _():
        pick_slot((step - 1) ^ me, (p0_ref, p1_ref, p2_ref, p3_ref), rows_s)
        mask_s[...] = mask_ref[pl.ds(pl.multiple_of(step * block, block), block), :]

    x = rows_s[...]
    normed_ref[...] = x
    proj = dot_t(x, w_s[...])
    gate = jax.nn.sigmoid(proj[:, wide : wide + lanes]) * mask_s[...]
    value = jnp.zeros((block, lanes), f32)
    for j in range(experts):
        value = value + gate[:, j : j + 1] * proj[:, j * lanes : (j + 1) * lanes]
    start = pl.multiple_of(step * block, block)
    keys = proj[:, wide + lanes : wide + 2 * lanes].astype(bf16)
    value = value.astype(bf16)
    k_s[pl.ds(start, block), :] = keys
    v_s[pl.ds(start, block), :] = value
    k_ref[...] = keys
    v_ref[...] = value
    ev_ref[...] = proj[:, :wide].astype(bf16)
    queries = proj[:, wide + 2 * lanes :].astype(bf16)
    q_ref[...] = queries

    @pl.when(step == 0)
    def _():
        gate_ref[...] = gate

    scale = head_width ** (-0.5)
    for count in range(1, 5):

        @pl.when(step == count)
        def _(count=count):
            span = (count + 1) * block
            scores = dot_t(queries, k_s[0:span, :]) * scale
            row = lax.broadcasted_iota(jnp.int32, (block, block), 0)
            col = lax.broadcasted_iota(jnp.int32, (block, block), 1)
            last = jnp.where(col <= row, scores[:, span - block :], masked_score)
            scores = jnp.concatenate([scores[:, : span - block], last], axis=1)
            top = jnp.max(scores, axis=-1, keepdims=True)
            exponent = jnp.exp(scores - top)
            total = jnp.sum(exponent, axis=-1, keepdims=True)
            probs = (exponent * (1.0 / total)).astype(bf16)
            attended = dot(probs, v_s[0:span, :])
            att_ref[...] = attended
            lane = lax.broadcasted_iota(jnp.int32, (block, lanes), 1)
            gate_ref[...] = jnp.where(lane == log_lane, top + jnp.log(total), gate)
            mixed = jnp.concatenate(
                [(gate[:, out_lane + j : out_lane + j + 1] * attended).astype(bf16) for j in range(experts)], axis=1
            )
            mixed_ref[...] = mixed
            store_slot((count - 1) ^ me, (o0_ref, o1_ref, o2_ref, o3_ref), dot(mixed, wo_s[...]).astype(bf16))


def attn_fwd(me, mems, slots, w, mask, experts, head_width):
    block, width = slots[0].shape
    total = 5 * block
    wide = experts * lanes
    later = lambda i, me_ref: (jnp.maximum(i - 1, 0), 0)
    every = lambda i, me_ref: (i, 0)
    shapes = lambda rows, cols, kind: jax.ShapeDtypeStruct((rows, cols), kind)
    grid_spec = pltpu.PrefetchScalarGridSpec(
        num_scalar_prefetch=1,
        grid=(5,),
        in_specs=[whole_spec((block // 4, width))] * 4
        + [whole_spec((block, width))] * 4
        + [whole_spec(a.shape) for a in w]
        + [whole_spec(mask.shape)],
        out_specs=[
            *[whole_spec((block, width))] * 4,
            pl.BlockSpec((block, width), every),
            pl.BlockSpec((block, lanes), every),
            pl.BlockSpec((block, lanes), every),
            pl.BlockSpec((block, lanes), every),
            pl.BlockSpec((block, wide), every),
            pl.BlockSpec((block, lanes), every),
            pl.BlockSpec((block, lanes), later),
            pl.BlockSpec((block, wide), later),
        ],
        scratch_shapes=[
            pltpu.VMEM((block, width), bf16),
            pltpu.VMEM((total, lanes), bf16),
            pltpu.VMEM((total, lanes), bf16),
            pltpu.VMEM((block, lanes), f32),
            pltpu.VMEM((wide + 3 * lanes, width), bf16),
            pltpu.VMEM((wide, width), bf16),
        ],
    )
    return pl.pallas_call(
        functools.partial(attn_fwd_kernel, experts, head_width),
        grid_spec=grid_spec,
        out_shape=(
            *[shapes(block, width, bf16)] * 4,
            shapes(total, width, bf16),
            shapes(total, lanes, bf16),
            shapes(total, lanes, bf16),
            shapes(total, lanes, bf16),
            shapes(total, wide, bf16),
            shapes(total, lanes, f32),
            shapes(4 * block, lanes, f32),
            shapes(4 * block, wide, bf16),
        ),
        compiler_params=params(dimension_semantics=("arbitrary",)),
        cost_estimate=cost(4 * total * width * wide, 16 * 1024 * 1024, total * total),
        name="attn_fwd",
    )(me, *mems, *slots, *w, mask)


def attn_bwd_kernel(
    experts,
    head_width,
    me_ref,
    d0_ref,
    d1_ref,
    d2_ref,
    d3_ref,
    wv_ref,
    wk_ref,
    wo_ref,
    q_ref,
    k_ref,
    v_ref,
    ev_ref,
    gate_ref,
    att_ref,
    n0_ref,
    n1_ref,
    n2_ref,
    n3_ref,
    ngm_ref,
    dproj_ref,
    da_ref,
    rows_s,
    dk_s,
    dv_s,
    dq_s,
    dlog_s,
    w_s,
    wo_s,
):
    step = pl.program_id(0)
    me = me_ref[0]
    here = 4 - step
    block = rows_s.shape[0]
    wide = experts * lanes
    scale = head_width ** (-0.5)
    gate = gate_ref[...]
    lane = lax.broadcasted_iota(jnp.int32, (block, lanes), 1)

    @pl.when(step == 0)
    def _():
        fill_weights(w_s, wo_s, wv_ref, wk_ref, wo_ref, experts, head_width)
        dk_s[...] = jnp.zeros_like(dk_s)
        dv_s[...] = jnp.zeros_like(dv_s)

    @pl.when(here == 0)
    def _():
        dq_s[...] = jnp.zeros_like(dq_s)
        dlog_s[...] = jnp.zeros_like(dlog_s)

    for count in range(1, 5):

        @pl.when(here == count)
        def _(count=count):
            pick_slot((count - 1) ^ me, (d0_ref, d1_ref, d2_ref, d3_ref), rows_s)
            rows = rows_s[...]
            da_ref[...] = rows
            mixed_grad = dot_t(rows, wo_s[...])
            attended = att_ref[...]
            att_grad = jnp.zeros((block, lanes), f32)
            logit_grad = jnp.zeros((block, lanes), f32)
            for j in range(experts):
                part = mixed_grad[:, j * lanes : (j + 1) * lanes]
                att_grad = att_grad + gate[:, out_lane + j : out_lane + j + 1] * part
                inner = jnp.sum(part * attended, axis=-1, keepdims=True)
                logit_grad = jnp.where(lane == out_lane + j, inner, logit_grad)
            dlog_s[...] = logit_grad
            grad_low = att_grad.astype(bf16)
            row_sum = jnp.sum(att_grad * attended, axis=-1, keepdims=True)
            log_total = gate[:, log_lane : log_lane + 1]
            span = (count + 1) * block
            queries = q_ref[...]
            keys = k_ref[0:span, :]
            scores = dot_t(queries, keys) * scale
            row = lax.broadcasted_iota(jnp.int32, (block, block), 0)
            col = lax.broadcasted_iota(jnp.int32, (block, block), 1)
            last = jnp.where(col <= row, scores[:, span - block :], masked_score)
            scores = jnp.concatenate([scores[:, : span - block], last], axis=1)
            probs = jnp.exp(scores - log_total)
            probs_grad = dot_t(grad_low, v_ref[0:span, :])
            score_grad = (probs * (probs_grad - row_sum)).astype(bf16)
            dq_s[...] = dot(score_grad, keys) * scale
            dk_s[0:span, :] += t_dot(score_grad, queries)
            dv_s[0:span, :] += t_dot(probs.astype(bf16), grad_low)

    start = pl.multiple_of(here * block, block)
    value_grad = dv_s[pl.ds(start, block), :].astype(bf16).astype(f32)
    parts = []
    logit_grad = dlog_s[...]
    for j in range(experts):
        parts.append((gate[:, j : j + 1] * value_grad).astype(bf16))
        inner = jnp.sum(value_grad * ev_ref[:, j * lanes : (j + 1) * lanes].astype(f32), axis=-1, keepdims=True)
        logit_grad = jnp.where(lane == j, inner, logit_grad)
    slope = jnp.where(lane < log_lane, gate * (1.0 - gate), 0.0)
    parts.append((logit_grad * slope).astype(bf16))
    parts.append((dk_s[pl.ds(start, block), :] * scale).astype(bf16))
    parts.append(dq_s[...].astype(bf16))
    dproj = jnp.concatenate(parts, axis=1)
    dproj_ref[...] = dproj
    normed_grad = dot(dproj, w_s[...]).astype(bf16)

    @pl.when(here > 0)
    def _():
        store_slot((here - 1) ^ me, (n0_ref, n1_ref, n2_ref, n3_ref), normed_grad)

    @pl.when(here == 0)
    def _():
        ngm_ref[...] = normed_grad


def attn_bwd(me, slots, w, saved, experts, head_width):
    q, k, v, ev, gate, att = saved
    block, width = slots[0].shape
    total = 5 * block
    wide = experts * lanes
    back = lambda i, me_ref: (4 - i, 0)
    later = lambda i, me_ref: (jnp.maximum(3 - i, 0), 0)
    grid_spec = pltpu.PrefetchScalarGridSpec(
        num_scalar_prefetch=1,
        grid=(5,),
        in_specs=[whole_spec((block, width))] * 4
        + [whole_spec(a.shape) for a in w]
        + [
            pl.BlockSpec((block, lanes), back),
            whole_spec(k.shape),
            whole_spec(v.shape),
            pl.BlockSpec((block, wide), back),
            pl.BlockSpec((block, lanes), back),
            pl.BlockSpec((block, lanes), later),
        ],
        out_specs=[
            *[whole_spec((block, width))] * 5,
            pl.BlockSpec((block, wide + 3 * lanes), back),
            pl.BlockSpec((block, width), later),
        ],
        scratch_shapes=[
            pltpu.VMEM((block, width), bf16),
            pltpu.VMEM((total, lanes), f32),
            pltpu.VMEM((total, lanes), f32),
            pltpu.VMEM((block, lanes), f32),
            pltpu.VMEM((block, lanes), f32),
            pltpu.VMEM((wide + 3 * lanes, width), bf16),
            pltpu.VMEM((wide, width), bf16),
        ],
    )
    return pl.pallas_call(
        functools.partial(attn_bwd_kernel, experts, head_width),
        grid_spec=grid_spec,
        out_shape=(
            *[jax.ShapeDtypeStruct((block, width), bf16)] * 5,
            jax.ShapeDtypeStruct((total, wide + 3 * lanes), bf16),
            jax.ShapeDtypeStruct((4 * block, width), bf16),
        ),
        compiler_params=params(dimension_semantics=("arbitrary",)),
        cost_estimate=cost(4 * total * width * wide, 16 * 1024 * 1024, total * total),
        name="attn_bwd",
    )(me, *slots, *w, q, k, v, ev, gate, att)


def ffn_fwd_kernel(a_ref, b_ref, wu_ref, bu_ref, wd_ref, *refs):
    oa_ref, ob_ref, rows_ref, upper_ref, active_ref = refs[-5:]
    half = a_ref.shape[0]
    rows_ref[0:half, :] = a_ref[...]
    rows_ref[half:, :] = b_ref[...]
    upper = dot(rows_ref[...], wu_ref[...]) + bu_ref[...]
    upper_ref[...] = upper.astype(bf16)
    active_ref[...] = jax.nn.gelu(upper).astype(bf16)
    out = dot(active_ref[...], wd_ref[...]).astype(bf16)
    oa_ref[...] = out[0:half]
    ob_ref[...] = out[half:]


def ffn_fwd(pair, number, wu, bu, wd, earlier):
    block, width = pair[0].shape
    hidden = wu.shape[1]
    here = lambda i: (number, 0)
    specs = [whole_spec((block, width))] * 2 + [whole_spec(wu.shape), whole_spec(bu.shape), whole_spec(wd.shape)]
    return pl.pallas_call(
        ffn_fwd_kernel,
        grid=(1,),
        in_specs=specs + [pl.BlockSpec(memory_space=pl.ANY)] * len(earlier),
        out_specs=[whole_spec((block, width))] * 2
        + [pl.BlockSpec((2 * block, width), here)]
        + [pl.BlockSpec((2 * block, hidden), here)] * 2,
        out_shape=(
            jax.ShapeDtypeStruct((block, width), bf16),
            jax.ShapeDtypeStruct((block, width), bf16),
            jax.ShapeDtypeStruct((4 * block, width), bf16),
            jax.ShapeDtypeStruct((4 * block, hidden), bf16),
            jax.ShapeDtypeStruct((4 * block, hidden), bf16),
        ),
        input_output_aliases={5 + i: 2 + i for i in range(len(earlier))},
        compiler_params=params(),
        cost_estimate=cost(8 * block * width * hidden, 9 * 1024 * 1024, 2 * block * hidden),
        name="ffn_fwd",
    )(*pair, wu, bu, wd, *earlier)


def ffn_bwd_kernel(a_ref, b_ref, upper_ref, wd_ref, wu_ref, *refs):
    oa_ref, ob_ref, bias_ref, rows_ref, ug_ref = refs[-5:]
    half = a_ref.shape[0]
    rows_ref[0:half, :] = a_ref[...]
    rows_ref[half:, :] = b_ref[...]
    active_grad = dot_t(rows_ref[...], wd_ref[...])
    u = upper_ref[...].astype(f32)
    square = u * u
    t = jnp.tanh(gelu_c * u * (1.0 + gelu_a * square))
    slope = 0.5 * (1.0 + t) + 0.5 * gelu_c * u * (1.0 - t * t) * (1.0 + 3.0 * gelu_a * square)
    upper_grad = (active_grad * slope).astype(bf16)
    ug_ref[...] = upper_grad
    bias_ref[...] = jnp.sum(upper_grad.astype(f32), axis=0, keepdims=True)
    out = dot_t(ug_ref[...], wu_ref[...]).astype(bf16)
    oa_ref[...] = out[0:half]
    ob_ref[...] = out[half:]


def ffn_bwd(pair, number, upper, wd, wu, earlier):
    block, width = pair[0].shape
    hidden = wu.shape[1]
    here = lambda i: (number, 0)
    specs = [whole_spec((block, width))] * 2
    specs += [pl.BlockSpec((2 * block, hidden), here), whole_spec(wd.shape), whole_spec(wu.shape)]
    return pl.pallas_call(
        ffn_bwd_kernel,
        grid=(1,),
        in_specs=specs + [pl.BlockSpec(memory_space=pl.ANY)] * len(earlier),
        out_specs=[whole_spec((block, width))] * 2
        + [whole_spec((1, hidden)), pl.BlockSpec((2 * block, width), here), pl.BlockSpec((2 * block, hidden), here)],
        out_shape=(
            jax.ShapeDtypeStruct((block, width), bf16),
            jax.ShapeDtypeStruct((block, width), bf16),
            jax.ShapeDtypeStruct((1, hidden), f32),
            jax.ShapeDtypeStruct((4 * block, width), bf16),
            jax.ShapeDtypeStruct((4 * block, hidden), bf16),
        ),
        input_output_aliases={5 + i: 3 + i for i in range(len(earlier))},
        compiler_params=params(),
        cost_estimate=cost(8 * block * width * hidden, 9 * 1024 * 1024, 2 * block * hidden),
        name="ffn_bwd",
    )(*pair, upper, wd, wu, *earlier)


def plus(a, b):
    return jax.tree.map(lambda one, two: (one.astype(f32) + two.astype(f32)).astype(one.dtype), a, b)


def move(a, axis, pairs):
    return jax.tree.map(lambda one: lax.ppermute(one, axis, pairs), a)


def after(a, token):
    return lax.optimization_barrier((a, token))[0]


class ChunkSums:
    def __init__(self):
        self.chunks = []
        self.token = None
        self.direct = lax.axis_size("dp") != 4
        place = lax.axis_index("dp")
        self.middle = (place == 1) | (place == 2)

    def add(self, own, got):
        self.chunks.append(dict(own=own, moving=got, step=0))

    def turn(self, number):
        chunk = self.chunks[number]
        got = chunk["moving"] if self.token is None else after(chunk["moving"], self.token)
        step = chunk["step"]
        chunk["step"] += 1
        if self.direct:
            if step == 0:
                chunk["end"] = lax.psum(plus(chunk["own"], got), "dp")
            return
        if step == 3:
            chunk["end"] = jax.tree.map(lambda full, far: jnp.where(self.middle, full, far), chunk["own"], got)
            return
        total = plus(chunk["own"], got)
        pairs = ([(0, 1), (3, 2)], [(1, 2), (2, 1)], [(1, 0), (2, 3)])[step]
        chunk["own"], chunk["moving"] = total, move(total, "dp", pairs)
        self.token = total

    def before(self, a):
        return a if self.token is None else after(a, self.token)


def cut(a, pieces):
    rows = a.shape[0] // pieces
    return [a[i * rows : (i + 1) * rows] for i in range(pieces)]


def padded_rows(a, rows):
    return jnp.pad(a, ((0, rows - a.shape[0]), (0, 0)))


def squeeze_out(wide, experts, width):
    return jnp.concatenate([wide[j * lanes : j * lanes + width] for j in range(experts)], axis=0)


def squeeze(wide, experts, width):
    base = experts * lanes
    parts = [wide[j * lanes : j * lanes + width] for j in range(experts)]
    parts.append(wide[base + lanes : base + lanes + width])
    parts.append(wide[base + 2 * lanes : base + 2 * lanes + width])
    parts.append(wide[base : base + 2 * out_lane])
    return jnp.concatenate(parts, axis=0)


def swap_weights(weights):
    size = lax.axis_size("dp")
    if size % 2:
        return [swap_section(a) for a in weights]
    odd = lax.axis_index("dp") % 2
    results = []
    token = None
    for a in weights:
        rows = a.shape[0] // 2
        half = lax.dynamic_slice_in_dim(a if token is None else after(a, token), odd * rows, rows, 0)
        token = half
        got = swap_section(half)
        other = lax.ppermute(got, "dp", [(i, i ^ 1) for i in range(size)])
        results.append(jnp.concatenate([jnp.where(odd == 0, got, other), jnp.where(odd == 0, other, got)], axis=0))
    return results


def route_mask(value_ids, out_ids, experts, memory_len):
    lane = jnp.arange(lanes, dtype=jnp.int32)[None, :]
    out_full = jnp.pad(out_ids, ((0, 0), (memory_len, 0)), constant_values=-1)
    hit = jnp.zeros((value_ids.shape[1], lanes), jnp.bool_)
    for k in range(value_ids.shape[0]):
        hit = hit | (lane == value_ids[k][:, None])
        hit = hit | ((lane == out_full[k][:, None] + out_lane) & (out_full[k][:, None] >= 0))
    return hit.astype(f32)


def on_device(
    inputs,
    memory,
    value_routes,
    out_routes,
    ln1_gain,
    ln1_bias,
    query_weight,
    key_weight,
    value_weight,
    value_router,
    out_router,
    output_weight,
    ln2_gain,
    ln2_bias,
    up_weight,
    up_bias,
    down_weight,
    down_bias,
    out_cot,
):
    experts = value_router.shape[-1]
    head_width = query_weight.shape[-1]
    sec = lax.axis_index("section")
    head = lax.axis_index("head")
    me = head.astype(jnp.int32).reshape(1)
    first = sec == 0
    pick = lambda a, index: lax.dynamic_index_in_dim(a, index, 0, keepdims=False)
    memory_len = memory.shape[2] * lax.axis_size("head")

    value_rows = experts * head_width
    router_rows = [padded_rows(a[0, 0].T, out_lane) for a in (value_router, out_router)]
    kqr = jnp.concatenate([key_weight[0, 0].T, query_weight[0, 0].T, *router_rows])
    weights = [kqr, value_weight[0, 0].T, output_weight[0, 0], up_weight[0], down_weight[0]]
    small = jnp.concatenate([ln1_gain, ln1_bias, ln2_gain, ln2_bias, up_bias, down_bias, ln1_gain, ln1_bias], axis=0)
    route_rows = jnp.concatenate(
        [
            jnp.transpose(value_routes[0, :, :, 0, :], (0, 2, 1)),
            jnp.pad(jnp.transpose(out_routes[0, :, :, 0, :], (0, 2, 1)), ((0, 0), (0, 0), (memory_len, 0)), constant_values=-1),
        ],
        axis=1,
    )
    sends = [small, pick(memory[0], 1 - sec), pick(route_rows, 1 - sec)]
    sends, weights = lax.optimization_barrier((sends, weights))
    gots = [swap_section(a) for a in sends]
    weights, gots = lax.optimization_barrier((weights, gots))
    small_got, memory_got, routes_got = gots

    def both_layers(own, got):
        return jnp.where(first, own, got), jnp.where(first, got, own)

    smalls = both_layers(small, small_got)
    route_sets = both_layers(pick(route_rows, sec), routes_got)
    memories = both_layers(pick(memory[0], sec), memory_got)
    weight_sets = [both_layers(a, got) for a, got in zip(weights, swap_weights(weights))]

    x = pick(inputs, sec)
    cot = pick(out_cot, sec)
    topk = value_routes.shape[-1]

    layers = []
    for number in range(2):
        vec = smalls[number]
        routes = route_sets[number]
        layers.append(
            dict(
                gain1=vec[0:1],
                shift1=vec[1:2],
                gain2=vec[2:3],
                shift2=vec[3:4],
                up_b=vec[4:5],
                down_b=vec[5:6],
                w=(weight_sets[1][number], weight_sets[0][number], weight_sets[2][number]),
                wu=weight_sets[3][number],
                wd=weight_sets[4][number],
                mask=route_mask(routes[:topk], routes[topk:, memory_len:], experts, memory_len),
                mem=memories[number],
            )
        )
    no_add = jnp.zeros_like(layers[0]["gain1"])

    own_norm = norm_only(x, layers[0]["gain1"], layers[0]["shift1"])
    slots = gather_slots(own_norm)
    for layer in layers:
        layer["mem_slots"] = gather_slots(norm_only(layer["mem"], layer["gain1"], layer["shift1"]))
    cot_slots = gather_slots(cot)

    saves = []
    rows_in = x
    layer_outs = []
    for number, layer in enumerate(layers):
        *out, normed, q, k, v, ev, gate, att, mixed = attn_fwd(
            me, layer["mem_slots"], slots, layer["w"], layer["mask"], experts, head_width
        )
        terms = scatter_slots(out)
        hidden, own_norm2 = add_norm(rows_in, terms, no_add, layer["gain2"], layer["shift2"], f32)
        n2_slots = gather_slots(own_norm2)
        near_a, near_b, *kept = ffn_fwd(n2_slots[0:2], 0, layer["wu"], layer["up_b"], layer["wd"], ())
        far_a, far_b, n2, upper, active = ffn_fwd(n2_slots[2:4], 1, layer["wu"], layer["up_b"], layer["wd"], kept)
        terms = scatter_slots([near_a, near_b, far_a, far_b])
        next_layer = layers[min(number + 1, 1)]
        result, own_norm = add_norm(hidden, terms, layer["down_b"], next_layer["gain1"], next_layer["shift1"], bf16)
        layer_outs.append(result)
        saves.append(
            dict(rows=rows_in, normed=normed, attn=(q, k, v, ev, gate, att), mixed=mixed, hidden=hidden, n2=n2, upper=upper, active=active)
        )
        if number == 0:
            rows_in = result
            slots = gather_slots(own_norm)

    def by_layer(one, two):
        got = swap_section(jnp.where(first, two, one))
        kept = jnp.where(first, one, two)
        return jnp.stack([jnp.where(first, kept, got), jnp.where(first, got, kept)])[None]

    def send_chunks(one, two, pieces):
        gots, owns = [], []
        for part_one, part_two in zip(cut(one, pieces), cut(two, pieces)):
            gots.append(jnp.where(first, part_two, part_one))
            owns.append(jnp.where(first, part_one, part_two))
        return gots, owns

    layer_out = by_layer(*layer_outs)
    sums = ChunkSums()
    grads = [{}, {}]
    smalls_out = [None, None]
    input_grads = [None, None]
    g_rows = cot
    g_slots = cot_slots
    for number in (1, 0):
        layer, saved, grad = layers[number], saves[number], grads[number]
        near_a, near_b, near_bias, *kept = ffn_bwd(g_slots[0:2], 0, saved["upper"], layer["wd"], layer["wu"], ())
        far_a, far_b, far_bias, g_all, upper_grad = ffn_bwd(g_slots[2:4], 1, saved["upper"], layer["wd"], layer["wu"], kept)
        grad["down"] = t_dot(saved["active"], g_all).astype(bf16)
        grad["up"] = t_dot(saved["n2"], upper_grad).astype(bf16)
        if number == 0:
            down_sends, down_owns = send_chunks(grads[0]["down"], grads[1]["down"], 2)
            up_sends, up_owns = send_chunks(grads[0]["up"], grads[1]["up"], 2)
            up_sends = after(up_sends, down_sends)
            beside = (down_sends, up_sends)
        else:
            beside = (grad["down"], grad["up"])
        terms, beside = scatter_slots([near_a, near_b, far_a, far_b], beside)
        if number == 0:
            for own, send in zip((*down_owns, *up_owns), (*down_sends, *up_sends)):
                sums.add(own, swap_section(send))
        else:
            grad["down"], grad["up"] = beside
        hidden_grad, hidden_low, small2 = norm_back(saved["hidden"], terms, layer["gain2"], g_rows)
        a_slots = gather_slots(hidden_low)
        if number == 0:
            sums.turn(0)
            sums.turn(1)
            a_slots[3] = sums.before(a_slots[3])
        *ngs, ngm, dproj, a_all = attn_bwd(me, a_slots, layer["w"], saved["attn"], experts, head_width)
        grad["out"] = squeeze_out(t_dot(saved["mixed"], a_all).astype(bf16), experts, head_width)
        grad["pack"] = squeeze(t_dot(dproj, saved["normed"]).astype(bf16), experts, head_width)
        if number == 0:
            out_sends, out_owns = send_chunks(grads[0]["out"], grads[1]["out"], 1)
            pack_sends, pack_owns = send_chunks(grads[0]["pack"], grads[1]["pack"], 2)
            pack_sends = after(pack_sends, out_sends)
            beside = (out_sends, pack_sends)
        else:
            beside = (grad["out"], grad["pack"], layer_out)
        seq_terms, beside = scatter_slots(ngs, beside)
        mem_terms = scatter_slots(cut(ngm, 4))
        if number == 0:
            for own, send in zip((*out_owns, *pack_owns), (*out_sends, *pack_sends)):
                sums.add(own, swap_section(send))
            sums.token = ngs[0]
            sums.turn(0)
            sums.turn(2)
            sums.turn(1)
            seq_terms = (*seq_terms[0:2], sums.before(seq_terms[2]))
        else:
            grad["out"], grad["pack"], layer_out = beside
        input_grad, input_low, small1 = norm_back(saved["rows"], seq_terms, layer["gain1"], hidden_grad)
        small_mem = norm_back_small(layer["mem"], mem_terms)
        input_grads[number] = input_low
        vec = jnp.concatenate([(small1 + small_mem)[0:2], small2[0:3], jnp.zeros_like(small2[0:3])], axis=0)
        vec = vec + to_core(vec)
        vec = vec + to_chip(vec)
        smalls_out[number] = jnp.concatenate([vec[0:5], near_bias + far_bias, vec[6:8]], axis=0)
        if number == 1:
            g_rows = input_low
            g_slots = gather_slots(input_low)

    vec_own = jnp.where(first, smalls_out[0], smalls_out[1])
    vec_got = swap_section(jnp.where(first, smalls_out[1], smalls_out[0]))
    last_chunk = sums.chunks[-1]
    last_chunk["own"], last_chunk["moving"] = (last_chunk["own"], vec_own), (last_chunk["moving"], vec_got)
    for newest in range(3, len(sums.chunks) + 3):
        for number in range(min(newest, len(sums.chunks) - 1), -1, -1):
            if sums.chunks[number]["step"] < 4:
                sums.turn(number)
    *chunks, (last, vec) = [chunk["end"] for chunk in sums.chunks]
    input_grad = by_layer(*input_grads)
    down_sum = jnp.concatenate(chunks[0:2], axis=0).astype(f32)
    up_sum = jnp.concatenate(chunks[2:4], axis=0).astype(f32)
    out_sum = chunks[4].astype(f32)
    pack_sum = jnp.concatenate([chunks[5], last], axis=0).astype(f32)
    value_sum, key_sum, query_sum = pack_sum[:value_rows], pack_sum[value_rows : value_rows + head_width], pack_sum[value_rows + head_width : value_rows + 2 * head_width]
    vroute_sum = pack_sum[value_rows + 2 * head_width : value_rows + 2 * head_width + experts]
    oroute_sum = pack_sum[value_rows + 2 * head_width + out_lane : value_rows + 2 * head_width + out_lane + experts]

    return (
        layer_out,
        input_grad,
        vec[0:1],
        vec[1:2],
        query_sum.T[None, None],
        key_sum.T[None, None],
        value_sum.T[None, None],
        vroute_sum.T[None, None],
        oroute_sum.T[None, None],
        out_sum[None, None],
        vec[2:3],
        vec[3:4],
        up_sum[None],
        vec[5:6],
        down_sum[None],
        vec[4:5],
    )


def solution(mesh):
    placed = (
        P("dp", "head", None),
        P("section", "dp", "head", None),
        P("section", "dp", None, "head", None),
        P("section", "dp", None, "head", None),
        P("section", None),
        P("section", None),
        P("section", "head", None, None),
        P("section", "head", None, None),
        P("section", "head", None, None),
        P("section", "head", None, None),
        P("section", "head", None, None),
        P("section", "head", None, None),
        P("section", None),
        P("section", None),
        P("section", None, "head"),
        P("section", "head"),
        P("section", "head", None),
        P("section", None),
        P("dp", "head", None),
    )
    return jax.shard_map(
        on_device,
        mesh=mesh,
        in_specs=placed,
        out_specs=(
            P("section", "dp", "head", None),
            P("section", "dp", "head", None),
            P("section", None),
            P("section", None),
            P("section", "head", None, None),
            P("section", "head", None, None),
            P("section", "head", None, None),
            P("section", "head", None, None),
            P("section", "head", None, None),
            P("section", "head", None, None),
            P("section", None),
            P("section", None),
            P("section", None, "head"),
            P("section", "head"),
            P("section", "head", None),
            P("section", None),
        ),
        check_vma=False,
    )
```

```python
import functools

import jax
import jax.numpy as jnp
from jax import lax
from jax.experimental import pallas as pl
from jax.experimental.pallas import tpu as pltpu
from jax.sharding import PartitionSpec as P

norm_eps = 1e-05
masked_score = -1e30
lanes = 128
out_lane = 8
log_lane = 16
bf16 = jnp.bfloat16
f32 = jnp.float32
gelu_c = 0.7978845608028654
gelu_a = 0.044715

core_pairs = [(0, 1), (1, 0), (2, 3), (3, 2)]
chip_pairs = [(0, 2), (2, 0), (1, 3), (3, 1)]
vmem_bytes = 50 * 1024 * 1024


def dot(a, b):
    return lax.dot_general(a, b, (((1,), (0,)), ((), ())), preferred_element_type=f32)


def dot_t(a, b):
    return lax.dot_general(a, b, (((1,), (1,)), ((), ())), preferred_element_type=f32)


def t_dot(a, b):
    return lax.dot_general(a, b, (((0,), (0,)), ((), ())), preferred_element_type=f32)


def params(**more):
    return pltpu.CompilerParams(vmem_limit_bytes=vmem_bytes, **more)


def whole_spec(shape):
    return pl.BlockSpec(shape, lambda *_: (0,) * len(shape))


def cost(flops, nbytes, trans=0):
    return pl.CostEstimate(flops=int(flops), bytes_accessed=int(nbytes), transcendentals=int(trans))


def to_core(a):
    return lax.ppermute(a, "head", core_pairs)


def to_chip(a):
    return lax.ppermute(a, "head", chip_pairs)


def swap_section(a):
    return lax.ppermute(a, "section", [(0, 1), (1, 0)])


def after(a, *tokens):
    return lax.optimization_barrier((a, tokens))[0]


def gather_slots(own, work=None):
    from_chip = to_chip(own)
    from_core = to_core(own)
    if work is None:
        return [own, from_core, from_chip, to_core(from_chip)]
    from_chip, done = lax.optimization_barrier((from_chip, work([own, from_core])))
    return [own, from_core, from_chip, to_core(from_chip)], done


def scatter_slots(parts, work=None, start_after=None):
    from_core_far = to_core(parts[3])
    from_core = to_core(parts[1])
    far = (parts[2].astype(f32) + from_core_far.astype(f32)).astype(bf16)
    if start_after is not None:
        far = after(far, start_after)
    from_chip = to_chip(far)
    if work is None:
        return parts[0], from_core, from_chip
    from_chip, done = lax.optimization_barrier((from_chip, work(far)))
    return (parts[0], from_core, from_chip), done


def norm_rows(x, gain, shift):
    average = jnp.mean(x, axis=-1, keepdims=True)
    centred = x - average
    variance = jnp.mean(centred * centred, axis=-1, keepdims=True)
    return centred * lax.rsqrt(variance + norm_eps) * gain + shift


def norm_kernel(x_ref, gain_ref, shift_ref, out_ref):
    out_ref[...] = norm_rows(x_ref[...].astype(f32), gain_ref[...], shift_ref[...]).astype(bf16)


def norm_only(x, gain, shift):
    return pl.pallas_call(
        norm_kernel,
        out_shape=jax.ShapeDtypeStruct(x.shape, bf16),
        compiler_params=params(),
        cost_estimate=cost(x.size * 8, x.size * 4),
        name="norm_only",
    )(x, gain, shift)


def add_norm_kernel(x_ref, a_ref, b_ref, c_ref, add_ref, gain_ref, shift_ref, sum_ref, out_ref):
    total = x_ref[...].astype(f32) + (a_ref[...].astype(f32) + b_ref[...].astype(f32) + c_ref[...].astype(f32))
    total = total + add_ref[...]
    sum_ref[...] = total.astype(sum_ref.dtype)
    total = sum_ref[...].astype(f32)
    out_ref[...] = norm_rows(total, gain_ref[...], shift_ref[...]).astype(bf16)


def add_norm(x, terms, add, gain, shift, sum_type):
    return pl.pallas_call(
        add_norm_kernel,
        out_shape=(jax.ShapeDtypeStruct(x.shape, sum_type), jax.ShapeDtypeStruct(x.shape, bf16)),
        compiler_params=params(),
        cost_estimate=cost(x.size * 12, x.size * 14),
        name="add_norm",
    )(x, *terms, add, gain, shift)


def norm_back_kernel(x_ref, a_ref, b_ref, c_ref, gain_ref, more_ref, dx_ref, low_ref, small_ref):
    x = x_ref[...].astype(f32)
    grad = a_ref[...].astype(f32) + b_ref[...].astype(f32) + c_ref[...].astype(f32)
    average = jnp.mean(x, axis=-1, keepdims=True)
    centred = x - average
    variance = jnp.mean(centred * centred, axis=-1, keepdims=True)
    scale = lax.rsqrt(variance + norm_eps)
    unit = centred * scale
    wide = grad * gain_ref[...]
    mean_wide = jnp.mean(wide, axis=-1, keepdims=True)
    mean_unit = jnp.mean(wide * unit, axis=-1, keepdims=True)
    more = more_ref[...].astype(f32)
    dx = more + scale * (wide - mean_wide - unit * mean_unit)
    dx_ref[...] = dx
    low_ref[...] = dx.astype(bf16)
    small_ref[0:1, :] = jnp.sum(grad * unit, axis=0, keepdims=True)
    small_ref[1:2, :] = jnp.sum(grad, axis=0, keepdims=True)
    small_ref[2:3, :] = jnp.sum(more, axis=0, keepdims=True)
    small_ref[3:8, :] = jnp.zeros((5, x.shape[1]), f32)


def norm_back(x, terms, gain, more):
    return pl.pallas_call(
        norm_back_kernel,
        out_shape=(
            jax.ShapeDtypeStruct(x.shape, f32),
            jax.ShapeDtypeStruct(x.shape, bf16),
            jax.ShapeDtypeStruct((8, x.shape[1]), f32),
        ),
        compiler_params=params(),
        cost_estimate=cost(x.size * 20, x.size * 20),
        name="norm_back",
    )(x, *terms, gain, more)


def norm_back_small_kernel(x_ref, a_ref, b_ref, c_ref, small_ref):
    x = x_ref[...].astype(f32)
    grad = a_ref[...].astype(f32) + b_ref[...].astype(f32) + c_ref[...].astype(f32)
    average = jnp.mean(x, axis=-1, keepdims=True)
    centred = x - average
    variance = jnp.mean(centred * centred, axis=-1, keepdims=True)
    unit = centred * lax.rsqrt(variance + norm_eps)
    small_ref[0:1, :] = jnp.sum(grad * unit, axis=0, keepdims=True)
    small_ref[1:2, :] = jnp.sum(grad, axis=0, keepdims=True)
    small_ref[2:8, :] = jnp.zeros((6, x.shape[1]), f32)


def norm_back_small(x, terms):
    return pl.pallas_call(
        norm_back_small_kernel,
        out_shape=jax.ShapeDtypeStruct((8, x.shape[1]), f32),
        compiler_params=params(),
        cost_estimate=cost(x.size * 10, x.size * 8),
        name="norm_back_small",
    )(x, *terms)


def pick_slot(slot, refs, target):
    for number, ref in enumerate(refs):

        @pl.when(slot == number)
        def _(ref=ref):
            target[...] = ref[...]


def store_slot(slot, refs, block):
    for number, ref in enumerate(refs):

        @pl.when(slot == number)
        def _(ref=ref):
            ref[...] = block


def fill_experts(target, source, experts, width):
    for j in range(experts):
        target[j * lanes : j * lanes + width, :] = source[j * width : (j + 1) * width, :]
        target[j * lanes + width : (j + 1) * lanes, :] = jnp.zeros((lanes - width, target.shape[1]), bf16)


def fill_weights(w_s, wo_s, wv_ref, wk_ref, wo_ref, experts, width):
    fill_experts(w_s, wv_ref, experts, width)
    fill_experts(wo_s, wo_ref, experts, width)
    start = 0
    for place, rows in ((experts + 1, width), (experts + 2, width), (experts, 2 * out_lane)):
        w_s[place * lanes : place * lanes + rows, :] = wk_ref[start : start + rows, :]
        w_s[place * lanes + rows : (place + 1) * lanes, :] = jnp.zeros((lanes - rows, w_s.shape[1]), bf16)
        start += rows


def attn_fwd_kernel(
    experts,
    head_width,
    me_ref,
    m0_ref,
    m1_ref,
    m2_ref,
    m3_ref,
    p0_ref,
    p1_ref,
    p2_ref,
    p3_ref,
    wv_ref,
    wk_ref,
    wo_ref,
    mask_ref,
    o0_ref,
    o1_ref,
    o2_ref,
    o3_ref,
    normed_ref,
    q_ref,
    k_ref,
    v_ref,
    ev_ref,
    gate_ref,
    att_ref,
    mixed_ref,
    rows_s,
    k_s,
    v_s,
    mask_s,
    w_s,
    wo_s,
):
    step = pl.program_id(0)
    me = me_ref[0]
    block = rows_s.shape[0]
    wide = experts * lanes
    quarter = block // 4

    @pl.when(step == 0)
    def _():
        fill_weights(w_s, wo_s, wv_ref, wk_ref, wo_ref, experts, head_width)
        for slot, mem_ref in enumerate((m0_ref, m1_ref, m2_ref, m3_ref)):
            rows_s[slot * quarter : (slot + 1) * quarter, :] = mem_ref[...]
            start = pl.multiple_of((me ^ slot) * quarter, quarter)
            mask_s[slot * quarter : (slot + 1) * quarter, :] = mask_ref[pl.ds(start, quarter), :]

    @pl.when(step > 0)
    def _():
        pick_slot((step - 1) ^ me, (p0_ref, p1_ref, p2_ref, p3_ref), rows_s)
        mask_s[...] = mask_ref[pl.ds(pl.multiple_of(step * block, block), block), :]

    x = rows_s[...]
    normed_ref[...] = x
    proj = dot_t(x, w_s[...])
    gate = jax.nn.sigmoid(proj[:, wide : wide + lanes]) * mask_s[...]
    value = jnp.zeros((block, lanes), f32)
    for j in range(experts):
        value = value + gate[:, j : j + 1] * proj[:, j * lanes : (j + 1) * lanes]
    start = pl.multiple_of(step * block, block)
    keys = proj[:, wide + lanes : wide + 2 * lanes].astype(bf16)
    value = value.astype(bf16)
    k_s[pl.ds(start, block), :] = keys
    v_s[pl.ds(start, block), :] = value
    k_ref[...] = keys
    v_ref[...] = value
    ev_ref[...] = proj[:, :wide].astype(bf16)
    queries = proj[:, wide + 2 * lanes :].astype(bf16)
    q_ref[...] = queries

    @pl.when(step == 0)
    def _():
        gate_ref[...] = gate

    scale = head_width ** (-0.5)
    for count in range(1, 5):

        @pl.when(step == count)
        def _(count=count):
            span = (count + 1) * block
            scores = dot_t(queries, k_s[0:span, :]) * scale
            row = lax.broadcasted_iota(jnp.int32, (block, block), 0)
            col = lax.broadcasted_iota(jnp.int32, (block, block), 1)
            last = jnp.where(col <= row, scores[:, span - block :], masked_score)
            scores = jnp.concatenate([scores[:, : span - block], last], axis=1)
            top = jnp.max(scores, axis=-1, keepdims=True)
            exponent = jnp.exp(scores - top)
            total = jnp.sum(exponent, axis=-1, keepdims=True)
            probs = (exponent * (1.0 / total)).astype(bf16)
            attended = dot(probs, v_s[0:span, :])
            att_ref[...] = attended
            lane = lax.broadcasted_iota(jnp.int32, (block, lanes), 1)
            gate_ref[...] = jnp.where(lane == log_lane, top + jnp.log(total), gate)
            mixed = jnp.concatenate(
                [(gate[:, out_lane + j : out_lane + j + 1] * attended).astype(bf16) for j in range(experts)], axis=1
            )
            mixed_ref[...] = mixed
            store_slot((count - 1) ^ me, (o0_ref, o1_ref, o2_ref, o3_ref), dot(mixed, wo_s[...]).astype(bf16))


def attn_fwd(me, mems, slots, w, mask, experts, head_width):
    block, width = slots[0].shape
    total = 5 * block
    wide = experts * lanes
    later = lambda i, me_ref: (jnp.maximum(i - 1, 0), 0)
    every = lambda i, me_ref: (i, 0)
    shapes = lambda rows, cols, kind: jax.ShapeDtypeStruct((rows, cols), kind)
    grid_spec = pltpu.PrefetchScalarGridSpec(
        num_scalar_prefetch=1,
        grid=(5,),
        in_specs=[whole_spec((block // 4, width))] * 4
        + [whole_spec((block, width))] * 4
        + [whole_spec(a.shape) for a in w]
        + [whole_spec(mask.shape)],
        out_specs=[
            *[whole_spec((block, width))] * 4,
            pl.BlockSpec((block, width), every),
            pl.BlockSpec((block, lanes), every),
            pl.BlockSpec((block, lanes), every),
            pl.BlockSpec((block, lanes), every),
            pl.BlockSpec((block, wide), every),
            pl.BlockSpec((block, lanes), every),
            pl.BlockSpec((block, lanes), later),
            pl.BlockSpec((block, wide), later),
        ],
        scratch_shapes=[
            pltpu.VMEM((block, width), bf16),
            pltpu.VMEM((total, lanes), bf16),
            pltpu.VMEM((total, lanes), bf16),
            pltpu.VMEM((block, lanes), f32),
            pltpu.VMEM((wide + 3 * lanes, width), bf16),
            pltpu.VMEM((wide, width), bf16),
        ],
    )
    return pl.pallas_call(
        functools.partial(attn_fwd_kernel, experts, head_width),
        grid_spec=grid_spec,
        out_shape=(
            *[shapes(block, width, bf16)] * 4,
            shapes(total, width, bf16),
            shapes(total, lanes, bf16),
            shapes(total, lanes, bf16),
            shapes(total, lanes, bf16),
            shapes(total, wide, bf16),
            shapes(total, lanes, f32),
            shapes(4 * block, lanes, f32),
            shapes(4 * block, wide, bf16),
        ),
        compiler_params=params(dimension_semantics=("arbitrary",)),
        cost_estimate=cost(4 * total * width * wide, 16 * 1024 * 1024, total * total),
        name="attn_fwd",
    )(me, *mems, *slots, *w, mask)


def attn_bwd_kernel(
    experts,
    head_width,
    me_ref,
    d0_ref,
    d1_ref,
    d2_ref,
    d3_ref,
    wv_ref,
    wk_ref,
    wo_ref,
    q_ref,
    k_ref,
    v_ref,
    ev_ref,
    gate_ref,
    att_ref,
    n0_ref,
    n1_ref,
    n2_ref,
    n3_ref,
    ngm_ref,
    dproj_ref,
    da_ref,
    rows_s,
    dk_s,
    dv_s,
    dq_s,
    dlog_s,
    w_s,
    wo_s,
):
    step = pl.program_id(0)
    me = me_ref[0]
    here = 4 - step
    block = rows_s.shape[0]
    wide = experts * lanes
    scale = head_width ** (-0.5)
    gate = gate_ref[...]
    lane = lax.broadcasted_iota(jnp.int32, (block, lanes), 1)

    @pl.when(step == 0)
    def _():
        fill_weights(w_s, wo_s, wv_ref, wk_ref, wo_ref, experts, head_width)
        dk_s[...] = jnp.zeros_like(dk_s)
        dv_s[...] = jnp.zeros_like(dv_s)

    @pl.when(here == 0)
    def _():
        dq_s[...] = jnp.zeros_like(dq_s)
        dlog_s[...] = jnp.zeros_like(dlog_s)

    for count in range(1, 5):

        @pl.when(here == count)
        def _(count=count):
            pick_slot((count - 1) ^ me, (d0_ref, d1_ref, d2_ref, d3_ref), rows_s)
            rows = rows_s[...]
            da_ref[...] = rows
            mixed_grad = dot_t(rows, wo_s[...])
            attended = att_ref[...]
            att_grad = jnp.zeros((block, lanes), f32)
            logit_grad = jnp.zeros((block, lanes), f32)
            for j in range(experts):
                part = mixed_grad[:, j * lanes : (j + 1) * lanes]
                att_grad = att_grad + gate[:, out_lane + j : out_lane + j + 1] * part
                inner = jnp.sum(part * attended, axis=-1, keepdims=True)
                logit_grad = jnp.where(lane == out_lane + j, inner, logit_grad)
            dlog_s[...] = logit_grad
            grad_low = att_grad.astype(bf16)
            row_sum = jnp.sum(att_grad * attended, axis=-1, keepdims=True)
            log_total = gate[:, log_lane : log_lane + 1]
            span = (count + 1) * block
            queries = q_ref[...]
            keys = k_ref[0:span, :]
            scores = dot_t(queries, keys) * scale
            row = lax.broadcasted_iota(jnp.int32, (block, block), 0)
            col = lax.broadcasted_iota(jnp.int32, (block, block), 1)
            last = jnp.where(col <= row, scores[:, span - block :], masked_score)
            scores = jnp.concatenate([scores[:, : span - block], last], axis=1)
            probs = jnp.exp(scores - log_total)
            probs_grad = dot_t(grad_low, v_ref[0:span, :])
            score_grad = (probs * (probs_grad - row_sum)).astype(bf16)
            dq_s[...] = dot(score_grad, keys) * scale
            dk_s[0:span, :] += t_dot(score_grad, queries)
            dv_s[0:span, :] += t_dot(probs.astype(bf16), grad_low)

    start = pl.multiple_of(here * block, block)
    value_grad = dv_s[pl.ds(start, block), :].astype(bf16).astype(f32)
    parts = []
    logit_grad = dlog_s[...]
    for j in range(experts):
        parts.append((gate[:, j : j + 1] * value_grad).astype(bf16))
        inner = jnp.sum(value_grad * ev_ref[:, j * lanes : (j + 1) * lanes].astype(f32), axis=-1, keepdims=True)
        logit_grad = jnp.where(lane == j, inner, logit_grad)
    slope = jnp.where(lane < log_lane, gate * (1.0 - gate), 0.0)
    parts.append((logit_grad * slope).astype(bf16))
    parts.append((dk_s[pl.ds(start, block), :] * scale).astype(bf16))
    parts.append(dq_s[...].astype(bf16))
    dproj = jnp.concatenate(parts, axis=1)
    dproj_ref[...] = dproj
    normed_grad = dot(dproj, w_s[...]).astype(bf16)

    @pl.when(here > 0)
    def _():
        store_slot((here - 1) ^ me, (n0_ref, n1_ref, n2_ref, n3_ref), normed_grad)

    @pl.when(here == 0)
    def _():
        ngm_ref[...] = normed_grad


def attn_bwd(me, slots, w, saved, experts, head_width):
    q, k, v, ev, gate, att = saved
    block, width = slots[0].shape
    total = 5 * block
    wide = experts * lanes
    back = lambda i, me_ref: (4 - i, 0)
    later = lambda i, me_ref: (jnp.maximum(3 - i, 0), 0)
    grid_spec = pltpu.PrefetchScalarGridSpec(
        num_scalar_prefetch=1,
        grid=(5,),
        in_specs=[whole_spec((block, width))] * 4
        + [whole_spec(a.shape) for a in w]
        + [
            pl.BlockSpec((block, lanes), back),
            whole_spec(k.shape),
            whole_spec(v.shape),
            pl.BlockSpec((block, wide), back),
            pl.BlockSpec((block, lanes), back),
            pl.BlockSpec((block, lanes), later),
        ],
        out_specs=[
            *[whole_spec((block, width))] * 5,
            pl.BlockSpec((block, wide + 3 * lanes), back),
            pl.BlockSpec((block, width), later),
        ],
        scratch_shapes=[
            pltpu.VMEM((block, width), bf16),
            pltpu.VMEM((total, lanes), f32),
            pltpu.VMEM((total, lanes), f32),
            pltpu.VMEM((block, lanes), f32),
            pltpu.VMEM((block, lanes), f32),
            pltpu.VMEM((wide + 3 * lanes, width), bf16),
            pltpu.VMEM((wide, width), bf16),
        ],
    )
    return pl.pallas_call(
        functools.partial(attn_bwd_kernel, experts, head_width),
        grid_spec=grid_spec,
        out_shape=(
            *[jax.ShapeDtypeStruct((block, width), bf16)] * 5,
            jax.ShapeDtypeStruct((total, wide + 3 * lanes), bf16),
            jax.ShapeDtypeStruct((4 * block, width), bf16),
        ),
        compiler_params=params(dimension_semantics=("arbitrary",)),
        cost_estimate=cost(4 * total * width * wide, 16 * 1024 * 1024, total * total),
        name="attn_bwd",
    )(me, *slots, *w, q, k, v, ev, gate, att)


def ffn_fwd_kernel(a_ref, b_ref, wu_ref, bu_ref, wd_ref, *refs):
    oa_ref, ob_ref, rows_ref, upper_ref, active_ref = refs[-5:]
    half = a_ref.shape[0]
    rows_ref[0:half, :] = a_ref[...]
    rows_ref[half:, :] = b_ref[...]
    upper = dot(rows_ref[...], wu_ref[...]) + bu_ref[...]
    upper_ref[...] = upper.astype(bf16)
    active_ref[...] = jax.nn.gelu(upper).astype(bf16)
    out = dot(active_ref[...], wd_ref[...]).astype(bf16)
    oa_ref[...] = out[0:half]
    ob_ref[...] = out[half:]


def ffn_fwd(pair, number, wu, bu, wd, earlier):
    block, width = pair[0].shape
    hidden = wu.shape[1]
    here = lambda i: (number, 0)
    specs = [whole_spec((block, width))] * 2 + [whole_spec(wu.shape), whole_spec(bu.shape), whole_spec(wd.shape)]
    return pl.pallas_call(
        ffn_fwd_kernel,
        grid=(1,),
        in_specs=specs + [pl.BlockSpec(memory_space=pl.ANY)] * len(earlier),
        out_specs=[whole_spec((block, width))] * 2
        + [pl.BlockSpec((2 * block, width), here)]
        + [pl.BlockSpec((2 * block, hidden), here)] * 2,
        out_shape=(
            jax.ShapeDtypeStruct((block, width), bf16),
            jax.ShapeDtypeStruct((block, width), bf16),
            jax.ShapeDtypeStruct((4 * block, width), bf16),
            jax.ShapeDtypeStruct((4 * block, hidden), bf16),
            jax.ShapeDtypeStruct((4 * block, hidden), bf16),
        ),
        input_output_aliases={5 + i: 2 + i for i in range(len(earlier))},
        compiler_params=params(),
        cost_estimate=cost(8 * block * width * hidden, 9 * 1024 * 1024, 2 * block * hidden),
        name="ffn_fwd",
    )(*pair, wu, bu, wd, *earlier)


def ffn_bwd_kernel(a_ref, b_ref, upper_ref, wd_ref, wu_ref, *refs):
    oa_ref, ob_ref, bias_ref, rows_ref, ug_ref = refs[-5:]
    half = a_ref.shape[0]
    rows_ref[0:half, :] = a_ref[...]
    rows_ref[half:, :] = b_ref[...]
    active_grad = dot_t(rows_ref[...], wd_ref[...])
    u = upper_ref[...].astype(f32)
    square = u * u
    t = jnp.tanh(gelu_c * u * (1.0 + gelu_a * square))
    slope = 0.5 * (1.0 + t) + 0.5 * gelu_c * u * (1.0 - t * t) * (1.0 + 3.0 * gelu_a * square)
    upper_grad = (active_grad * slope).astype(bf16)
    ug_ref[...] = upper_grad
    bias_ref[...] = jnp.sum(upper_grad.astype(f32), axis=0, keepdims=True)
    out = dot_t(ug_ref[...], wu_ref[...]).astype(bf16)
    oa_ref[...] = out[0:half]
    ob_ref[...] = out[half:]


def ffn_bwd(pair, number, upper, wd, wu, earlier):
    block, width = pair[0].shape
    hidden = wu.shape[1]
    here = lambda i: (number, 0)
    specs = [whole_spec((block, width))] * 2
    specs += [pl.BlockSpec((2 * block, hidden), here), whole_spec(wd.shape), whole_spec(wu.shape)]
    return pl.pallas_call(
        ffn_bwd_kernel,
        grid=(1,),
        in_specs=specs + [pl.BlockSpec(memory_space=pl.ANY)] * len(earlier),
        out_specs=[whole_spec((block, width))] * 2
        + [whole_spec((1, hidden)), pl.BlockSpec((2 * block, width), here), pl.BlockSpec((2 * block, hidden), here)],
        out_shape=(
            jax.ShapeDtypeStruct((block, width), bf16),
            jax.ShapeDtypeStruct((block, width), bf16),
            jax.ShapeDtypeStruct((1, hidden), f32),
            jax.ShapeDtypeStruct((4 * block, width), bf16),
            jax.ShapeDtypeStruct((4 * block, hidden), bf16),
        ),
        input_output_aliases={5 + i: 3 + i for i in range(len(earlier))},
        compiler_params=params(),
        cost_estimate=cost(8 * block * width * hidden, 9 * 1024 * 1024, 2 * block * hidden),
        name="ffn_bwd",
    )(*pair, upper, wd, wu, *earlier)


def plus(a, b):
    return jax.tree.map(lambda one, two: (one.astype(f32) + two.astype(f32)).astype(one.dtype), a, b)


def move(a, axis, pairs):
    return jax.tree.map(lambda one: lax.ppermute(one, axis, pairs), a)


class ChunkSums:
    def __init__(self):
        self.chunks = []
        self.token = None
        self.direct = lax.axis_size("dp") != 4
        place = lax.axis_index("dp")
        self.middle = (place == 1) | (place == 2)

    def add(self, own, got):
        self.chunks.append(dict(own=own, moving=got, step=0))

    def turn(self, number):
        chunk = self.chunks[number]
        got = chunk["moving"] if self.token is None else after(chunk["moving"], self.token)
        step = chunk["step"]
        chunk["step"] += 1
        if self.direct:
            if step == 0:
                chunk["end"] = lax.psum(plus(chunk["own"], got), "dp")
            return
        if step == 3:
            chunk["end"] = jax.tree.map(lambda full, far: jnp.where(self.middle, full, far), chunk["own"], got)
            return
        total = plus(chunk["own"], got)
        pairs = ([(0, 1), (3, 2)], [(1, 2), (2, 1)], [(1, 0), (2, 3)])[step]
        chunk["own"], chunk["moving"] = total, move(total, "dp", pairs)
        self.token = total

    def before(self, a):
        return a if self.token is None else after(a, self.token)


def cut(a, pieces):
    rows = a.shape[0] // pieces
    return [a[i * rows : (i + 1) * rows] for i in range(pieces)]


def padded_rows(a, rows):
    return jnp.pad(a, ((0, rows - a.shape[0]), (0, 0)))


def squeeze_out(wide, experts, width):
    return jnp.concatenate([wide[j * lanes : j * lanes + width] for j in range(experts)], axis=0)


def squeeze(wide, experts, width):
    base = experts * lanes
    parts = [wide[j * lanes : j * lanes + width] for j in range(experts)]
    parts.append(wide[base + lanes : base + lanes + width])
    parts.append(wide[base + 2 * lanes : base + 2 * lanes + width])
    parts.append(wide[base : base + 2 * out_lane])
    return jnp.concatenate(parts, axis=0)


def swap_weights(weights, start_after):
    size = lax.axis_size("dp")
    odd = lax.axis_index("dp") % 2
    results = []
    gots = []
    for a, pieces in weights:
        parts = []
        for part in cut(a, pieces):
            part = after(part, start_after, *gots[: max(0, len(gots) - 1)])
            if size % 2:
                gots.append(swap_section(part))
                parts.append(gots[-1])
                continue
            rows = part.shape[0] // 2
            gots.append(swap_section(lax.dynamic_slice_in_dim(part, odd * rows, rows, 0)))
            got = gots[-1]
            other = lax.ppermute(got, "dp", [(i, i ^ 1) for i in range(size)])
            parts += [jnp.where(odd == 0, got, other), jnp.where(odd == 0, other, got)]
        results.append(jnp.concatenate(parts, axis=0))
    return results


def route_mask(value_ids, out_ids, experts, memory_len):
    lane = jnp.arange(lanes, dtype=jnp.int32)[None, :]
    out_full = jnp.pad(out_ids, ((0, 0), (memory_len, 0)), constant_values=-1)
    hit = jnp.zeros((value_ids.shape[1], lanes), jnp.bool_)
    for k in range(value_ids.shape[0]):
        hit = hit | (lane == value_ids[k][:, None])
        hit = hit | ((lane == out_full[k][:, None] + out_lane) & (out_full[k][:, None] >= 0))
    return hit.astype(f32)


def on_device(
    inputs,
    memory,
    value_routes,
    out_routes,
    ln1_gain,
    ln1_bias,
    query_weight,
    key_weight,
    value_weight,
    value_router,
    out_router,
    output_weight,
    ln2_gain,
    ln2_bias,
    up_weight,
    up_bias,
    down_weight,
    down_bias,
    out_cot,
):
    experts = value_router.shape[-1]
    head_width = query_weight.shape[-1]
    sec = lax.axis_index("section")
    head = lax.axis_index("head")
    me = head.astype(jnp.int32).reshape(1)
    first = sec == 0
    pick = lambda a, index: lax.dynamic_index_in_dim(a, index, 0, keepdims=False)
    memory_len = memory.shape[2] * lax.axis_size("head")

    value_rows = experts * head_width
    router_rows = [padded_rows(a[0, 0].T, out_lane) for a in (value_router, out_router)]
    kqr = jnp.concatenate([key_weight[0, 0].T, query_weight[0, 0].T, *router_rows])
    weights = [value_weight[0, 0].T, kqr, output_weight[0, 0], up_weight[0], down_weight[0]]

    small = jnp.concatenate([ln1_gain, ln1_bias, ln2_gain, ln2_bias, up_bias, down_bias, ln1_gain, ln1_bias], axis=0)
    route_rows = jnp.concatenate(
        [
            jnp.transpose(value_routes[0, :, :, 0, :], (0, 2, 1)),
            jnp.pad(jnp.transpose(out_routes[0, :, :, 0, :], (0, 2, 1)), ((0, 0), (0, 0), (memory_len, 0)), constant_values=-1),
        ],
        axis=1,
    )
    sends = [small, pick(memory[0], 1 - sec), pick(route_rows, 1 - sec)]
    small_got, memory_got, routes_got = [swap_section(a) for a in sends]

    def both_layers(own, got):
        return jnp.where(first, own, got), jnp.where(first, got, own)

    smalls = both_layers(small, small_got)
    route_sets = both_layers(pick(route_rows, sec), routes_got)
    memories = both_layers(pick(memory[0], sec), memory_got)
    weights_got = swap_weights(list(zip(weights, (1, 1, 1, 1, 1))), sends)
    weight_sets = [both_layers(a, got) for a, got in zip(weights, weights_got)]

    x = pick(inputs, sec)
    cot = pick(out_cot, sec)
    own_norm = norm_only(x, smalls[0][0:1], smalls[0][1:2])
    slots = gather_slots(own_norm)
    route_sets = after(route_sets, own_norm)
    topk = value_routes.shape[-1]

    layers = []
    for number in range(2):
        vec = smalls[number]
        routes = route_sets[number]
        layers.append(
            dict(
                gain1=vec[0:1],
                shift1=vec[1:2],
                gain2=vec[2:3],
                shift2=vec[3:4],
                up_b=vec[4:5],
                down_b=vec[5:6],
                w=(weight_sets[0][number], weight_sets[1][number], weight_sets[2][number]),
                wu=weight_sets[3][number],
                wd=weight_sets[4][number],
                mask=route_mask(routes[:topk], routes[topk:, memory_len:], experts, memory_len),
                mem=memories[number],
            )
        )
    no_add = jnp.zeros_like(layers[0]["gain1"])

    for layer in layers:
        layer["mem_slots"] = gather_slots(norm_only(after(layer["mem"], own_norm), layer["gain1"], layer["shift1"]))
    cot_slots = gather_slots(after(cot, slots[2], layers[0]["mem_slots"][2]))
    slots[3] = after(slots[3], layers[0]["mask"], layers[1]["mask"])

    saves = []
    rows_in = x
    layer_outs = []
    for number, layer in enumerate(layers):
        *out, normed, q, k, v, ev, gate, att, mixed = attn_fwd(
            me, layer["mem_slots"], slots, layer["w"], layer["mask"], experts, head_width
        )
        if number == 0:
            out[3] = after(out[3], cot_slots[2], layers[1]["mem_slots"][2])
        terms = scatter_slots(out)
        hidden, own_norm2 = add_norm(rows_in, terms, no_add, layer["gain2"], layer["shift2"], f32)
        wu, wd = layer["wu"], layer["wd"]

        def near_work(near):
            done = ffn_fwd(near, 0, wu, layer["up_b"], wd, ())
            return done, (ffn_bwd(cot_slots[0:2], 0, done[3], wd, wu, ()) if number == 1 else ())

        n2_slots, ((near_a, near_b, *kept), near_back) = gather_slots(own_norm2, near_work)
        far_a, far_b, n2, upper, active = ffn_fwd(n2_slots[2:4], 1, wu, layer["up_b"], wd, kept)
        saves.append(
            dict(rows=rows_in, normed=normed, attn=(q, k, v, ev, gate, att), mixed=mixed, hidden=hidden, n2=n2, upper=upper, active=active)
        )
        if number == 0:
            terms = scatter_slots([near_a, near_b, far_a, far_b])
            rows_in, own_norm = add_norm(hidden, terms, layer["down_b"], layers[1]["gain1"], layers[1]["shift1"], bf16)
            layer_outs.append(rows_in)
            slots = gather_slots(own_norm)
        else:
            last_parts = [near_a, near_b, far_a, far_b]

    def by_layer(one, two):
        got = swap_section(jnp.where(first, two, one))
        kept = jnp.where(first, one, two)
        return jnp.stack([jnp.where(first, kept, got), jnp.where(first, got, kept)])[None]

    def send_chunks(one, two, pieces):
        chunks = []
        for part_one, part_two in zip(cut(one, pieces), cut(two, pieces)):
            send = jnp.where(first, part_two, part_one)
            sums.add(jnp.where(first, part_one, part_two), swap_section(send))
            chunks.append(send)
        return chunks

    sums = ChunkSums()
    grads = [{}, {}]
    smalls_out = [None, None]
    input_grads = [None, None]
    g_rows = cot
    g_slots = cot_slots
    for number in (1, 0):
        layer, saved, grad = layers[number], saves[number], grads[number]
        wu, wd = layer["wu"], layer["wd"]
        if number == 0:
            near_work = lambda near: ffn_bwd(near, 0, saved["upper"], wd, wu, ())
            g_slots, near_back = gather_slots(g_rows, near_work)
        near_a, near_b, near_bias, *kept = near_back
        far_a, far_b, far_bias, g_all, upper_grad = ffn_bwd(g_slots[2:4], 1, saved["upper"], wd, wu, kept)

        def feed_grads(token):
            grad["down"] = t_dot(saved["active"], after(g_all, token)).astype(bf16)
            sent = send_chunks(grad["down"], grads[1]["down"], 2) if number == 0 else grad["down"]
            grad["up"] = t_dot(saved["n2"], after(upper_grad, token, sent)).astype(bf16)
            return sent, (send_chunks(grad["up"], grads[1]["up"], 2) if number == 0 else grad["up"])

        terms, (down_done, up_done) = scatter_slots([near_a, near_b, far_a, far_b], feed_grads)
        if number == 1:
            grad["down"], grad["up"] = down_done, up_done
        hidden_grad, hidden_low, small2 = norm_back(saved["hidden"], terms, layer["gain2"], g_rows)
        a_slots = gather_slots(hidden_low)
        if number == 0:
            sums.turn(0)
            a_slots[3] = sums.before(a_slots[3])
        else:
            last_terms = scatter_slots(last_parts, start_after=a_slots[2])
        *ngs, ngm, dproj, a_all = attn_bwd(me, a_slots, layer["w"], saved["attn"], experts, head_width)
        if number == 1:
            ngs[3] = after(ngs[3], last_terms[2])
            last_out, _ = add_norm(saved["hidden"], last_terms, layer["down_b"], layer["gain1"], layer["shift1"], bf16)
            layer_out = by_layer(layer_outs[0], last_out)

        def attn_grads(token):
            mixed = saved["mixed"] if token is None else after(saved["mixed"], token)
            grad["out"] = squeeze_out(t_dot(mixed, a_all).astype(bf16), experts, head_width)
            sent = send_chunks(grad["out"], grads[1]["out"], 1) if number == 0 else grad["out"]
            grad["pack"] = squeeze(t_dot(after(dproj, sent), saved["normed"]).astype(bf16), experts, head_width)
            return sent, (send_chunks(grad["pack"], grads[1]["pack"], 2) if number == 0 else grad["pack"])

        if number == 1:
            seq_terms, (grad["out"], grad["pack"], layer_out) = scatter_slots(ngs, lambda token: (*attn_grads(token), layer_out))
        else:
            sums.token = ngs[3]
            sums.turn(0)
            sums.turn(1)

            def rest(token):
                sent = attn_grads(token)
                sums.token = sent
                sums.turn(2)
                sums.turn(0)
                sums.turn(1)
                return sums.token

            seq_terms, _ = scatter_slots([*ngs[0:3], sums.before(ngs[3])], rest)
        mem_terms = scatter_slots(cut(ngm, 4))
        input_grad, input_low, small1 = norm_back(saved["rows"], seq_terms, layer["gain1"], hidden_grad)
        small_mem = norm_back_small(layer["mem"], mem_terms)
        input_grads[number] = input_low
        vec = jnp.concatenate([(small1 + small_mem)[0:2], small2[0:3], jnp.zeros_like(small2[0:3])], axis=0)
        vec = vec + to_core(vec)
        vec = vec + to_chip(vec)
        smalls_out[number] = jnp.concatenate([vec[0:5], near_bias + far_bias, vec[6:8]], axis=0)
        g_rows = input_low

    vec_own = jnp.where(first, smalls_out[0], smalls_out[1])
    vec_got = swap_section(jnp.where(first, smalls_out[1], smalls_out[0]))
    last_chunk = sums.chunks[-1]
    last_chunk["own"], last_chunk["moving"] = (last_chunk["own"], vec_own), (last_chunk["moving"], vec_got)
    for newest in range(3, len(sums.chunks) + 3):
        for number in range(newest, newest - 4, -1):
            if 0 <= number < len(sums.chunks):
                sums.turn(number)
        if newest == len(sums.chunks) - 1:
            last_sum = sums.chunks[-1]["own"]
    *chunks, (last, vec) = [chunk["end"] for chunk in sums.chunks]
    input_grad = by_layer(*[after(a, last_sum) for a in input_grads])
    down_sum = jnp.concatenate(chunks[0:2], axis=0).astype(f32)
    up_sum = jnp.concatenate(chunks[2:4], axis=0).astype(f32)
    out_sum = chunks[4].astype(f32)
    pack_sum = jnp.concatenate([chunks[5], last], axis=0).astype(f32)
    value_sum, key_sum, query_sum = pack_sum[:value_rows], pack_sum[value_rows : value_rows + head_width], pack_sum[value_rows + head_width : value_rows + 2 * head_width]
    vroute_sum = pack_sum[value_rows + 2 * head_width : value_rows + 2 * head_width + experts]
    oroute_sum = pack_sum[value_rows + 2 * head_width + out_lane : value_rows + 2 * head_width + out_lane + experts]

    return (
        layer_out,
        input_grad,
        vec[0:1],
        vec[1:2],
        query_sum.T[None, None],
        key_sum.T[None, None],
        value_sum.T[None, None],
        vroute_sum.T[None, None],
        oroute_sum.T[None, None],
        out_sum[None, None],
        vec[2:3],
        vec[3:4],
        up_sum[None],
        vec[5:6],
        down_sum[None],
        vec[4:5],
    )


def solution(mesh):
    placed = (
        P("dp", "head", None),
        P("section", "dp", "head", None),
        P("section", "dp", None, "head", None),
        P("section", "dp", None, "head", None),
        P("section", None),
        P("section", None),
        P("section", "head", None, None),
        P("section", "head", None, None),
        P("section", "head", None, None),
        P("section", "head", None, None),
        P("section", "head", None, None),
        P("section", "head", None, None),
        P("section", None),
        P("section", None),
        P("section", None, "head"),
        P("section", "head"),
        P("section", "head", None),
        P("section", None),
        P("dp", "head", None),
    )
    return jax.shard_map(
        on_device,
        mesh=mesh,
        in_specs=placed,
        out_specs=(
            P("section", "dp", "head", None),
            P("section", "dp", "head", None),
            P("section", None),
            P("section", None),
            P("section", "head", None, None),
            P("section", "head", None, None),
            P("section", "head", None, None),
            P("section", "head", None, None),
            P("section", "head", None, None),
            P("section", "head", None, None),
            P("section", None),
            P("section", None),
            P("section", None, "head"),
            P("section", "head"),
            P("section", "head", None),
            P("section", None),
        ),
        check_vma=False,
    )
```

```python
import functools

import jax
import jax.numpy as jnp
from jax import lax
from jax.experimental import pallas as pl
from jax.experimental.pallas import tpu as pltpu
from jax.sharding import PartitionSpec as P

norm_eps = 1e-05
masked_score = -1e30
lanes = 128
out_lane = 8
log_lane = 16
bf16 = jnp.bfloat16
f32 = jnp.float32
gelu_c = 0.7978845608028654
gelu_a = 0.044715

core_pairs = [(0, 1), (1, 0), (2, 3), (3, 2)]
chip_pairs = [(0, 2), (2, 0), (1, 3), (3, 1)]


def dot(a, b):
    return lax.dot_general(a, b, (((1,), (0,)), ((), ())), preferred_element_type=f32)


def dot_t(a, b):
    return lax.dot_general(a, b, (((1,), (1,)), ((), ())), preferred_element_type=f32)


def t_dot(a, b):
    return lax.dot_general(a, b, (((0,), (0,)), ((), ())), preferred_element_type=f32)


def params(mebibytes=16):
    return pltpu.CompilerParams(vmem_limit_bytes=mebibytes * 1024 * 1024)


def whole_spec(shape):
    return pl.BlockSpec(shape, lambda *_: (0,) * len(shape))


def rows_spec(a, part, rows):
    index = part if a.shape[0] > rows else 0
    return pl.BlockSpec((rows, a.shape[1]), lambda *_: (index, 0))


in_vmem = pl.BlockSpec(memory_space=pltpu.VMEM)
in_smem = pl.BlockSpec(memory_space=pltpu.SMEM)
anywhere = pl.BlockSpec(memory_space=pl.ANY)


class Sender:
    def __init__(self, sems):
        self.sems, self.copies = sems, []

    def __call__(self, source, target):
        copy = pltpu.make_async_copy(source, target, self.sems.at[len(self.copies)])
        copy.start()
        self.copies.append(copy)

    def wait(self):
        for copy in self.copies:
            copy.wait()


def cost(flops, nbytes, trans=0):
    return pl.CostEstimate(flops=int(flops), bytes_accessed=int(nbytes), transcendentals=int(trans))


def to_core(a):
    return lax.ppermute(a, "head", core_pairs)


def to_chip(a):
    return lax.ppermute(a, "head", chip_pairs)


def swap_section(a):
    return lax.ppermute(a, "section", [(0, 1), (1, 0)])


def after(a, *tokens):
    return lax.optimization_barrier((a, tokens))[0]


def plus(a, b):
    return jax.tree.map(lambda one, two: (one.astype(f32) + two.astype(f32)).astype(one.dtype), a, b)


def gather_slots(own):
    from_chip = to_chip(own)
    from_core = to_core(own)
    return [own, from_core, from_chip, to_core(from_chip)]


def scatter_slots(parts):
    far = plus(parts[2], to_core(parts[3]))
    return (parts[0], to_core(parts[1]), to_chip(far)), far


def scatter_halves(parts, token=None):
    from_core_far = to_core(parts[3])
    from_core = to_core(parts[1])
    rows = parts[0].shape[0] // 2
    terms = []
    for part in range(2):
        here = slice(part * rows, (part + 1) * rows)
        far = plus(parts[2][here], from_core_far[here])
        if token is not None:
            far = after(far, token)
        token = far
        terms.append((parts[0], from_core, to_chip(far)))
    return terms, token


def norm_rows(x, gain, shift):
    average = jnp.mean(x, axis=-1, keepdims=True)
    centred = x - average
    variance = jnp.mean(centred * centred, axis=-1, keepdims=True)
    return centred * lax.rsqrt(variance + norm_eps) * gain + shift


def norm_kernel(x_ref, gain_ref, shift_ref, out_ref):
    out_ref[...] = norm_rows(x_ref[...].astype(f32), gain_ref[...], shift_ref[...]).astype(bf16)


def norm_only(x, gain, shift):
    return pl.pallas_call(
        norm_kernel,
        out_shape=jax.ShapeDtypeStruct(x.shape, bf16),
        compiler_params=params(),
        cost_estimate=cost(x.size * 8, x.size * 4),
        name="norm_only",
    )(x, gain, shift)


def add_norm_kernel(x_ref, a_ref, b_ref, c_ref, add_ref, gain_ref, shift_ref, sum_ref, out_ref):
    total = x_ref[...].astype(f32) + (a_ref[...].astype(f32) + b_ref[...].astype(f32) + c_ref[...].astype(f32))
    total = (total + add_ref[...]).astype(sum_ref.dtype)
    sum_ref[...] = total
    out_ref[...] = norm_rows(total.astype(f32), gain_ref[...], shift_ref[...]).astype(bf16)


def add_norm(x, terms, part, add, gain, shift, sum_type):
    rows, width = terms[2].shape
    return pl.pallas_call(
        add_norm_kernel,
        grid=(1,),
        in_specs=[rows_spec(a, part, rows) for a in (x, *terms)] + [whole_spec(add.shape)] * 3,
        out_specs=[whole_spec((rows, width))] * 2,
        out_shape=(jax.ShapeDtypeStruct((rows, width), sum_type), jax.ShapeDtypeStruct((rows, width), bf16)),
        compiler_params=params(),
        cost_estimate=cost(rows * width * 12, rows * width * 14),
        name="add_norm",
    )(x, *terms, add, gain, shift)


def norm_back_kernel(x_ref, a_ref, b_ref, c_ref, gain_ref, more_ref, dx_ref, low_ref, small_ref):
    x = x_ref[...].astype(f32)
    grad = a_ref[...].astype(f32) + b_ref[...].astype(f32) + c_ref[...].astype(f32)
    average = jnp.mean(x, axis=-1, keepdims=True)
    centred = x - average
    variance = jnp.mean(centred * centred, axis=-1, keepdims=True)
    scale = lax.rsqrt(variance + norm_eps)
    unit = centred * scale
    wide = grad * gain_ref[...]
    mean_wide = jnp.mean(wide, axis=-1, keepdims=True)
    mean_unit = jnp.mean(wide * unit, axis=-1, keepdims=True)
    more = more_ref[...].astype(f32)
    dx = more + scale * (wide - mean_wide - unit * mean_unit)
    dx_ref[...] = dx
    low_ref[...] = dx.astype(bf16)
    small_ref[0:1, :] = jnp.sum(grad * unit, axis=0, keepdims=True)
    small_ref[1:2, :] = jnp.sum(grad, axis=0, keepdims=True)
    small_ref[2:3, :] = jnp.sum(more, axis=0, keepdims=True)
    small_ref[3:8, :] = jnp.zeros((5, x.shape[1]), f32)


def norm_back(x, terms, part, gain, more):
    rows, width = terms[2].shape
    return pl.pallas_call(
        norm_back_kernel,
        grid=(1,),
        in_specs=[rows_spec(a, part, rows) for a in (x, *terms)] + [whole_spec(gain.shape), rows_spec(more, part, rows)],
        out_specs=[whole_spec((rows, width))] * 2 + [whole_spec((8, width))],
        out_shape=(
            jax.ShapeDtypeStruct((rows, width), f32),
            jax.ShapeDtypeStruct((rows, width), bf16),
            jax.ShapeDtypeStruct((8, width), f32),
        ),
        compiler_params=params(),
        cost_estimate=cost(rows * width * 20, rows * width * 20),
        name="norm_back",
    )(x, *terms, gain, more)


def norm_back_small_kernel(x_ref, a_ref, b_ref, c_ref, small_ref):
    x = x_ref[...].astype(f32)
    grad = a_ref[...].astype(f32) + b_ref[...].astype(f32) + c_ref[...].astype(f32)
    average = jnp.mean(x, axis=-1, keepdims=True)
    centred = x - average
    variance = jnp.mean(centred * centred, axis=-1, keepdims=True)
    unit = centred * lax.rsqrt(variance + norm_eps)
    small_ref[0:1, :] = jnp.sum(grad * unit, axis=0, keepdims=True)
    small_ref[1:2, :] = jnp.sum(grad, axis=0, keepdims=True)
    small_ref[2:8, :] = jnp.zeros((6, x.shape[1]), f32)


def norm_back_small(x, terms):
    return pl.pallas_call(
        norm_back_small_kernel,
        out_shape=jax.ShapeDtypeStruct((8, x.shape[1]), f32),
        compiler_params=params(),
        cost_estimate=cost(x.size * 10, x.size * 8),
        name="norm_back_small",
    )(x, *terms)


log2_e = 1.4426950408889634


def fill_experts(target, source, experts, width):
    for j in range(experts):
        target[j * lanes : j * lanes + width, :] = source[j * width : (j + 1) * width, :]
        target[j * lanes + width : (j + 1) * lanes, :] = jnp.zeros((lanes - width, target.shape[1]), bf16)


def fill_weights(w_s, wo_s, wv_ref, wk_ref, wo_ref, experts, width):
    fill_experts(w_s, wv_ref, experts, width)
    fill_experts(wo_s, wo_ref, experts, width)
    start = 0
    for place, rows in ((experts + 1, width), (experts + 2, width), (experts, 2 * out_lane)):
        w_s[place * lanes : place * lanes + rows, :] = wk_ref[start : start + rows, :]
        w_s[place * lanes + rows : (place + 1) * lanes, :] = jnp.zeros((lanes - rows, w_s.shape[1]), bf16)
        start += rows


def attn_fwd_kernel(experts, head_width, slot_count, me_ref, *refs):
    mem_refs, slot_refs, refs = refs[:4], refs[4 : 4 + slot_count], refs[4 + slot_count :]
    wv_ref, wk_ref, wo_ref, mask_ref = refs[:4]
    *out_refs, normed_out, q_out, k_out, v_out, ev_out, gate_out, att_out, mixed_out = refs[4:16]
    normed, q_s, k_s, v_s, ev_s, gate_s, att_s, mixed_s, w_s, wo_s, out_s, mask_s, sems = refs[16:]
    me = me_ref[0]
    block = out_s.shape[1]
    quarter = block // 4
    wide = experts * lanes
    send = Sender(sems)

    for slot, ref in enumerate(mem_refs):
        here = slice(slot * quarter, (slot + 1) * quarter)
        normed[here, :] = ref[...]
        mask_s[here, :] = mask_ref[pl.ds(pl.multiple_of((me ^ slot) * quarter, quarter), quarter), :]
    halves = slot_count // 4
    rows = block // halves
    for number, ref in enumerate(slot_refs):
        start = (me ^ (number // halves)) * block + block + number % halves * rows
        normed[pl.ds(pl.multiple_of(start, rows), rows), :] = ref[...]
    send(normed, normed_out)
    fill_weights(w_s, wo_s, wv_ref, wk_ref, wo_ref, experts, head_width)

    scale = head_width ** (-0.5) * log2_e
    for i in range(5):
        here = slice(i * block, (i + 1) * block)
        proj = dot_t(normed[here, :], w_s[...])
        gate = jax.nn.sigmoid(proj[:, wide : wide + lanes]) * (mask_ref[here, :] if i else mask_s[...])
        value = gate[:, 0:1] * proj[:, 0:lanes]
        for j in range(1, experts):
            value = value + gate[:, j : j + 1] * proj[:, j * lanes : (j + 1) * lanes]
        k_s[here, :] = proj[:, wide + lanes : wide + 2 * lanes].astype(bf16)
        v_s[here, :] = value.astype(bf16)
        ev_s[here, :] = proj[:, :wide].astype(bf16)
        q_s[here, :] = (proj[:, wide + 2 * lanes :] * scale).astype(bf16)
        gate_s[here, :] = gate
    send(ev_s, ev_out)
    send(q_s, q_out)
    send(k_s, k_out)
    send(v_s, v_out)

    row = lax.broadcasted_iota(jnp.int32, (block, block), 0)
    col = lax.broadcasted_iota(jnp.int32, (block, block), 1)
    lane = lax.broadcasted_iota(jnp.int32, (block, lanes), 1)
    for i in range(1, 5):
        here, before = slice(i * block, (i + 1) * block), slice(0, i * block)
        own = slice((i - 1) * block, i * block)
        queries = q_s[here, :]
        early = dot_t(queries, k_s[before, :])
        late = jnp.where(col <= row, dot_t(queries, k_s[here, :]), masked_score)
        top = jnp.maximum(jnp.max(early, axis=-1, keepdims=True), jnp.max(late, axis=-1, keepdims=True))
        early = jnp.exp2(early - top)
        late = jnp.exp2(late - top)
        total = jnp.sum(early, axis=-1, keepdims=True) + jnp.sum(late, axis=-1, keepdims=True)
        attended = dot(early.astype(bf16), v_s[before, :]) + dot(late.astype(bf16), v_s[here, :])
        attended = attended * (1.0 / total)
        att_s[own, :] = attended
        gate = gate_s[here, :]
        gate_s[here, :] = jnp.where(lane == log_lane, top + jnp.log2(total), gate)
        for j in range(experts):
            opened = gate[:, out_lane + j : out_lane + j + 1] * attended
            mixed_s[own, j * lanes : (j + 1) * lanes] = opened.astype(bf16)
    send(gate_s, gate_out)
    send(att_s, att_out)
    send(mixed_s, mixed_out)
    for slot in (3, 2, 1, 0):
        start = pl.multiple_of((me ^ slot) * block, block)
        out_s[slot] = dot(mixed_s[pl.ds(start, block), :], wo_s[...]).astype(bf16)
        send(out_s.at[slot], out_refs[slot])
    send.wait()


def attn_fwd(me, mems, slots, w, mask, experts, head_width):
    width = mems[0].shape[1]
    block = 4 * mems[0].shape[0]
    total = 5 * block
    wide = experts * lanes
    shape = lambda rows, cols, kind: jax.ShapeDtypeStruct((rows, cols), kind)
    kept = [
        shape(total, width, bf16),
        *[shape(total, lanes, bf16)] * 3,
        shape(total, wide, bf16),
        shape(total, lanes, f32),
        shape(4 * block, lanes, f32),
        shape(4 * block, wide, bf16),
    ]
    outs = [shape(block, width, bf16)] * 4 + kept
    operands = (*mems, *slots, *w, mask)
    return pl.pallas_call(
        functools.partial(attn_fwd_kernel, experts, head_width, len(slots)),
        in_specs=[in_smem] + [in_vmem] * len(operands),
        out_specs=[anywhere] * len(outs),
        out_shape=outs,
        scratch_shapes=[pltpu.VMEM(a.shape, a.dtype) for a in kept]
        + [
            pltpu.VMEM((wide + 3 * lanes, width), bf16),
            pltpu.VMEM((wide, width), bf16),
            pltpu.VMEM((4, block, width), bf16),
            pltpu.VMEM((block, lanes), f32),
            pltpu.SemaphoreType.DMA((12,)),
        ],
        compiler_params=params(30),
        cost_estimate=cost(4 * total * width * wide, 16 * 1024 * 1024, total * total),
        name="attn_fwd",
    )(me, *operands)


def attn_bwd_kernel(experts, head_width, slot_count, me_ref, *refs):
    slot_refs, refs = refs[:slot_count], refs[slot_count:]
    wv_ref, wk_ref, wo_ref, q_ref, k_ref, v_ref, ev_ref, gate_ref, att_ref = refs[:9]
    *grad_outs, mem_out, dproj_out, rows_out = refs[9:16]
    w_s, wo_s, rows_s, dproj_s, grad_s, mem_s, dk_s, dv_s, sems = refs[16:]
    me = me_ref[0]
    block = mem_s.shape[0]
    wide = experts * lanes
    scale = head_width ** (-0.5)
    send = Sender(sems)

    halves = slot_count // 4
    rows = block // halves
    for number, ref in enumerate(slot_refs):
        start = (me ^ (number // halves)) * block + number % halves * rows
        rows_s[pl.ds(pl.multiple_of(start, rows), rows), :] = ref[...]
    send(rows_s, rows_out)
    fill_weights(w_s, wo_s, wv_ref, wk_ref, wo_ref, experts, head_width)

    row = lax.broadcasted_iota(jnp.int32, (block, block), 0)
    col = lax.broadcasted_iota(jnp.int32, (block, block), 1)
    lane = lax.broadcasted_iota(jnp.int32, (block, lanes), 1)
    for i in range(4, -1, -1):
        here = slice(i * block, (i + 1) * block)
        gate = gate_ref[here, :]
        logit_grad = jnp.zeros((block, lanes), f32)
        if i > 0:
            own = slice((i - 1) * block, i * block)
            mixed_grad = dot_t(rows_s[own, :], wo_s[...])
            attended = att_ref[own, :]
            att_grad = jnp.zeros((block, lanes), f32)
            for j in range(experts):
                part = mixed_grad[:, j * lanes : (j + 1) * lanes]
                att_grad = att_grad + gate[:, out_lane + j : out_lane + j + 1] * part
                inner = jnp.sum(part * attended, axis=-1, keepdims=True)
                logit_grad = jnp.where(lane == out_lane + j, inner, logit_grad)
            grad_low = att_grad.astype(bf16)
            row_sum = jnp.sum(att_grad * attended, axis=-1, keepdims=True)
            log_total = gate[:, log_lane : log_lane + 1]
            queries = q_ref[here, :]
            query_grad = jnp.zeros((block, lanes), f32)
            for span in (slice(0, i * block), here):
                keys = k_ref[span, :]
                scores = dot_t(queries, keys)
                if span is here:
                    scores = jnp.where(col <= row, scores, masked_score)
                probs = jnp.exp2(scores - log_total)
                score_grad = (probs * (dot_t(grad_low, v_ref[span, :]) - row_sum)).astype(bf16)
                query_grad = query_grad + dot(score_grad, keys)
                key_part = t_dot(score_grad, queries)
                value_part = t_dot(probs.astype(bf16), grad_low)
                if i == 4:
                    dk_s[span, :] = key_part
                    dv_s[span, :] = value_part
                else:
                    dk_s[span, :] += key_part
                    dv_s[span, :] += value_part
            dproj_s[here, wide + 2 * lanes :] = (query_grad * scale).astype(bf16)
        else:
            dproj_s[here, wide + 2 * lanes :] = jnp.zeros((block, lanes), bf16)
        value_grad = dv_s[here, :].astype(bf16).astype(f32)
        for j in range(experts):
            cols = slice(j * lanes, (j + 1) * lanes)
            dproj_s[here, cols] = (gate[:, j : j + 1] * value_grad).astype(bf16)
            inner = jnp.sum(value_grad * ev_ref[here, cols].astype(f32), axis=-1, keepdims=True)
            logit_grad = jnp.where(lane == j, inner, logit_grad)
        slope = jnp.where(lane < log_lane, gate * (1.0 - gate), 0.0)
        dproj_s[here, wide : wide + lanes] = (logit_grad * slope).astype(bf16)
        dproj_s[here, wide + lanes : wide + 2 * lanes] = (dk_s[here, :] * (1.0 / log2_e)).astype(bf16)
        normed_grad = dot(dproj_s[here, :], w_s[...]).astype(bf16)
        if i > 0:
            grad_s[pl.ds((i - 1) ^ me, 1)] = normed_grad[None]
        else:
            mem_s[...] = normed_grad
    for slot in (3, 2, 1, 0):
        send(grad_s.at[slot], grad_outs[slot])
    send(dproj_s, dproj_out)
    send(mem_s, mem_out)
    send.wait()


def attn_bwd(me, slots, w, saved, experts, head_width):
    width = slots[0].shape[1]
    block = sum(a.shape[0] for a in slots) // 4
    total = 5 * block
    wide = experts * lanes
    shape = lambda rows, cols: jax.ShapeDtypeStruct((rows, cols), bf16)
    outs = [shape(block, width)] * 5 + [shape(total, wide + 3 * lanes), shape(4 * block, width)]
    operands = (*slots, *w, *saved)
    return pl.pallas_call(
        functools.partial(attn_bwd_kernel, experts, head_width, len(slots)),
        in_specs=[in_smem] + [in_vmem] * len(operands),
        out_specs=[anywhere] * len(outs),
        out_shape=outs,
        scratch_shapes=[
            pltpu.VMEM((wide + 3 * lanes, width), bf16),
            pltpu.VMEM((wide, width), bf16),
            pltpu.VMEM((4 * block, width), bf16),
            pltpu.VMEM((total, wide + 3 * lanes), bf16),
            pltpu.VMEM((4, block, width), bf16),
            pltpu.VMEM((block, width), bf16),
            pltpu.VMEM((total, lanes), f32),
            pltpu.VMEM((total, lanes), f32),
            pltpu.SemaphoreType.DMA((7,)),
        ],
        compiler_params=params(32),
        cost_estimate=cost(4 * total * width * wide, 16 * 1024 * 1024, total * total),
        name="attn_bwd",
    )(me, *operands)


def gelu_parts(u):
    square = u * u
    t = jnp.tanh(gelu_c * u * (1.0 + gelu_a * square))
    slope = 0.5 * (1.0 + t) + 0.5 * gelu_c * u * (1.0 - t * t) * (1.0 + 3.0 * gelu_a * square)
    return 0.5 * u * (1.0 + t), slope


def load_pieces(target, refs, part):
    rows = target.shape[0] // len(refs)
    for number, ref in enumerate(refs):
        start = part * rows if ref.shape[0] > rows else 0
        target[number * rows : (number + 1) * rows, :] = ref[start : start + rows, :]


def send_rows(send, source, outs, span):
    rows = source.shape[0] // len(outs)
    for number in range(len(outs) - 1, -1, -1):
        if span.start <= number * rows < span.stop:
            send(source.at[pl.ds(number * rows, rows)], outs[number])


def two_spans(rows):
    return slice(0, rows // 2), slice(rows // 2, rows)


def ffn_fwd_kernel(part, *refs):
    pieces, (wu_ref, bu_ref, wd_ref) = refs[:4], refs[4:7]
    *outs, rows_out, upper_out, active_out = refs[-12:-5]
    rows_s, upper_s, active_s, out_s, sems = refs[-5:]
    send = Sender(sems)
    total = rows_s.shape[0]
    here = pl.ds(part * total, total)
    load_pieces(rows_s, pieces, part)
    send(rows_s, rows_out.at[here])
    for span in two_spans(total):
        upper = dot(rows_s[span, :], wu_ref[...]) + bu_ref[...]
        upper_s[span, :] = upper.astype(bf16)
        active_s[span, :] = jax.nn.gelu(upper).astype(bf16)
    send(upper_s, upper_out.at[here])
    send(active_s, active_out.at[here])
    for span in two_spans(total)[::-1]:
        out_s[span, :] = dot(active_s[span, :], wd_ref[...]).astype(bf16)
        send_rows(send, out_s, outs, span)
    send.wait()


def ffn_fwd(pieces, part, wu, bu, wd, earlier):
    rows, width = pieces[0].shape
    hidden = wu.shape[1]
    total = 4 * rows
    shape = lambda *dims: jax.ShapeDtypeStruct(dims, bf16)
    operands = (*pieces, wu, bu, wd)
    outs = [shape(rows, width)] * 4 + [shape(2 * total, width), shape(2 * total, hidden), shape(2 * total, hidden)]
    return pl.pallas_call(
        functools.partial(ffn_fwd_kernel, part),
        in_specs=[in_vmem] * len(operands) + [anywhere] * len(earlier),
        out_specs=[anywhere] * len(outs),
        out_shape=outs,
        input_output_aliases={len(operands) + i: 4 + i for i in range(len(earlier))},
        scratch_shapes=[
            pltpu.VMEM((total, width), bf16),
            pltpu.VMEM((total, hidden), bf16),
            pltpu.VMEM((total, hidden), bf16),
            pltpu.VMEM((total, width), bf16),
            pltpu.SemaphoreType.DMA((7,)),
        ],
        compiler_params=params(24),
        cost_estimate=cost(4 * total * width * hidden, 9 * 1024 * 1024, total * hidden),
        name="ffn_fwd",
    )(*operands, *earlier)


def ffn_bwd_kernel(part, forward, *refs):
    pieces, refs = refs[:4], refs[4:]
    if forward:
        normed_refs, (bu_ref, wd_ref, wu_ref), refs = refs[:4], refs[4:7], refs[7:]
        *outs, bias_out, rows_out, grad_out, normed_out, active_out = refs[-15:-6]
    else:
        (upper_ref, wd_ref, wu_ref), refs = refs[:3], refs[3:]
        *outs, bias_out, rows_out, grad_out = refs[-13:-6]
    rows_s, grad_s, out_s, normed_s, active_s, sems = refs[-6:]
    send = Sender(sems)
    total = rows_s.shape[0]
    here = pl.ds(part * total, total)
    load_pieces(rows_s, pieces, part)
    send(rows_s, rows_out.at[here])
    if forward:
        load_pieces(normed_s, normed_refs, part)
        send(normed_s, normed_out.at[here])
    sums = jnp.zeros((1, grad_s.shape[1]), f32)
    for span in two_spans(total):
        if forward:
            upper = dot(normed_s[span, :], wu_ref[...]) + bu_ref[...]
        else:
            upper = upper_ref[span, :].astype(f32)
        active_grad = dot_t(rows_s[span, :], wd_ref[...])
        active, slope = gelu_parts(upper)
        if forward:
            active_s[span, :] = active.astype(bf16)
        upper_grad = (active_grad * slope).astype(bf16)
        grad_s[span, :] = upper_grad
        sums = sums + jnp.sum(upper_grad.astype(f32), axis=0, keepdims=True)
    bias_out[...] = sums
    send(grad_s, grad_out.at[here])
    if forward:
        send(active_s, active_out.at[here])
    for span in two_spans(total)[::-1]:
        out_s[span, :] = dot_t(grad_s[span, :], wu_ref[...]).astype(bf16)
        send_rows(send, out_s, outs, span)
    send.wait()


def ffn_bwd(pieces, part, wd, wu, earlier, upper=None, normed=None, bu=None):
    forward = normed is not None
    width, hidden = wu.shape
    rows = min(a.shape[0] for a in (normed if forward else pieces))
    total = 4 * rows
    shape = lambda *dims: jax.ShapeDtypeStruct(dims, bf16)
    kept = [shape(2 * total, width), shape(2 * total, hidden)]
    outs = [shape(rows, width)] * 4 + [jax.ShapeDtypeStruct((1, hidden), f32)] + kept + (kept if forward else [])
    operands = (*pieces, *normed, bu, wd, wu) if forward else (*pieces, upper, wd, wu)
    specs = [whole_spec(a.shape) for a in operands]
    if not forward:
        specs[4] = rows_spec(upper, part, total)
    spare = (total, width) if forward else (8, lanes)
    return pl.pallas_call(
        functools.partial(ffn_bwd_kernel, part, forward),
        grid=(1,),
        in_specs=specs + [anywhere] * len(earlier),
        out_specs=[anywhere] * 4 + [whole_spec((1, hidden))] + [anywhere] * (len(outs) - 5),
        out_shape=outs,
        input_output_aliases={len(operands) + i: 5 + i for i in range(len(earlier))},
        scratch_shapes=[
            pltpu.VMEM((total, width), bf16),
            pltpu.VMEM((total, hidden), bf16),
            pltpu.VMEM((total, width), bf16),
            pltpu.VMEM(spare, bf16),
            pltpu.VMEM(spare, bf16),
            pltpu.SemaphoreType.DMA((8,)),
        ],
        compiler_params=params(36),
        cost_estimate=cost(4 * total * width * hidden, 9 * 1024 * 1024, total * hidden),
        name="ffn_bwd",
    )(*operands, *earlier)


def attn_grads_kernel(experts, head_width, *refs):
    sources, (out_ref, dproj_s, normed_s, mixed_s, rows_s, grad_s, loads, sems) = refs[:4], refs[4:]
    send = Sender(sems)
    fetch = Sender(loads)
    for source, target in zip(sources, (dproj_s, normed_s, mixed_s, rows_s)):
        fetch(source, target)

    def fill(start, left, right, counts):
        for pair in range(0, len(counts), 2):
            here = counts[pair : pair + 2]
            wide = t_dot(left[:, pair * lanes : (pair + len(here)) * lanes], right[...]).astype(bf16)
            for number, count in enumerate(here):
                grad_s[start : start + count, :] = wide[number * lanes : number * lanes + count]
                start += count
        return start

    fetch.copies[0].wait()
    fetch.copies[1].wait()
    pack = fill(0, dproj_s, normed_s, [head_width] * experts + [2 * out_lane] + [head_width] * 2)
    send(grad_s.at[pl.ds(0, pack)], out_ref.at[pl.ds(0, pack)])
    fetch.copies[2].wait()
    fetch.copies[3].wait()
    total = fill(pack, mixed_s, rows_s, [head_width] * experts)
    send(grad_s.at[pl.ds(pack, total - pack)], out_ref.at[pl.ds(pack, total - pack)])
    send.wait()


def attn_grads(dproj, normed, mixed, rows, experts, head_width):
    count = (2 * experts + 2) * head_width + 2 * out_lane
    width = normed.shape[1]
    operands = (dproj, normed, mixed, rows)
    return pl.pallas_call(
        functools.partial(attn_grads_kernel, experts, head_width),
        in_specs=[anywhere] * len(operands),
        out_specs=anywhere,
        out_shape=jax.ShapeDtypeStruct((count, width), bf16),
        scratch_shapes=[pltpu.VMEM(a.shape, a.dtype) for a in operands]
        + [pltpu.VMEM((count, width), bf16), pltpu.SemaphoreType.DMA((4,)), pltpu.SemaphoreType.DMA((2,))],
        compiler_params=params(28),
        cost_estimate=cost(0, 0),
        name="attn_grads",
    )(*operands)


class DpSums:
    def __init__(self):
        self.chunks = {}
        self.token = ()
        self.direct = lax.axis_size("dp") != 4
        place = lax.axis_index("dp")
        self.middle = (place == 1) | (place == 2)

    def add(self, name, own, got):
        self.chunks[name] = dict(own=own, moving=got, step=0)

    def turns(self, *names):
        for name in names:
            self.turn(self.chunks[name])

    def turn(self, chunk):
        step = chunk["step"]
        chunk["step"] += 1
        if self.direct:
            if step == 0:
                chunk["end"] = lax.psum(plus(chunk["own"], chunk["moving"]), "dp")
            return
        got = after(chunk["moving"], self.token)
        if step == 3:
            chunk["end"] = jax.tree.map(lambda full, far: jnp.where(self.middle, full, far), chunk["own"], got)
            return
        total = plus(chunk["own"], got)
        pairs = ([(0, 1), (3, 2)], [(1, 2), (2, 1)], [(1, 0), (2, 3)])[step]
        chunk["own"] = self.token = total
        chunk["moving"] = jax.tree.map(lambda a: lax.ppermute(a, "dp", pairs), total)


def split_tiles(rows, pieces):
    size = rows // 16 // pieces * 16
    return [rows - size * (pieces - 1)] + [size] * (pieces - 1)


def cut(a, pieces):
    rows = a.shape[0] // pieces
    return [a[i * rows : (i + 1) * rows] for i in range(pieces)]


def padded_rows(a, rows):
    return jnp.pad(a, ((0, rows - a.shape[0]), (0, 0)))


def swap_weights(weights, start_after):
    size = lax.axis_size("dp")
    odd = lax.axis_index("dp") % 2
    results = []
    gots = []
    for a, pieces in weights:
        parts = []
        for part in cut(a, pieces):
            part = after(part, start_after, *gots[: max(0, len(gots) - 1)])
            if size % 2:
                gots.append(swap_section(part))
                parts.append(gots[-1])
                continue
            rows = part.shape[0] // 2
            gots.append(swap_section(lax.dynamic_slice_in_dim(part, odd * rows, rows, 0)))
            got = gots[-1]
            other = lax.ppermute(got, "dp", [(i, i ^ 1) for i in range(size)])
            parts += [jnp.where(odd == 0, got, other), jnp.where(odd == 0, other, got)]
        results.append(jnp.concatenate(parts, axis=0))
    return results


def route_mask(value_ids, out_ids, experts, memory_len):
    lane = jnp.arange(lanes, dtype=jnp.int32)[None, :]
    out_full = jnp.pad(out_ids, ((0, 0), (memory_len, 0)), constant_values=-1)
    hit = jnp.zeros((value_ids.shape[1], lanes), jnp.bool_)
    for k in range(value_ids.shape[0]):
        hit = hit | (lane == value_ids[k][:, None])
        hit = hit | ((lane == out_full[k][:, None] + out_lane) & (out_full[k][:, None] >= 0))
    return hit.astype(f32)


def on_device(
    inputs,
    memory,
    value_routes,
    out_routes,
    ln1_gain,
    ln1_bias,
    query_weight,
    key_weight,
    value_weight,
    value_router,
    out_router,
    output_weight,
    ln2_gain,
    ln2_bias,
    up_weight,
    up_bias,
    down_weight,
    down_bias,
    out_cot,
):
    experts = value_router.shape[-1]
    head_width = query_weight.shape[-1]
    sec = lax.axis_index("section")
    head = lax.axis_index("head")
    me = head.astype(jnp.int32).reshape(1)
    first = sec == 0
    pick = lambda a, index: lax.dynamic_index_in_dim(a, index, 0, keepdims=False)
    memory_len = memory.shape[2] * lax.axis_size("head")

    value_rows = experts * head_width
    router_rows = [padded_rows(a[0, 0].T, out_lane) for a in (value_router, out_router)]
    kqr = jnp.concatenate([key_weight[0, 0].T, query_weight[0, 0].T, *router_rows])
    weights = [value_weight[0, 0].T, kqr, output_weight[0, 0], up_weight[0], down_weight[0]]

    small = jnp.concatenate([ln1_gain, ln1_bias, ln2_gain, ln2_bias, up_bias, down_bias, ln1_gain, ln1_bias], axis=0)
    route_rows = jnp.concatenate(
        [
            jnp.transpose(value_routes[0, :, :, 0, :], (0, 2, 1)),
            jnp.pad(jnp.transpose(out_routes[0, :, :, 0, :], (0, 2, 1)), ((0, 0), (0, 0), (memory_len, 0)), constant_values=-1),
        ],
        axis=1,
    )
    sends = [small, pick(memory[0], 1 - sec), pick(route_rows, 1 - sec)]
    small_got, memory_got, routes_got = [swap_section(a) for a in sends]

    def both_layers(own, got):
        return jnp.where(first, own, got), jnp.where(first, got, own)

    smalls = both_layers(small, small_got)
    route_sets = both_layers(pick(route_rows, sec), routes_got)
    memories = both_layers(pick(memory[0], sec), memory_got)
    weights_got = swap_weights(list(zip(weights, (1, 1, 1, 1, 1))), sends)
    weight_sets = [both_layers(a, got) for a, got in zip(weights, weights_got)]

    x = pick(inputs, sec)
    cot = pick(out_cot, sec)
    own_norm = norm_only(x, smalls[0][0:1], smalls[0][1:2])
    slots = gather_slots(own_norm)
    route_sets = after(route_sets, own_norm)
    topk = value_routes.shape[-1]

    layers = []
    for number in range(2):
        vec = smalls[number]
        routes = route_sets[number]
        layers.append(
            dict(
                gain1=vec[0:1],
                shift1=vec[1:2],
                gain2=vec[2:3],
                shift2=vec[3:4],
                up_b=vec[4:5],
                down_b=vec[5:6],
                w=(weight_sets[0][number], weight_sets[1][number], weight_sets[2][number]),
                wu=weight_sets[3][number],
                wd=weight_sets[4][number],
                mask=route_mask(routes[:topk], routes[topk:, memory_len:], experts, memory_len),
                mem=memories[number],
            )
        )
    one, two = layers
    no_add = jnp.zeros_like(one["gain1"])
    for layer in layers:
        layer["mem_slots"] = gather_slots(norm_only(after(layer["mem"], own_norm), layer["gain1"], layer["shift1"]))
    cot_slots = gather_slots(after(cot, slots[2], one["mem_slots"][2]))
    slots[3] = after(slots[3], one["mask"], two["mask"])

    def attention(layer, rows_in, slots):
        *out, layer["normed"], q, k, v, ev, gate, att, layer["mixed"] = attn_fwd(
            me, layer["mem_slots"], slots, layer["w"], layer["mask"], experts, head_width
        )
        layer["saved"] = (q, k, v, ev, gate, att)
        if layer is one:
            out[3] = after(out[3], cot_slots[2], two["mem_slots"][2])
        terms, _ = scatter_halves(out)
        layer["hidden"], slots = [], []
        for part in range(2):
            hidden, normed = add_norm(rows_in[part], terms[part], part, no_add, layer["gain2"], layer["shift2"], f32)
            layer["hidden"].append(hidden)
            slots.append(gather_slots(normed))
        return slots

    one["rows"] = [x, x]
    halves = attention(one, one["rows"], slots)
    kept = ()
    two["rows"], slots = [], []
    for part in range(2):
        *out, n2, upper, active = ffn_fwd(halves[part], part, one["wu"], one["up_b"], one["wd"], kept)
        kept = (n2, upper, active)
        terms, _ = scatter_slots(out)
        rows, normed = add_norm(one["hidden"][part], terms, part, one["down_b"], two["gain1"], two["shift1"], bf16)
        two["rows"].append(rows)
        slots.append(gather_slots(normed))
    one["n2"], one["upper"], one["active"] = kept
    slots = [half[slot] for slot in range(4) for half in slots]
    halves = attention(two, two["rows"], slots)

    def by_layer(one, two):
        got = swap_section(jnp.where(first, two, one))
        kept = jnp.where(first, one, two)
        return jnp.stack([jnp.where(first, kept, got), jnp.where(first, got, kept)])[None]

    def send_chunks(one, two, names, sizes):
        start = 0
        for name, size in zip(names, sizes):
            part_one, part_two = one[start : start + size], two[start : start + size]
            start += size
            send = jnp.where(first, part_two, part_one)
            if sums.chunks:
                send = after(send, list(sums.chunks.values())[-1]["moving"])
            sums.add(name, jnp.where(first, part_one, part_two), swap_section(send))

    sums = DpSums()
    grads = [{}, {}]
    smalls_out, mem_grads = [None, None], [None, None]
    input_grads = [None, None]
    for number in (1, 0):
        layer, grad = layers[number], grads[number]
        wu, wd = layer["wu"], layer["wd"]
        if number == 1:
            g_rows = [cot, cot]
        kept = ()
        terms, bias = [], []
        for part in range(2):
            if number == 1:
                *out, sums_here, g_all, upper_grad, n2, active = ffn_bwd(
                    cot_slots, part, wd, wu, kept, normed=halves[part], bu=layer["up_b"]
                )
                kept = (g_all, upper_grad, n2, active)
            else:
                *out, sums_here, g_all, upper_grad = ffn_bwd(halves[part], part, wd, wu, kept, upper=layer["upper"])
                kept = (g_all, upper_grad)
                n2, active = layer["n2"], layer["active"]
            bias.append(sums_here)
            terms_here, token = scatter_slots(out)
            terms.append(terms_here)
        grad["down"] = t_dot(active, after(g_all, token)).astype(bf16)
        grad["up"] = t_dot(after(n2, grad["down"]), upper_grad).astype(bf16)
        if number == 0:
            halved = [wd.shape[0] // 2] * 2
            send_chunks(grad["down"], grads[1]["down"], ("down0", "down1"), halved)
            send_chunks(grad["up"], grads[1]["up"], ("up0", "up1"), halved)
        terms[1] = (*terms[1][0:2], after(terms[1][2], grad["up"]))
        hidden_grads, a_halves, small2 = [], [], []
        for part in range(2):
            dx, low, small_here = norm_back(layer["hidden"][part], terms[part], part, layer["gain2"], g_rows[part])
            hidden_grads.append(dx)
            small2.append(small_here)
            a_halves.append(gather_slots(low))
        a_slots = [half[slot] for slot in range(4) for half in a_halves]
        if number == 0:
            sums.turns("down0")
            a_slots[7] = after(a_slots[7], sums.token)
        else:
            down_out = dot(active, after(wd, a_halves[1][0])).astype(bf16)
            rows = down_out.shape[0] // 8
            last_parts = [
                jnp.concatenate([down_out[s * rows : (s + 1) * rows], down_out[(4 + s) * rows : (5 + s) * rows]])
                for s in range(4)
            ]
            last_terms, _ = scatter_halves(last_parts, a_halves[1][2])
        *ngs, ngm, dproj, a_all = attn_bwd(me, a_slots, layer["w"], layer["saved"], experts, head_width)
        if number == 1:
            ngs[3] = after(ngs[3], [here[2] for here in last_terms])
            near, from_core, _ = last_terms[0]
            last_out = jnp.concatenate(layer["hidden"]) + layer["down_b"] + near.astype(f32) + from_core.astype(f32)
            last_out = (last_out + jnp.concatenate([here[2] for here in last_terms]).astype(f32)).astype(bf16)
            layer_out = by_layer(jnp.concatenate(layer["rows"]), last_out)
        terms, token = scatter_halves(ngs)
        grad["attn"] = attn_grads(after(dproj, token), layer["normed"], layer["mixed"], a_all, experts, head_width)
        token = grad["attn"]
        if number == 0:
            sizes = split_tiles(token.shape[0], 4)
            send_chunks(token, grads[1]["attn"], ("attn0", "attn1", "attn2", "attn3"), sizes)
            sums.token = token
            sums.turns("down0", "down1")
            token = sums.token
        terms[1] = (*terms[1][0:2], after(terms[1][2], token))
        rows_grads, low_grads, small1, halves = [], [], [], []
        for part in range(2):
            dx, low, small_here = norm_back(layer["rows"][part], terms[part], part, layer["gain1"], hidden_grads[part])
            rows_grads.append(dx)
            low_grads.append(low)
            small1.append(small_here)
            if number == 1:
                halves.append(gather_slots(low))
        g_rows = rows_grads if number == 0 else low_grads
        mem_grads[number] = cut(ngm, 4)
        input_grads[number] = jnp.concatenate(low_grads)
        smalls_out[number] = (small1[0] + small1[1], small2[0] + small2[1], bias[0] + bias[1])

    mem_terms, _ = scatter_slots([jnp.concatenate(pair) for pair in zip(*mem_grads)])
    rows = memories[0].shape[0]
    vecs = []
    for number, (small1, small2, bias) in enumerate(smalls_out):
        here = slice(number * rows, (number + 1) * rows)
        small_mem = norm_back_small(layers[number]["mem"], [a[here] for a in mem_terms])
        vecs.append(jnp.concatenate([(small1 + small_mem)[0:2], small2[0:6]]))
    vec = jnp.concatenate(vecs)
    vec = vec + to_core(vec)
    vec = vec + to_chip(vec)
    vecs = [jnp.concatenate([part[0:5], bias, part[6:8]]) for part, (_, _, bias) in zip(cut(vec, 2), smalls_out)]
    last_chunk = sums.chunks["attn3"]
    last_chunk["own"] = (last_chunk["own"], jnp.where(first, vecs[0], vecs[1]))
    last_chunk["moving"] = (last_chunk["moving"], swap_section(jnp.where(first, vecs[1], vecs[0])))
    sums.turns("down0", "down1", "up0", "down0", "down1", "up0", "up1", "down1", "attn0", "up0", "up1", "attn0", "attn1")
    sums.turns("up0", "up1", "attn1", "attn2", "attn0", "up1", "attn2", "attn1", "attn3")
    last_sum = sums.token
    sums.turns("attn0", "attn2", "attn3", "attn1", "attn3", "attn2", "attn3")
    ends = {name: chunk["end"] for name, chunk in sums.chunks.items()}
    ends["attn3"], vec = ends["attn3"]
    input_grad = by_layer(*[after(a, last_sum) for a in input_grads])
    join = lambda *names: jnp.concatenate([ends[name] for name in names]).astype(f32)
    down_sum, up_sum = join("down0", "down1"), join("up0", "up1")
    attn_sum = join("attn0", "attn1", "attn2", "attn3")

    def take(start, count):
        return attn_sum[start : start + count]

    routers = value_rows + 2 * out_lane
    value_sum, vroute_sum, oroute_sum = take(0, value_rows), take(value_rows, experts), take(value_rows + out_lane, experts)
    key_sum, query_sum = take(routers, head_width), take(routers + head_width, head_width)
    out_sum = take(routers + 2 * head_width, value_rows)

    return (
        layer_out,
        input_grad,
        vec[0:1],
        vec[1:2],
        query_sum.T[None, None],
        key_sum.T[None, None],
        value_sum.T[None, None],
        vroute_sum.T[None, None],
        oroute_sum.T[None, None],
        out_sum[None, None],
        vec[2:3],
        vec[3:4],
        up_sum[None],
        vec[5:6],
        down_sum[None],
        vec[4:5],
    )


def solution(mesh):
    placed = (
        P("dp", "head", None),
        P("section", "dp", "head", None),
        P("section", "dp", None, "head", None),
        P("section", "dp", None, "head", None),
        P("section", None),
        P("section", None),
        P("section", "head", None, None),
        P("section", "head", None, None),
        P("section", "head", None, None),
        P("section", "head", None, None),
        P("section", "head", None, None),
        P("section", "head", None, None),
        P("section", None),
        P("section", None),
        P("section", None, "head"),
        P("section", "head"),
        P("section", "head", None),
        P("section", None),
        P("dp", "head", None),
    )
    return jax.shard_map(
        on_device,
        mesh=mesh,
        in_specs=placed,
        out_specs=(
            P("section", "dp", "head", None),
            P("section", "dp", "head", None),
            P("section", None),
            P("section", None),
            P("section", "head", None, None),
            P("section", "head", None, None),
            P("section", "head", None, None),
            P("section", "head", None, None),
            P("section", "head", None, None),
            P("section", "head", None, None),
            P("section", None),
            P("section", None),
            P("section", None, "head"),
            P("section", "head"),
            P("section", "head", None),
            P("section", None),
        ),
        check_vma=False,
    )
```

```python
import functools
from types import SimpleNamespace

import jax
import jax.numpy as jnp
from jax import lax
from jax.experimental import pallas as pl
from jax.experimental.pallas import tpu as pltpu
from jax.sharding import PartitionSpec as P

norm_eps = 1e-05
masked_score = -1e30
section_axis, head_axis, dp_axis = "section", "head", "dp"
lanes = 128
out_lane = 8
log_lane = 16
bf16 = jnp.bfloat16
f32 = jnp.float32
gelu_c = 0.7978845608028654
gelu_a = 0.044715

core_pairs = [(0, 1), (1, 0), (2, 3), (3, 2)]
chip_pairs = [(0, 2), (2, 0), (1, 3), (3, 1)]


def dot(a, b):
    return lax.dot_general(a, b, (((1,), (0,)), ((), ())), preferred_element_type=f32)


def dot_t(a, b):
    return lax.dot_general(a, b, (((1,), (1,)), ((), ())), preferred_element_type=f32)


def t_dot(a, b):
    return lax.dot_general(a, b, (((0,), (0,)), ((), ())), preferred_element_type=f32)


def params(mebibytes=16):
    return pltpu.CompilerParams(vmem_limit_bytes=mebibytes * 1024 * 1024)


def whole_spec(shape):
    return pl.BlockSpec(shape, lambda *_: (0,) * len(shape))


def rows_spec(a, part, rows):
    index = part if a.shape[0] > rows else 0
    return pl.BlockSpec((rows, a.shape[1]), lambda *_: (index, 0))


in_vmem = pl.BlockSpec(memory_space=pltpu.VMEM)
in_smem = pl.BlockSpec(memory_space=pltpu.SMEM)
anywhere = pl.BlockSpec(memory_space=pl.ANY)


class Sender:
    def __init__(self, sems):
        self.sems, self.copies = sems, []

    def __call__(self, source, target):
        copy = pltpu.make_async_copy(source, target, self.sems.at[len(self.copies)])
        copy.start()
        self.copies.append(copy)

    def wait(self):
        for copy in self.copies:
            copy.wait()


def cost(flops, nbytes, trans=0):
    return pl.CostEstimate(flops=int(flops), bytes_accessed=int(nbytes), transcendentals=int(trans))


def to_core(a):
    return lax.ppermute(a, head_axis, core_pairs)


def to_chip(a):
    return lax.ppermute(a, head_axis, chip_pairs)


def swap_section(a):
    return lax.ppermute(a, section_axis, [(0, 1), (1, 0)])


def after(a, *tokens):
    return lax.optimization_barrier((a, tokens))[0]


def plus(a, b):
    return jax.tree.map(lambda one, two: (one.astype(f32) + two.astype(f32)).astype(one.dtype), a, b)


def gather_slots(own):
    return receive_half(send_half(own))


def send_half(own):
    from_chip = to_chip(own)
    return own, to_core(own), from_chip


def receive_half(half):
    own, from_core, from_chip = half
    return [own, from_core, from_chip, to_core(from_chip)]


def scatter_slots(parts):
    far = plus(parts[2], to_core(parts[3]))
    return (parts[0], to_core(parts[1]), to_chip(far)), far


def scatter_halves(parts, token=None):
    from_core_far = to_core(parts[3])
    from_core = to_core(parts[1])
    rows = parts[0].shape[0] // 2
    terms = []
    for part in range(2):
        here = slice(part * rows, (part + 1) * rows)
        far = plus(parts[2][here], from_core_far[here])
        if token is not None:
            far = after(far, token)
        token = far
        terms.append((parts[0], from_core, to_chip(far)))
    return terms, token


def norm_rows(x, gain, shift):
    average = jnp.mean(x, axis=-1, keepdims=True)
    centred = x - average
    variance = jnp.mean(centred * centred, axis=-1, keepdims=True)
    return centred * lax.rsqrt(variance + norm_eps) * gain + shift


def norm_kernel(x_ref, gain_ref, shift_ref, out_ref):
    out_ref[...] = norm_rows(x_ref[...].astype(f32), gain_ref[...], shift_ref[...]).astype(bf16)


def norm_only(x, gain, shift):
    return pl.pallas_call(
        norm_kernel,
        out_shape=jax.ShapeDtypeStruct(x.shape, bf16),
        compiler_params=params(),
        cost_estimate=cost(x.size * 8, x.size * 4),
        name="norm_only",
    )(x, gain, shift)


def add_norm_kernel(x_ref, a_ref, b_ref, c_ref, add_ref, gain_ref, shift_ref, sum_ref, out_ref):
    total = x_ref[...].astype(f32) + (a_ref[...].astype(f32) + b_ref[...].astype(f32) + c_ref[...].astype(f32))
    total = (total + add_ref[...]).astype(sum_ref.dtype)
    sum_ref[...] = total
    out_ref[...] = norm_rows(total.astype(f32), gain_ref[...], shift_ref[...]).astype(bf16)


def add_norm(x, terms, part, add, gain, shift, sum_type):
    rows, width = terms[2].shape
    return pl.pallas_call(
        add_norm_kernel,
        grid=(1,),
        in_specs=[rows_spec(a, part, rows) for a in (x, *terms)] + [whole_spec(add.shape)] * 3,
        out_specs=[whole_spec((rows, width))] * 2,
        out_shape=(jax.ShapeDtypeStruct((rows, width), sum_type), jax.ShapeDtypeStruct((rows, width), bf16)),
        compiler_params=params(),
        cost_estimate=cost(rows * width * 12, rows * width * 14),
        name="add_norm",
    )(x, *terms, add, gain, shift)


def norm_back_kernel(x_ref, a_ref, b_ref, c_ref, gain_ref, more_ref, dx_ref, low_ref, small_ref):
    x = x_ref[...].astype(f32)
    grad = a_ref[...].astype(f32) + b_ref[...].astype(f32) + c_ref[...].astype(f32)
    average = jnp.mean(x, axis=-1, keepdims=True)
    centred = x - average
    variance = jnp.mean(centred * centred, axis=-1, keepdims=True)
    scale = lax.rsqrt(variance + norm_eps)
    unit = centred * scale
    wide = grad * gain_ref[...]
    mean_wide = jnp.mean(wide, axis=-1, keepdims=True)
    mean_unit = jnp.mean(wide * unit, axis=-1, keepdims=True)
    more = more_ref[...].astype(f32)
    dx = more + scale * (wide - mean_wide - unit * mean_unit)
    dx_ref[...] = dx
    low_ref[...] = dx.astype(bf16)
    small_ref[0:1, :] = jnp.sum(grad * unit, axis=0, keepdims=True)
    small_ref[1:2, :] = jnp.sum(grad, axis=0, keepdims=True)
    small_ref[2:3, :] = jnp.sum(more, axis=0, keepdims=True)
    small_ref[3:8, :] = jnp.zeros((5, x.shape[1]), f32)


def norm_back(x, terms, part, gain, more):
    rows, width = terms[2].shape
    return pl.pallas_call(
        norm_back_kernel,
        grid=(1,),
        in_specs=[rows_spec(a, part, rows) for a in (x, *terms)] + [whole_spec(gain.shape), rows_spec(more, part, rows)],
        out_specs=[whole_spec((rows, width))] * 2 + [whole_spec((8, width))],
        out_shape=(
            jax.ShapeDtypeStruct((rows, width), f32),
            jax.ShapeDtypeStruct((rows, width), bf16),
            jax.ShapeDtypeStruct((8, width), f32),
        ),
        compiler_params=params(),
        cost_estimate=cost(rows * width * 20, rows * width * 20),
        name="norm_back",
    )(x, *terms, gain, more)


def norm_back_small_kernel(x_ref, a_ref, b_ref, c_ref, small_ref):
    x = x_ref[...].astype(f32)
    grad = a_ref[...].astype(f32) + b_ref[...].astype(f32) + c_ref[...].astype(f32)
    average = jnp.mean(x, axis=-1, keepdims=True)
    centred = x - average
    variance = jnp.mean(centred * centred, axis=-1, keepdims=True)
    unit = centred * lax.rsqrt(variance + norm_eps)
    small_ref[0:1, :] = jnp.sum(grad * unit, axis=0, keepdims=True)
    small_ref[1:2, :] = jnp.sum(grad, axis=0, keepdims=True)
    small_ref[2:8, :] = jnp.zeros((6, x.shape[1]), f32)


def norm_back_small(x, terms):
    return pl.pallas_call(
        norm_back_small_kernel,
        out_shape=jax.ShapeDtypeStruct((8, x.shape[1]), f32),
        compiler_params=params(),
        cost_estimate=cost(x.size * 10, x.size * 8),
        name="norm_back_small",
    )(x, *terms)


log2_e = 1.4426950408889634


def fill_experts(target, source, experts, width):
    for j in range(experts):
        target[j * lanes : j * lanes + width, :] = source[j * width : (j + 1) * width, :]
        target[j * lanes + width : (j + 1) * lanes, :] = jnp.zeros((lanes - width, target.shape[1]), bf16)


def fill_weights(w_s, wo_s, wv_ref, wk_ref, wo_ref, experts, width):
    fill_experts(w_s, wv_ref, experts, width)
    fill_experts(wo_s, wo_ref, experts, width)
    start = 0
    for place, rows in ((experts + 1, width), (experts + 2, width), (experts, 2 * out_lane)):
        w_s[place * lanes : place * lanes + rows, :] = wk_ref[start : start + rows, :]
        w_s[place * lanes + rows : (place + 1) * lanes, :] = jnp.zeros((lanes - rows, w_s.shape[1]), bf16)
        start += rows


def attn_fwd_kernel(experts, head_width, slot_count, me_ref, *refs):
    mem_refs, slot_refs, refs = refs[:4], refs[4 : 4 + slot_count], refs[4 + slot_count :]
    wv_ref, wk_ref, wo_ref, mask_ref = refs[:4]
    *out_refs, normed_out, q_out, k_out, v_out, ev_out, gate_out, att_out, mixed_out = refs[4:16]
    normed, q_s, k_s, v_s, ev_s, gate_s, att_s, mixed_s, w_s, wo_s, out_s, mask_s, sems = refs[16:]
    me = me_ref[0]
    block = out_s.shape[1]
    quarter = block // 4
    wide = experts * lanes
    send = Sender(sems)

    for slot, ref in enumerate(mem_refs):
        here = slice(slot * quarter, (slot + 1) * quarter)
        normed[here, :] = ref[...]
        mask_s[here, :] = mask_ref[pl.ds(pl.multiple_of((me ^ slot) * quarter, quarter), quarter), :]
    halves = slot_count // 4
    rows = block // halves
    for number, ref in enumerate(slot_refs):
        start = (me ^ (number // halves)) * block + block + number % halves * rows
        normed[pl.ds(pl.multiple_of(start, rows), rows), :] = ref[...]
    send(normed, normed_out)
    fill_weights(w_s, wo_s, wv_ref, wk_ref, wo_ref, experts, head_width)

    scale = head_width ** (-0.5) * log2_e
    for i in range(5):
        here = slice(i * block, (i + 1) * block)
        proj = dot_t(normed[here, :], w_s[...])
        gate = jax.nn.sigmoid(proj[:, wide : wide + lanes]) * (mask_ref[here, :] if i else mask_s[...])
        value = gate[:, 0:1] * proj[:, 0:lanes]
        for j in range(1, experts):
            value = value + gate[:, j : j + 1] * proj[:, j * lanes : (j + 1) * lanes]
        k_s[here, :] = proj[:, wide + lanes : wide + 2 * lanes].astype(bf16)
        v_s[here, :] = value.astype(bf16)
        ev_s[here, :] = proj[:, :wide].astype(bf16)
        q_s[here, :] = (proj[:, wide + 2 * lanes :] * scale).astype(bf16)
        gate_s[here, :] = gate
    send(ev_s, ev_out)
    send(q_s, q_out)
    send(k_s, k_out)
    send(v_s, v_out)

    row = lax.broadcasted_iota(jnp.int32, (block, block), 0)
    col = lax.broadcasted_iota(jnp.int32, (block, block), 1)
    lane = lax.broadcasted_iota(jnp.int32, (block, lanes), 1)
    for i in range(1, 5):
        here, before = slice(i * block, (i + 1) * block), slice(0, i * block)
        own = slice((i - 1) * block, i * block)
        queries = q_s[here, :]
        early = dot_t(queries, k_s[before, :])
        late = jnp.where(col <= row, dot_t(queries, k_s[here, :]), masked_score)
        top = jnp.maximum(jnp.max(early, axis=-1, keepdims=True), jnp.max(late, axis=-1, keepdims=True))
        early = jnp.exp2(early - top)
        late = jnp.exp2(late - top)
        total = jnp.sum(early, axis=-1, keepdims=True) + jnp.sum(late, axis=-1, keepdims=True)
        attended = dot(early.astype(bf16), v_s[before, :]) + dot(late.astype(bf16), v_s[here, :])
        attended = attended * (1.0 / total)
        att_s[own, :] = attended
        gate = gate_s[here, :]
        gate_s[here, :] = jnp.where(lane == log_lane, top + jnp.log2(total), gate)
        for j in range(experts):
            opened = gate[:, out_lane + j : out_lane + j + 1] * attended
            mixed_s[own, j * lanes : (j + 1) * lanes] = opened.astype(bf16)
    send(gate_s, gate_out)
    send(att_s, att_out)
    send(mixed_s, mixed_out)
    for slot in (3, 2, 1, 0):
        start = pl.multiple_of((me ^ slot) * block, block)
        out_s[slot] = dot(mixed_s[pl.ds(start, block), :], wo_s[...]).astype(bf16)
        send(out_s.at[slot], out_refs[slot])
    send.wait()


def attn_fwd(me, mems, slots, w, mask, experts, head_width):
    width = mems[0].shape[1]
    block = 4 * mems[0].shape[0]
    total = 5 * block
    wide = experts * lanes
    shape = lambda rows, cols, kind: jax.ShapeDtypeStruct((rows, cols), kind)
    kept = [
        shape(total, width, bf16),
        *[shape(total, lanes, bf16)] * 3,
        shape(total, wide, bf16),
        shape(total, lanes, f32),
        shape(4 * block, lanes, f32),
        shape(4 * block, wide, bf16),
    ]
    outs = [shape(block, width, bf16)] * 4 + kept
    operands = (*mems, *slots, *w, mask)
    return pl.pallas_call(
        functools.partial(attn_fwd_kernel, experts, head_width, len(slots)),
        in_specs=[in_smem] + [in_vmem] * len(operands),
        out_specs=[anywhere] * len(outs),
        out_shape=outs,
        scratch_shapes=[pltpu.VMEM(a.shape, a.dtype) for a in kept]
        + [
            pltpu.VMEM((wide + 3 * lanes, width), bf16),
            pltpu.VMEM((wide, width), bf16),
            pltpu.VMEM((4, block, width), bf16),
            pltpu.VMEM((block, lanes), f32),
            pltpu.SemaphoreType.DMA((12,)),
        ],
        compiler_params=params(30),
        cost_estimate=cost(4 * total * width * wide, 16 * 1024 * 1024, total * total),
        name="attn_fwd",
    )(me, *operands)


def attn_bwd_kernel(experts, head_width, slot_count, me_ref, *refs):
    slot_refs, refs = refs[:slot_count], refs[slot_count:]
    wv_ref, wk_ref, wo_ref, q_ref, k_ref, v_ref, ev_ref, gate_ref, att_ref = refs[:9]
    *grad_outs, mem_out, dproj_out, rows_out = refs[9:16]
    w_s, wo_s, rows_s, dproj_s, grad_s, mem_s, dk_s, dv_s, sems = refs[16:]
    me = me_ref[0]
    block = mem_s.shape[0]
    wide = experts * lanes
    scale = head_width ** (-0.5)
    send = Sender(sems)

    halves = slot_count // 4
    rows = block // halves
    for number, ref in enumerate(slot_refs):
        start = (me ^ (number // halves)) * block + number % halves * rows
        rows_s[pl.ds(pl.multiple_of(start, rows), rows), :] = ref[...]
    send(rows_s, rows_out)
    fill_weights(w_s, wo_s, wv_ref, wk_ref, wo_ref, experts, head_width)

    row = lax.broadcasted_iota(jnp.int32, (block, block), 0)
    col = lax.broadcasted_iota(jnp.int32, (block, block), 1)
    lane = lax.broadcasted_iota(jnp.int32, (block, lanes), 1)
    for i in range(4, -1, -1):
        here = slice(i * block, (i + 1) * block)
        gate = gate_ref[here, :]
        logit_grad = jnp.zeros((block, lanes), f32)
        if i > 0:
            own = slice((i - 1) * block, i * block)
            mixed_grad = dot_t(rows_s[own, :], wo_s[...])
            attended = att_ref[own, :]
            att_grad = jnp.zeros((block, lanes), f32)
            for j in range(experts):
                part = mixed_grad[:, j * lanes : (j + 1) * lanes]
                att_grad = att_grad + gate[:, out_lane + j : out_lane + j + 1] * part
                inner = jnp.sum(part * attended, axis=-1, keepdims=True)
                logit_grad = jnp.where(lane == out_lane + j, inner, logit_grad)
            grad_low = att_grad.astype(bf16)
            row_sum = jnp.sum(att_grad * attended, axis=-1, keepdims=True)
            log_total = gate[:, log_lane : log_lane + 1]
            queries = q_ref[here, :]
            query_grad = jnp.zeros((block, lanes), f32)
            for span in (slice(0, i * block), here):
                keys = k_ref[span, :]
                scores = dot_t(queries, keys)
                if span is here:
                    scores = jnp.where(col <= row, scores, masked_score)
                probs = jnp.exp2(scores - log_total)
                score_grad = (probs * (dot_t(grad_low, v_ref[span, :]) - row_sum)).astype(bf16)
                query_grad = query_grad + dot(score_grad, keys)
                key_part = t_dot(score_grad, queries)
                value_part = t_dot(probs.astype(bf16), grad_low)
                if i == 4:
                    dk_s[span, :] = key_part
                    dv_s[span, :] = value_part
                else:
                    dk_s[span, :] += key_part
                    dv_s[span, :] += value_part
            dproj_s[here, wide + 2 * lanes :] = (query_grad * scale).astype(bf16)
        else:
            dproj_s[here, wide + 2 * lanes :] = jnp.zeros((block, lanes), bf16)
        value_grad = dv_s[here, :].astype(bf16).astype(f32)
        for j in range(experts):
            cols = slice(j * lanes, (j + 1) * lanes)
            dproj_s[here, cols] = (gate[:, j : j + 1] * value_grad).astype(bf16)
            inner = jnp.sum(value_grad * ev_ref[here, cols].astype(f32), axis=-1, keepdims=True)
            logit_grad = jnp.where(lane == j, inner, logit_grad)
        slope = jnp.where(lane < log_lane, gate * (1.0 - gate), 0.0)
        dproj_s[here, wide : wide + lanes] = (logit_grad * slope).astype(bf16)
        dproj_s[here, wide + lanes : wide + 2 * lanes] = (dk_s[here, :] * (1.0 / log2_e)).astype(bf16)
        normed_grad = dot(dproj_s[here, :], w_s[...]).astype(bf16)
        if i > 0:
            grad_s[pl.ds((i - 1) ^ me, 1)] = normed_grad[None]
        else:
            mem_s[...] = normed_grad
    for slot in (3, 2, 1, 0):
        send(grad_s.at[slot], grad_outs[slot])
    send(dproj_s, dproj_out)
    send(mem_s, mem_out)
    send.wait()


def attn_bwd(me, slots, w, saved, experts, head_width):
    width = slots[0].shape[1]
    block = sum(a.shape[0] for a in slots) // 4
    total = 5 * block
    wide = experts * lanes
    shape = lambda rows, cols: jax.ShapeDtypeStruct((rows, cols), bf16)
    outs = [shape(block, width)] * 5 + [shape(total, wide + 3 * lanes), shape(4 * block, width)]
    operands = (*slots, *w, *saved)
    return pl.pallas_call(
        functools.partial(attn_bwd_kernel, experts, head_width, len(slots)),
        in_specs=[in_smem] + [in_vmem] * len(operands),
        out_specs=[anywhere] * len(outs),
        out_shape=outs,
        scratch_shapes=[
            pltpu.VMEM((wide + 3 * lanes, width), bf16),
            pltpu.VMEM((wide, width), bf16),
            pltpu.VMEM((4 * block, width), bf16),
            pltpu.VMEM((total, wide + 3 * lanes), bf16),
            pltpu.VMEM((4, block, width), bf16),
            pltpu.VMEM((block, width), bf16),
            pltpu.VMEM((total, lanes), f32),
            pltpu.VMEM((total, lanes), f32),
            pltpu.SemaphoreType.DMA((7,)),
        ],
        compiler_params=params(32),
        cost_estimate=cost(4 * total * width * wide, 16 * 1024 * 1024, total * total),
        name="attn_bwd",
    )(me, *operands)


def gelu_parts(u):
    square = u * u
    t = jnp.tanh(gelu_c * u * (1.0 + gelu_a * square))
    slope = 0.5 * (1.0 + t) + 0.5 * gelu_c * u * (1.0 - t * t) * (1.0 + 3.0 * gelu_a * square)
    return 0.5 * u * (1.0 + t), slope


def load_pieces(target, refs, part):
    rows = target.shape[0] // len(refs)
    for number, ref in enumerate(refs):
        start = part * rows if ref.shape[0] > rows else 0
        target[number * rows : (number + 1) * rows, :] = ref[start : start + rows, :]


def send_rows(send, source, outs, span):
    rows = source.shape[0] // len(outs)
    for number in range(len(outs) - 1, -1, -1):
        if span.start <= number * rows < span.stop:
            send(source.at[pl.ds(number * rows, rows)], outs[number])


def two_spans(rows):
    return slice(0, rows // 2), slice(rows // 2, rows)


def ffn_fwd_kernel(part, *refs):
    pieces, (wu_ref, bu_ref, wd_ref) = refs[:4], refs[4:7]
    *outs, rows_out, upper_out, active_out = refs[-12:-5]
    rows_s, upper_s, active_s, out_s, sems = refs[-5:]
    send = Sender(sems)
    total = rows_s.shape[0]
    here = pl.ds(part * total, total)
    load_pieces(rows_s, pieces, part)
    send(rows_s, rows_out.at[here])
    for span in two_spans(total):
        upper = dot(rows_s[span, :], wu_ref[...]) + bu_ref[...]
        upper_s[span, :] = upper.astype(bf16)
        active_s[span, :] = jax.nn.gelu(upper).astype(bf16)
    send(upper_s, upper_out.at[here])
    send(active_s, active_out.at[here])
    for span in two_spans(total)[::-1]:
        out_s[span, :] = dot(active_s[span, :], wd_ref[...]).astype(bf16)
        send_rows(send, out_s, outs, span)
    send.wait()


def ffn_fwd(pieces, part, wu, bu, wd, earlier):
    rows, width = pieces[0].shape
    hidden = wu.shape[1]
    total = 4 * rows
    shape = lambda *dims: jax.ShapeDtypeStruct(dims, bf16)
    operands = (*pieces, wu, bu, wd)
    outs = [shape(rows, width)] * 4 + [shape(2 * total, width), shape(2 * total, hidden), shape(2 * total, hidden)]
    return pl.pallas_call(
        functools.partial(ffn_fwd_kernel, part),
        in_specs=[in_vmem] * len(operands) + [anywhere] * len(earlier),
        out_specs=[anywhere] * len(outs),
        out_shape=outs,
        input_output_aliases={len(operands) + i: 4 + i for i in range(len(earlier))},
        scratch_shapes=[
            pltpu.VMEM((total, width), bf16),
            pltpu.VMEM((total, hidden), bf16),
            pltpu.VMEM((total, hidden), bf16),
            pltpu.VMEM((total, width), bf16),
            pltpu.SemaphoreType.DMA((7,)),
        ],
        compiler_params=params(24),
        cost_estimate=cost(4 * total * width * hidden, 9 * 1024 * 1024, total * hidden),
        name="ffn_fwd",
    )(*operands, *earlier)


def ffn_bwd_kernel(part, forward, *refs):
    pieces, refs = refs[:4], refs[4:]
    if forward:
        normed_refs, (bu_ref, wd_ref, wu_ref), refs = refs[:4], refs[4:7], refs[7:]
        *outs, bias_out, rows_out, grad_out, normed_out, active_out = refs[-15:-6]
    else:
        (upper_ref, wd_ref, wu_ref), refs = refs[:3], refs[3:]
        *outs, bias_out, rows_out, grad_out = refs[-13:-6]
    rows_s, grad_s, out_s, normed_s, active_s, sems = refs[-6:]
    send = Sender(sems)
    total = rows_s.shape[0]
    here = pl.ds(part * total, total)
    load_pieces(rows_s, pieces, part)
    send(rows_s, rows_out.at[here])
    if forward:
        load_pieces(normed_s, normed_refs, part)
        send(normed_s, normed_out.at[here])
    sums = jnp.zeros((1, grad_s.shape[1]), f32)
    for span in two_spans(total):
        if forward:
            upper = dot(normed_s[span, :], wu_ref[...]) + bu_ref[...]
        else:
            upper = upper_ref[span, :].astype(f32)
        active_grad = dot_t(rows_s[span, :], wd_ref[...])
        active, slope = gelu_parts(upper)
        if forward:
            active_s[span, :] = active.astype(bf16)
        upper_grad = (active_grad * slope).astype(bf16)
        grad_s[span, :] = upper_grad
        sums = sums + jnp.sum(upper_grad.astype(f32), axis=0, keepdims=True)
    bias_out[...] = sums
    send(grad_s, grad_out.at[here])
    if forward:
        send(active_s, active_out.at[here])
    for span in two_spans(total)[::-1]:
        out_s[span, :] = dot_t(grad_s[span, :], wu_ref[...]).astype(bf16)
        send_rows(send, out_s, outs, span)
    send.wait()


def ffn_bwd(pieces, part, wd, wu, earlier, upper=None, normed=None, bu=None):
    forward = normed is not None
    width, hidden = wu.shape
    rows = min(a.shape[0] for a in (normed if forward else pieces))
    total = 4 * rows
    shape = lambda *dims: jax.ShapeDtypeStruct(dims, bf16)
    kept = [shape(2 * total, width), shape(2 * total, hidden)]
    outs = [shape(rows, width)] * 4 + [jax.ShapeDtypeStruct((1, hidden), f32)] + kept + (kept if forward else [])
    operands = (*pieces, *normed, bu, wd, wu) if forward else (*pieces, upper, wd, wu)
    specs = [whole_spec(a.shape) for a in operands]
    if not forward:
        specs[4] = rows_spec(upper, part, total)
    spare = (total, width) if forward else (8, lanes)
    return pl.pallas_call(
        functools.partial(ffn_bwd_kernel, part, forward),
        grid=(1,),
        in_specs=specs + [anywhere] * len(earlier),
        out_specs=[anywhere] * 4 + [whole_spec((1, hidden))] + [anywhere] * (len(outs) - 5),
        out_shape=outs,
        input_output_aliases={len(operands) + i: 5 + i for i in range(len(earlier))},
        scratch_shapes=[
            pltpu.VMEM((total, width), bf16),
            pltpu.VMEM((total, hidden), bf16),
            pltpu.VMEM((total, width), bf16),
            pltpu.VMEM(spare, bf16),
            pltpu.VMEM(spare, bf16),
            pltpu.SemaphoreType.DMA((8,)),
        ],
        compiler_params=params(36),
        cost_estimate=cost(4 * total * width * hidden, 9 * 1024 * 1024, total * hidden),
        name="ffn_bwd",
    )(*operands, *earlier)


def attn_grads_kernel(experts, head_width, *refs):
    sources, (out_ref, dproj_s, normed_s, mixed_s, rows_s, grad_s, loads, sems) = refs[:4], refs[4:]
    send = Sender(sems)
    fetch = Sender(loads)
    for source, target in zip(sources, (dproj_s, normed_s, mixed_s, rows_s)):
        fetch(source, target)

    def fill(start, left, right, counts):
        for pair in range(0, len(counts), 2):
            here = counts[pair : pair + 2]
            wide = t_dot(left[:, pair * lanes : (pair + len(here)) * lanes], right[...]).astype(bf16)
            for number, count in enumerate(here):
                grad_s[start : start + count, :] = wide[number * lanes : number * lanes + count]
                start += count
        return start

    fetch.copies[0].wait()
    fetch.copies[1].wait()
    pack = fill(0, dproj_s, normed_s, [head_width] * experts + [2 * out_lane] + [head_width] * 2)
    send(grad_s.at[pl.ds(0, pack)], out_ref.at[pl.ds(0, pack)])
    fetch.copies[2].wait()
    fetch.copies[3].wait()
    total = fill(pack, mixed_s, rows_s, [head_width] * experts)
    send(grad_s.at[pl.ds(pack, total - pack)], out_ref.at[pl.ds(pack, total - pack)])
    send.wait()


def attn_grads(dproj, normed, mixed, rows, experts, head_width):
    count = (2 * experts + 2) * head_width + 2 * out_lane
    width = normed.shape[1]
    operands = (dproj, normed, mixed, rows)
    return pl.pallas_call(
        functools.partial(attn_grads_kernel, experts, head_width),
        in_specs=[anywhere] * len(operands),
        out_specs=anywhere,
        out_shape=jax.ShapeDtypeStruct((count, width), bf16),
        scratch_shapes=[pltpu.VMEM(a.shape, a.dtype) for a in operands]
        + [pltpu.VMEM((count, width), bf16), pltpu.SemaphoreType.DMA((4,)), pltpu.SemaphoreType.DMA((2,))],
        compiler_params=params(28),
        cost_estimate=cost(0, 0),
        name="attn_grads",
    )(*operands)


class Chunk:
    def __init__(self, own, moving):
        self.own, self.moving, self.step, self.end = own, moving, 0, None


class Turns:
    def __init__(self):
        self.token = ()
        self.direct = lax.axis_size(dp_axis) != 4
        place = lax.axis_index(dp_axis)
        self.middle = (place == 1) | (place == 2)

    def __call__(self, *chunks):
        for chunk in chunks:
            self.turn(chunk)

    def turn(self, chunk):
        step = chunk.step
        chunk.step += 1
        if self.direct:
            if step == 0:
                chunk.end = lax.psum(plus(chunk.own, chunk.moving), dp_axis)
            return
        got = after(chunk.moving, self.token)
        if step == 3:
            chunk.end = jax.tree.map(lambda full, far: jnp.where(self.middle, full, far), chunk.own, got)
            return
        chunk.own = self.token = plus(chunk.own, got)
        pairs = ([(0, 1), (3, 2)], [(1, 2), (2, 1)], [(1, 0), (2, 3)])[step]
        chunk.moving = jax.tree.map(lambda a: lax.ppermute(a, dp_axis, pairs), chunk.own)


def order_turns(chunks):
    lags = (0, 1.5, 2.5, 3.5)
    left = [(number + lags[step], step, number) for number, chunk in enumerate(chunks) for step in range(chunk.step, 4)]
    return [chunks[number] for _, _, number in sorted(left)]


def split_tiles(rows):
    size = rows // 32 * 16
    return [rows - size, size]


def cut(a, pieces):
    rows = a.shape[0] // pieces
    return [a[i * rows : (i + 1) * rows] for i in range(pieces)]


def padded_rows(a, rows):
    return jnp.pad(a, ((0, rows - a.shape[0]), (0, 0)))


def swap_weights(weights, start_after):
    size = lax.axis_size(dp_axis)
    odd = lax.axis_index(dp_axis) % 2
    results, gots = [], []
    for a in weights:
        a = after(a, start_after, *gots[: max(0, len(gots) - 1)])
        if size % 2:
            gots.append(swap_section(a))
            results.append(gots[-1])
            continue
        rows = a.shape[0] // 2
        got = swap_section(lax.dynamic_slice_in_dim(a, odd * rows, rows, 0))
        gots.append(got)
        other = lax.ppermute(got, dp_axis, [(i, i ^ 1) for i in range(size)])
        results.append(jnp.concatenate([jnp.where(odd == 0, got, other), jnp.where(odd == 0, other, got)], axis=0))
    return results


def route_mask(value_ids, out_ids, experts, memory_len):
    lane = jnp.arange(lanes, dtype=jnp.int32)[None, :]
    out_full = jnp.pad(out_ids, ((0, 0), (memory_len, 0)), constant_values=-1)
    hit = jnp.zeros((value_ids.shape[1], lanes), jnp.bool_)
    for k in range(value_ids.shape[0]):
        hit = hit | (lane == value_ids[k][:, None])
        hit = hit | ((lane == out_full[k][:, None] + out_lane) & (out_full[k][:, None] >= 0))
    return hit.astype(f32)


def on_device(
    inputs,
    memory,
    value_routes,
    out_routes,
    ln1_gain,
    ln1_bias,
    query_weight,
    key_weight,
    value_weight,
    value_router,
    out_router,
    output_weight,
    ln2_gain,
    ln2_bias,
    up_weight,
    up_bias,
    down_weight,
    down_bias,
    out_cot,
):
    experts = value_router.shape[-1]
    head_width = query_weight.shape[-1]
    sec = lax.axis_index(section_axis)
    head = lax.axis_index(head_axis)
    me = head.astype(jnp.int32).reshape(1)
    first = sec == 0
    pick = lambda a, index: lax.dynamic_index_in_dim(a, index, 0, keepdims=False)
    memory_len = memory.shape[2] * lax.axis_size(head_axis)

    value_rows = experts * head_width
    router_rows = [padded_rows(a[0, 0].T, out_lane) for a in (value_router, out_router)]
    kqr = jnp.concatenate([key_weight[0, 0].T, query_weight[0, 0].T, *router_rows])
    weights = [value_weight[0, 0].T, kqr, output_weight[0, 0], up_weight[0], down_weight[0]]

    small = jnp.concatenate([ln1_gain, ln1_bias, ln2_gain, ln2_bias, up_bias, down_bias, ln1_gain, ln1_bias], axis=0)
    route_rows = jnp.concatenate(
        [
            jnp.transpose(value_routes[0, :, :, 0, :], (0, 2, 1)),
            jnp.pad(jnp.transpose(out_routes[0, :, :, 0, :], (0, 2, 1)), ((0, 0), (0, 0), (memory_len, 0)), constant_values=-1),
        ],
        axis=1,
    )
    sends = [small, pick(memory[0], 1 - sec), pick(route_rows, 1 - sec)]
    small_got, memory_got, routes_got = [swap_section(a) for a in sends]

    def both_layers(own, got):
        return jnp.where(first, own, got), jnp.where(first, got, own)

    smalls = both_layers(small, small_got)
    route_sets = both_layers(pick(route_rows, sec), routes_got)
    memories = both_layers(pick(memory[0], sec), memory_got)
    weight_sets = [both_layers(a, got) for a, got in zip(weights, swap_weights(weights, sends))]

    x = pick(inputs, sec)
    cot = pick(out_cot, sec)
    own_norm = norm_only(x, smalls[0][0:1], smalls[0][1:2])
    slots = gather_slots(own_norm)
    route_sets = after(route_sets, own_norm)
    topk = value_routes.shape[-1]

    layers = []
    for number in range(2):
        layer = SimpleNamespace(mem=memories[number], w=[a[number] for a in weight_sets[:3]])
        layer.wu, layer.wd = [a[number] for a in weight_sets[3:]]
        vec = smalls[number]
        layer.gain1, layer.shift1, layer.gain2, layer.shift2, layer.up_b, layer.down_b = (vec[i : i + 1] for i in range(6))
        routes = route_sets[number]
        layer.mask = route_mask(routes[:topk], routes[topk:, memory_len:], experts, memory_len)
        layers.append(layer)
    one, two = layers
    no_add = jnp.zeros_like(one.gain1)
    for layer in layers:
        layer.mem_slots = gather_slots(norm_only(after(layer.mem, own_norm), layer.gain1, layer.shift1))
    cot_slots = gather_slots(after(cot, slots[2], one.mem_slots[2]))
    slots[3] = after(slots[3], one.mask, two.mask)

    def attention(layer, slots):
        *out, layer.normed, q, k, v, ev, gate, att, layer.mixed = attn_fwd(
            me, layer.mem_slots, slots, layer.w, layer.mask, experts, head_width
        )
        layer.saved = (q, k, v, ev, gate, att)
        if layer is one:
            out[3] = after(out[3], cot_slots[2], two.mem_slots[2])
        terms, _ = scatter_halves(out)
        layer.hidden, halves = [], []
        for part in range(2):
            hidden, normed = add_norm(layer.rows[part], terms[part], part, no_add, layer.gain2, layer.shift2, f32)
            layer.hidden.append(hidden)
            halves.append(send_half(normed))
        return [receive_half(half) for half in halves]

    one.rows = [x, x]
    halves = attention(one, slots)
    kept = ()
    two.rows, sent = [], []
    for part in range(2):
        pieces = halves[part]
        *out, n2, upper, active = ffn_fwd(pieces, part, one.wu, one.up_b, one.wd, kept)
        kept = (n2, upper, active)
        terms, _ = scatter_slots(out)
        rows, normed = add_norm(one.hidden[part], terms, part, one.down_b, two.gain1, two.shift1, bf16)
        two.rows.append(rows)
        sent.append(send_half(normed))
    one.n2, one.upper, one.active = kept
    sent = [receive_half(half) for half in sent]
    halves = attention(two, [half[slot] for slot in range(4) for half in sent])

    def by_layer(one, two):
        got = swap_section(jnp.where(first, two, one))
        kept = jnp.where(first, one, two)
        return jnp.stack([jnp.where(first, kept, got), jnp.where(first, got, kept)])[None]

    def send_chunks(one, two, sizes):
        start = 0
        for size in sizes:
            part_one, part_two = one[start : start + size], two[start : start + size]
            start += size
            send = jnp.where(first, part_two, part_one)
            if chunks:
                send = after(send, chunks[-1].moving)
            chunks.append(Chunk(jnp.where(first, part_one, part_two), swap_section(send)))

    chunks = []
    turns = Turns()
    for number in (1, 0):
        layer = layers[number]
        if number == 1:
            g_rows = [cot, cot]
        kept = ()
        terms, layer.bias = [], []
        for part in range(2):
            pieces = halves[part]
            if number == 1:
                *out, sums_here, g_all, upper_grad, n2, active = ffn_bwd(
                    cot_slots, part, layer.wd, layer.wu, kept, normed=pieces, bu=layer.up_b
                )
                kept = (g_all, upper_grad, n2, active)
            else:
                *out, sums_here, g_all, upper_grad = ffn_bwd(pieces, part, layer.wd, layer.wu, kept, upper=layer.upper)
                kept = (g_all, upper_grad)
                n2, active = layer.n2, layer.active
            layer.bias.append(sums_here)
            terms_here, token = scatter_slots(out)
            terms.append(terms_here)
        layer.down = t_dot(active, after(g_all, token)).astype(bf16)
        layer.up = t_dot(after(n2, layer.down), upper_grad).astype(bf16)
        if number == 0:
            for grad, second in ((layer.down, two.down), (layer.up, two.up)):
                send_chunks(grad, second, [grad.shape[0] // 2] * 2)
        terms[1] = (*terms[1][0:2], after(terms[1][2], layer.up))
        hidden_grads, layer.small2, sent = [], [], []
        for part in range(2):
            dx, low, small_here = norm_back(layer.hidden[part], terms[part], part, layer.gain2, g_rows[part])
            hidden_grads.append(dx)
            layer.small2.append(small_here)
            sent.append(send_half(low))
        sent = [receive_half(half) for half in sent]
        slots = [half[slot] for slot in range(4) for half in sent]
        if number == 0:
            turns(chunks[0])
            slots[7] = after(slots[7], turns.token)
        else:
            down_out = dot(active, after(layer.wd, low)).astype(bf16)
            rows = down_out.shape[0] // 8
            last_parts = [
                jnp.concatenate([down_out[s * rows : (s + 1) * rows], down_out[(4 + s) * rows : (5 + s) * rows]])
                for s in range(4)
            ]
            last_terms, _ = scatter_halves(last_parts, sent[1][2])
        *ngs, ngm, dproj, a_all = attn_bwd(me, slots, layer.w, layer.saved, experts, head_width)
        if number == 1:
            ngs[3] = after(ngs[3], [here[2] for here in last_terms])
            near, from_core, _ = last_terms[0]
            last_out = jnp.concatenate(layer.hidden) + layer.down_b + near.astype(f32) + from_core.astype(f32)
            last_out = (last_out + jnp.concatenate([here[2] for here in last_terms]).astype(f32)).astype(bf16)
            layer_out = by_layer(jnp.concatenate(layer.rows), last_out)
        terms, token = scatter_halves(ngs)
        layer.attn = attn_grads(after(dproj, token), layer.normed, layer.mixed, a_all, experts, head_width)
        token = layer.attn
        if number == 0:
            pack = (experts + 2) * head_width + 2 * out_lane
            send_chunks(layer.attn, two.attn, split_tiles(pack) + split_tiles(value_rows))
            turns.token = layer.attn
            turns(chunks[0], chunks[1])
            token = turns.token
        terms[1] = (*terms[1][0:2], after(terms[1][2], token))
        rows_grads, low_grads, layer.small1, halves = [], [], [], []
        for part in range(2):
            dx, low, small_here = norm_back(layer.rows[part], terms[part], part, layer.gain1, hidden_grads[part])
            rows_grads.append(dx)
            low_grads.append(low)
            layer.small1.append(small_here)
            halves.append(send_half(low) if number == 1 else (low,))
        if number == 1:
            halves = [receive_half(half) for half in halves]
        g_rows = low_grads
        layer.mem_grads = cut(ngm, 4)
        layer.input_grad = jnp.concatenate(low_grads)

    mem_terms, _ = scatter_slots([jnp.concatenate(pair) for pair in zip(one.mem_grads, two.mem_grads)])
    rows = one.mem.shape[0]
    vecs = []
    for number, layer in enumerate(layers):
        small_mem = norm_back_small(layer.mem, [a[number * rows : (number + 1) * rows] for a in mem_terms])
        vecs.append((layer.small1[0] + layer.small1[1] + small_mem)[0:2])
        vecs.append((layer.small2[0] + layer.small2[1])[0:6])
    vec = jnp.concatenate(vecs)
    vec = vec + to_core(vec)
    vec = vec + to_chip(vec)
    vecs = [
        jnp.concatenate([part[0:5], layer.bias[0] + layer.bias[1], part[6:8]]) for part, layer in zip(cut(vec, 2), layers)
    ]
    down0, down1, up0, up1, pack0, pack1, out0, out1 = chunks
    out1.own = (out1.own, jnp.where(first, vecs[0], vecs[1]))
    out1.moving = (out1.moving, swap_section(jnp.where(first, vecs[1], vecs[0])))
    for chunk in order_turns(chunks):
        turns(chunk)
        if chunk is out1 and chunk.step == 1:
            last_sum = turns.token
    out_end, vec = out1.end
    input_grad = by_layer(*[after(layer.input_grad, last_sum) for layer in layers])
    join = lambda *parts: jnp.concatenate(parts).astype(f32)
    pack_sum = join(pack0.end, pack1.end)

    def take(start, count):
        return pack_sum[start : start + count].T[None, None]

    keys = value_rows + 2 * out_lane

    return (
        layer_out,
        input_grad,
        vec[0:1],
        vec[1:2],
        take(keys + head_width, head_width),
        take(keys, head_width),
        take(0, value_rows),
        take(value_rows, experts),
        take(value_rows + out_lane, experts),
        join(out0.end, out_end)[None, None],
        vec[2:3],
        vec[3:4],
        join(up0.end, up1.end)[None],
        vec[5:6],
        join(down0.end, down1.end)[None],
        vec[4:5],
    )


def solution(mesh):
    rows = P(dp_axis, head_axis, None)
    layer_rows = P(section_axis, dp_axis, head_axis, None)
    routes = P(section_axis, dp_axis, None, head_axis, None)
    by_layer = P(section_axis, None)
    by_head = P(section_axis, head_axis, None, None)
    up, up_shift, down = P(section_axis, None, head_axis), P(section_axis, head_axis), P(section_axis, head_axis, None)
    params = [by_layer] * 2 + [by_head] * 6 + [by_layer] * 2 + [up, up_shift, down, by_layer]
    return jax.shard_map(
        on_device,
        mesh=mesh,
        in_specs=(rows, layer_rows, routes, routes, *params, rows),
        out_specs=(layer_rows, layer_rows, *params),
        check_vma=False,
    )
```

```python
import functools
from types import SimpleNamespace

import jax
import jax.numpy as jnp
from jax import lax
from jax.experimental import pallas as pl
from jax.experimental.pallas import tpu as pltpu
from jax.sharding import PartitionSpec as P

norm_eps = 1e-05
masked_score = -1e30
section_axis, head_axis, dp_axis = "section", "head", "dp"
lanes = 128
out_lane = 8
log_lane = 16
bf16 = jnp.bfloat16
f32 = jnp.float32
gelu_c = 0.7978845608028654
gelu_a = 0.044715

core_pairs = [(0, 1), (1, 0), (2, 3), (3, 2)]
chip_pairs = [(0, 2), (2, 0), (1, 3), (3, 1)]


def dot(a, b):
    return lax.dot_general(a, b, (((1,), (0,)), ((), ())), preferred_element_type=f32)


def dot_t(a, b):
    return lax.dot_general(a, b, (((1,), (1,)), ((), ())), preferred_element_type=f32)


def t_dot(a, b):
    return lax.dot_general(a, b, (((0,), (0,)), ((), ())), preferred_element_type=f32)


def params(mebibytes=16):
    return pltpu.CompilerParams(vmem_limit_bytes=mebibytes * 1024 * 1024)


def whole_spec(shape):
    return pl.BlockSpec(shape, lambda *_: (0,) * len(shape))


def rows_spec(a, part, rows):
    index = part if a.shape[0] > rows else 0
    return pl.BlockSpec((rows, a.shape[1]), lambda *_: (index, 0))


in_vmem = pl.BlockSpec(memory_space=pltpu.VMEM)
in_smem = pl.BlockSpec(memory_space=pltpu.SMEM)
anywhere = pl.BlockSpec(memory_space=pl.ANY)


class Sender:
    def __init__(self, sems):
        self.sems, self.copies = sems, []

    def __call__(self, source, target):
        copy = pltpu.make_async_copy(source, target, self.sems.at[len(self.copies)])
        copy.start()
        self.copies.append(copy)

    def wait(self):
        for copy in self.copies:
            copy.wait()


def cost(flops, nbytes, trans=0):
    return pl.CostEstimate(flops=int(flops), bytes_accessed=int(nbytes), transcendentals=int(trans))


def to_core(a):
    return lax.ppermute(a, head_axis, core_pairs)


def to_chip(a):
    return lax.ppermute(a, head_axis, chip_pairs)


def swap_section(a):
    return lax.ppermute(a, section_axis, [(0, 1), (1, 0)])


def after(a, *tokens):
    return lax.optimization_barrier((a, tokens))[0]


def plus(a, b):
    return jax.tree.map(lambda one, two: (one.astype(f32) + two.astype(f32)).astype(one.dtype), a, b)


def gather_slots(own):
    return receive_half(send_half(own))


def send_half(own):
    from_chip = to_chip(own)
    return own, to_core(own), from_chip


def receive_half(half):
    own, from_core, from_chip = half
    return [own, from_core, from_chip, to_core(from_chip)]


def in_order(terms, sent):
    return (*terms[0:2], after(terms[2], sent[-1][0])) if sent else terms


def scatter_slots(parts):
    far = plus(parts[2], to_core(parts[3]))
    return (parts[0], to_core(parts[1]), to_chip(far)), far


def scatter_halves(parts, token=None):
    from_core_far = to_core(parts[3])
    from_core = to_core(parts[1])
    rows = parts[0].shape[0] // 2
    terms = []
    for part in range(2):
        here = slice(part * rows, (part + 1) * rows)
        far = plus(parts[2][here], from_core_far[here])
        if token is not None:
            far = after(far, token)
        token = far
        terms.append((parts[0], from_core, to_chip(far)))
    return terms, token


def norm_rows(x, gain, shift):
    average = jnp.mean(x, axis=-1, keepdims=True)
    centred = x - average
    variance = jnp.mean(centred * centred, axis=-1, keepdims=True)
    return centred * lax.rsqrt(variance + norm_eps) * gain + shift


def norm_kernel(x_ref, gain_ref, shift_ref, out_ref):
    out_ref[...] = norm_rows(x_ref[...].astype(f32), gain_ref[...], shift_ref[...]).astype(bf16)


def norm_only(x, gain, shift):
    return pl.pallas_call(
        norm_kernel,
        out_shape=jax.ShapeDtypeStruct(x.shape, bf16),
        compiler_params=params(),
        cost_estimate=cost(x.size * 8, x.size * 4),
        name="norm_only",
    )(x, gain, shift)


def add_norm_kernel(x_ref, a_ref, b_ref, c_ref, add_ref, gain_ref, shift_ref, sum_ref, out_ref):
    total = x_ref[...].astype(f32) + (a_ref[...].astype(f32) + b_ref[...].astype(f32) + c_ref[...].astype(f32))
    total = (total + add_ref[...]).astype(sum_ref.dtype)
    sum_ref[...] = total
    out_ref[...] = norm_rows(total.astype(f32), gain_ref[...], shift_ref[...]).astype(bf16)


def add_norm(x, terms, part, add, gain, shift, sum_type):
    rows, width = terms[2].shape
    return pl.pallas_call(
        add_norm_kernel,
        grid=(1,),
        in_specs=[rows_spec(a, part, rows) for a in (x, *terms)] + [whole_spec(add.shape)] * 3,
        out_specs=[whole_spec((rows, width))] * 2,
        out_shape=(jax.ShapeDtypeStruct((rows, width), sum_type), jax.ShapeDtypeStruct((rows, width), bf16)),
        compiler_params=params(),
        cost_estimate=cost(rows * width * 12, rows * width * 14),
        name="add_norm",
    )(x, *terms, add, gain, shift)


def norm_back_kernel(x_ref, a_ref, b_ref, c_ref, gain_ref, more_ref, dx_ref, low_ref, small_ref):
    x = x_ref[...].astype(f32)
    grad = a_ref[...].astype(f32) + b_ref[...].astype(f32) + c_ref[...].astype(f32)
    average = jnp.mean(x, axis=-1, keepdims=True)
    centred = x - average
    variance = jnp.mean(centred * centred, axis=-1, keepdims=True)
    scale = lax.rsqrt(variance + norm_eps)
    unit = centred * scale
    wide = grad * gain_ref[...]
    mean_wide = jnp.mean(wide, axis=-1, keepdims=True)
    mean_unit = jnp.mean(wide * unit, axis=-1, keepdims=True)
    more = more_ref[...].astype(f32)
    dx = more + scale * (wide - mean_wide - unit * mean_unit)
    dx_ref[...] = dx
    low_ref[...] = dx.astype(bf16)
    small_ref[0:1, :] = jnp.sum(grad * unit, axis=0, keepdims=True)
    small_ref[1:2, :] = jnp.sum(grad, axis=0, keepdims=True)
    small_ref[2:3, :] = jnp.sum(more, axis=0, keepdims=True)
    small_ref[3:8, :] = jnp.zeros((5, x.shape[1]), f32)


def norm_back(x, terms, part, gain, more):
    rows, width = terms[2].shape
    return pl.pallas_call(
        norm_back_kernel,
        grid=(1,),
        in_specs=[rows_spec(a, part, rows) for a in (x, *terms)] + [whole_spec(gain.shape), rows_spec(more, part, rows)],
        out_specs=[whole_spec((rows, width))] * 2 + [whole_spec((8, width))],
        out_shape=(
            jax.ShapeDtypeStruct((rows, width), f32),
            jax.ShapeDtypeStruct((rows, width), bf16),
            jax.ShapeDtypeStruct((8, width), f32),
        ),
        compiler_params=params(),
        cost_estimate=cost(rows * width * 20, rows * width * 20),
        name="norm_back",
    )(x, *terms, gain, more)


def norm_back_small_kernel(x_ref, a_ref, b_ref, c_ref, small_ref):
    x = x_ref[...].astype(f32)
    grad = a_ref[...].astype(f32) + b_ref[...].astype(f32) + c_ref[...].astype(f32)
    average = jnp.mean(x, axis=-1, keepdims=True)
    centred = x - average
    variance = jnp.mean(centred * centred, axis=-1, keepdims=True)
    unit = centred * lax.rsqrt(variance + norm_eps)
    small_ref[0:1, :] = jnp.sum(grad * unit, axis=0, keepdims=True)
    small_ref[1:2, :] = jnp.sum(grad, axis=0, keepdims=True)
    small_ref[2:8, :] = jnp.zeros((6, x.shape[1]), f32)


def norm_back_small(x, terms):
    return pl.pallas_call(
        norm_back_small_kernel,
        out_shape=jax.ShapeDtypeStruct((8, x.shape[1]), f32),
        compiler_params=params(),
        cost_estimate=cost(x.size * 10, x.size * 8),
        name="norm_back_small",
    )(x, *terms)


log2_e = 1.4426950408889634


def fill_experts(target, source, experts, width):
    for j in range(experts):
        target[j * lanes : j * lanes + width, :] = source[j * width : (j + 1) * width, :]
        target[j * lanes + width : (j + 1) * lanes, :] = jnp.zeros((lanes - width, target.shape[1]), bf16)


def fill_weights(w_s, wo_s, wv_ref, wk_ref, wo_ref, experts, width):
    fill_experts(w_s, wv_ref, experts, width)
    fill_experts(wo_s, wo_ref, experts, width)
    start = 0
    for place, rows in ((experts + 1, width), (experts + 2, width), (experts, 2 * out_lane)):
        w_s[place * lanes : place * lanes + rows, :] = wk_ref[start : start + rows, :]
        w_s[place * lanes + rows : (place + 1) * lanes, :] = jnp.zeros((lanes - rows, w_s.shape[1]), bf16)
        start += rows


def attn_fwd_kernel(experts, head_width, slot_count, me_ref, *refs):
    mem_refs, slot_refs, refs = refs[:4], refs[4 : 4 + slot_count], refs[4 + slot_count :]
    wv_ref, wk_ref, wo_ref, mask_ref = refs[:4]
    *out_refs, normed_out, q_out, k_out, v_out, ev_out, gate_out, att_out, mixed_out = refs[4:16]
    normed, q_s, k_s, v_s, ev_s, gate_s, att_s, mixed_s, w_s, wo_s, out_s, mask_s, sems = refs[16:]
    me = me_ref[0]
    block = out_s.shape[1]
    quarter = block // 4
    wide = experts * lanes
    send = Sender(sems)

    for slot, ref in enumerate(mem_refs):
        here = slice(slot * quarter, (slot + 1) * quarter)
        normed[here, :] = ref[...]
        mask_s[here, :] = mask_ref[pl.ds(pl.multiple_of((me ^ slot) * quarter, quarter), quarter), :]
    halves = slot_count // 4
    rows = block // halves
    for number, ref in enumerate(slot_refs):
        start = (me ^ (number // halves)) * block + block + number % halves * rows
        normed[pl.ds(pl.multiple_of(start, rows), rows), :] = ref[...]
    send(normed, normed_out)
    fill_weights(w_s, wo_s, wv_ref, wk_ref, wo_ref, experts, head_width)

    scale = head_width ** (-0.5) * log2_e
    for i in range(5):
        here = slice(i * block, (i + 1) * block)
        proj = dot_t(normed[here, :], w_s[...])
        gate = jax.nn.sigmoid(proj[:, wide : wide + lanes]) * (mask_ref[here, :] if i else mask_s[...])
        value = gate[:, 0:1] * proj[:, 0:lanes]
        for j in range(1, experts):
            value = value + gate[:, j : j + 1] * proj[:, j * lanes : (j + 1) * lanes]
        k_s[here, :] = proj[:, wide + lanes : wide + 2 * lanes].astype(bf16)
        v_s[here, :] = value.astype(bf16)
        ev_s[here, :] = proj[:, :wide].astype(bf16)
        q_s[here, :] = (proj[:, wide + 2 * lanes :] * scale).astype(bf16)
        gate_s[here, :] = gate
    send(ev_s, ev_out)
    send(q_s, q_out)
    send(k_s, k_out)
    send(v_s, v_out)

    row = lax.broadcasted_iota(jnp.int32, (block, block), 0)
    col = lax.broadcasted_iota(jnp.int32, (block, block), 1)
    lane = lax.broadcasted_iota(jnp.int32, (block, lanes), 1)
    for i in range(1, 5):
        here, before = slice(i * block, (i + 1) * block), slice(0, i * block)
        own = slice((i - 1) * block, i * block)
        queries = q_s[here, :]
        early = dot_t(queries, k_s[before, :])
        late = jnp.where(col <= row, dot_t(queries, k_s[here, :]), masked_score)
        top = jnp.maximum(jnp.max(early, axis=-1, keepdims=True), jnp.max(late, axis=-1, keepdims=True))
        early = jnp.exp2(early - top)
        late = jnp.exp2(late - top)
        total = jnp.sum(early, axis=-1, keepdims=True) + jnp.sum(late, axis=-1, keepdims=True)
        attended = dot(early.astype(bf16), v_s[before, :]) + dot(late.astype(bf16), v_s[here, :])
        attended = attended * (1.0 / total)
        att_s[own, :] = attended
        gate = gate_s[here, :]
        gate_s[here, :] = jnp.where(lane == log_lane, top + jnp.log2(total), gate)
        for j in range(experts):
            opened = gate[:, out_lane + j : out_lane + j + 1] * attended
            mixed_s[own, j * lanes : (j + 1) * lanes] = opened.astype(bf16)
    send(gate_s, gate_out)
    send(att_s, att_out)
    send(mixed_s, mixed_out)
    for slot in (3, 2, 1, 0):
        start = pl.multiple_of((me ^ slot) * block, block)
        out_s[slot] = dot(mixed_s[pl.ds(start, block), :], wo_s[...]).astype(bf16)
        send(out_s.at[slot], out_refs[slot])
    send.wait()


def attn_fwd(me, mems, slots, w, mask, experts, head_width):
    width = mems[0].shape[1]
    block = 4 * mems[0].shape[0]
    total = 5 * block
    wide = experts * lanes
    shape = lambda rows, cols, kind: jax.ShapeDtypeStruct((rows, cols), kind)
    kept = [
        shape(total, width, bf16),
        *[shape(total, lanes, bf16)] * 3,
        shape(total, wide, bf16),
        shape(total, lanes, f32),
        shape(4 * block, lanes, f32),
        shape(4 * block, wide, bf16),
    ]
    outs = [shape(block, width, bf16)] * 4 + kept
    operands = (*mems, *slots, *w, mask)
    return pl.pallas_call(
        functools.partial(attn_fwd_kernel, experts, head_width, len(slots)),
        in_specs=[in_smem] + [in_vmem] * len(operands),
        out_specs=[anywhere] * len(outs),
        out_shape=outs,
        scratch_shapes=[pltpu.VMEM(a.shape, a.dtype) for a in kept]
        + [
            pltpu.VMEM((wide + 3 * lanes, width), bf16),
            pltpu.VMEM((wide, width), bf16),
            pltpu.VMEM((4, block, width), bf16),
            pltpu.VMEM((block, lanes), f32),
            pltpu.SemaphoreType.DMA((12,)),
        ],
        compiler_params=params(30),
        cost_estimate=cost(4 * total * width * wide, 16 * 1024 * 1024, total * total),
        name="attn_fwd",
    )(me, *operands)


def attn_bwd_kernel(experts, head_width, slot_count, me_ref, *refs):
    slot_refs, refs = refs[:slot_count], refs[slot_count:]
    wv_ref, wk_ref, wo_ref, q_ref, k_ref, v_ref, ev_ref, gate_ref, att_ref = refs[:9]
    *grad_outs, mem_out, dproj_out, rows_out = refs[9:16]
    w_s, wo_s, rows_s, dproj_s, grad_s, mem_s, dk_s, dv_s, sems = refs[16:]
    me = me_ref[0]
    block = mem_s.shape[0]
    wide = experts * lanes
    scale = head_width ** (-0.5)
    send = Sender(sems)

    halves = slot_count // 4
    rows = block // halves
    for number, ref in enumerate(slot_refs):
        start = (me ^ (number // halves)) * block + number % halves * rows
        rows_s[pl.ds(pl.multiple_of(start, rows), rows), :] = ref[...]
    send(rows_s, rows_out)
    fill_weights(w_s, wo_s, wv_ref, wk_ref, wo_ref, experts, head_width)

    row = lax.broadcasted_iota(jnp.int32, (block, block), 0)
    col = lax.broadcasted_iota(jnp.int32, (block, block), 1)
    lane = lax.broadcasted_iota(jnp.int32, (block, lanes), 1)
    for i in range(4, -1, -1):
        here = slice(i * block, (i + 1) * block)
        gate = gate_ref[here, :]
        logit_grad = jnp.zeros((block, lanes), f32)
        if i > 0:
            own = slice((i - 1) * block, i * block)
            mixed_grad = dot_t(rows_s[own, :], wo_s[...])
            attended = att_ref[own, :]
            att_grad = jnp.zeros((block, lanes), f32)
            for j in range(experts):
                part = mixed_grad[:, j * lanes : (j + 1) * lanes]
                att_grad = att_grad + gate[:, out_lane + j : out_lane + j + 1] * part
                inner = jnp.sum(part * attended, axis=-1, keepdims=True)
                logit_grad = jnp.where(lane == out_lane + j, inner, logit_grad)
            grad_low = att_grad.astype(bf16)
            row_sum = jnp.sum(att_grad * attended, axis=-1, keepdims=True)
            log_total = gate[:, log_lane : log_lane + 1]
            queries = q_ref[here, :]
            query_grad = jnp.zeros((block, lanes), f32)
            for span in (slice(0, i * block), here):
                keys = k_ref[span, :]
                scores = dot_t(queries, keys)
                if span is here:
                    scores = jnp.where(col <= row, scores, masked_score)
                probs = jnp.exp2(scores - log_total)
                score_grad = (probs * (dot_t(grad_low, v_ref[span, :]) - row_sum)).astype(bf16)
                query_grad = query_grad + dot(score_grad, keys)
                key_part = t_dot(score_grad, queries)
                value_part = t_dot(probs.astype(bf16), grad_low)
                if i == 4:
                    dk_s[span, :] = key_part
                    dv_s[span, :] = value_part
                else:
                    dk_s[span, :] += key_part
                    dv_s[span, :] += value_part
            dproj_s[here, wide + 2 * lanes :] = (query_grad * scale).astype(bf16)
        else:
            dproj_s[here, wide + 2 * lanes :] = jnp.zeros((block, lanes), bf16)
        value_grad = dv_s[here, :].astype(bf16).astype(f32)
        for j in range(experts):
            cols = slice(j * lanes, (j + 1) * lanes)
            dproj_s[here, cols] = (gate[:, j : j + 1] * value_grad).astype(bf16)
            inner = jnp.sum(value_grad * ev_ref[here, cols].astype(f32), axis=-1, keepdims=True)
            logit_grad = jnp.where(lane == j, inner, logit_grad)
        slope = jnp.where(lane < log_lane, gate * (1.0 - gate), 0.0)
        dproj_s[here, wide : wide + lanes] = (logit_grad * slope).astype(bf16)
        dproj_s[here, wide + lanes : wide + 2 * lanes] = (dk_s[here, :] * (1.0 / log2_e)).astype(bf16)
        normed_grad = dot(dproj_s[here, :], w_s[...]).astype(bf16)
        if i > 0:
            grad_s[pl.ds((i - 1) ^ me, 1)] = normed_grad[None]
        else:
            mem_s[...] = normed_grad
    for slot in (3, 2, 1, 0):
        send(grad_s.at[slot], grad_outs[slot])
    send(dproj_s, dproj_out)
    send(mem_s, mem_out)
    send.wait()


def attn_bwd(me, slots, w, saved, experts, head_width):
    width = slots[0].shape[1]
    block = sum(a.shape[0] for a in slots) // 4
    total = 5 * block
    wide = experts * lanes
    shape = lambda rows, cols: jax.ShapeDtypeStruct((rows, cols), bf16)
    outs = [shape(block, width)] * 5 + [shape(total, wide + 3 * lanes), shape(4 * block, width)]
    operands = (*slots, *w, *saved)
    return pl.pallas_call(
        functools.partial(attn_bwd_kernel, experts, head_width, len(slots)),
        in_specs=[in_smem] + [in_vmem] * len(operands),
        out_specs=[anywhere] * len(outs),
        out_shape=outs,
        scratch_shapes=[
            pltpu.VMEM((wide + 3 * lanes, width), bf16),
            pltpu.VMEM((wide, width), bf16),
            pltpu.VMEM((4 * block, width), bf16),
            pltpu.VMEM((total, wide + 3 * lanes), bf16),
            pltpu.VMEM((4, block, width), bf16),
            pltpu.VMEM((block, width), bf16),
            pltpu.VMEM((total, lanes), f32),
            pltpu.VMEM((total, lanes), f32),
            pltpu.SemaphoreType.DMA((7,)),
        ],
        compiler_params=params(32),
        cost_estimate=cost(4 * total * width * wide, 16 * 1024 * 1024, total * total),
        name="attn_bwd",
    )(me, *operands)


def gelu_parts(u):
    square = u * u
    t = jnp.tanh(gelu_c * u * (1.0 + gelu_a * square))
    slope = 0.5 * (1.0 + t) + 0.5 * gelu_c * u * (1.0 - t * t) * (1.0 + 3.0 * gelu_a * square)
    return 0.5 * u * (1.0 + t), slope


def load_pieces(target, refs, part):
    rows = target.shape[0] // len(refs)
    for number, ref in enumerate(refs):
        start = part * rows if ref.shape[0] > rows else 0
        target[number * rows : (number + 1) * rows, :] = ref[start : start + rows, :]


def send_rows(send, source, outs, span):
    rows = source.shape[0] // len(outs)
    for number in range(len(outs) - 1, -1, -1):
        if span.start <= number * rows < span.stop:
            send(source.at[pl.ds(number * rows, rows)], outs[number])


def two_spans(rows):
    return slice(0, rows // 2), slice(rows // 2, rows)


def ffn_fwd_kernel(part, *refs):
    pieces, (wu_ref, bu_ref, wd_ref) = refs[:4], refs[4:7]
    *outs, rows_out, upper_out, active_out = refs[-12:-5]
    rows_s, upper_s, active_s, out_s, sems = refs[-5:]
    send = Sender(sems)
    total = rows_s.shape[0]
    here = pl.ds(part * total, total)
    load_pieces(rows_s, pieces, part)
    send(rows_s, rows_out.at[here])
    for span in two_spans(total):
        upper = dot(rows_s[span, :], wu_ref[...]) + bu_ref[...]
        upper_s[span, :] = upper.astype(bf16)
        active_s[span, :] = jax.nn.gelu(upper).astype(bf16)
    send(upper_s, upper_out.at[here])
    send(active_s, active_out.at[here])
    for span in two_spans(total)[::-1]:
        out_s[span, :] = dot(active_s[span, :], wd_ref[...]).astype(bf16)
        send_rows(send, out_s, outs, span)
    send.wait()


def ffn_fwd(pieces, part, wu, bu, wd, earlier):
    rows, width = pieces[0].shape
    hidden = wu.shape[1]
    total = 4 * rows
    shape = lambda *dims: jax.ShapeDtypeStruct(dims, bf16)
    operands = (*pieces, wu, bu, wd)
    outs = [shape(rows, width)] * 4 + [shape(2 * total, width), shape(2 * total, hidden), shape(2 * total, hidden)]
    return pl.pallas_call(
        functools.partial(ffn_fwd_kernel, part),
        in_specs=[in_vmem] * len(operands) + [anywhere] * len(earlier),
        out_specs=[anywhere] * len(outs),
        out_shape=outs,
        input_output_aliases={len(operands) + i: 4 + i for i in range(len(earlier))},
        scratch_shapes=[
            pltpu.VMEM((total, width), bf16),
            pltpu.VMEM((total, hidden), bf16),
            pltpu.VMEM((total, hidden), bf16),
            pltpu.VMEM((total, width), bf16),
            pltpu.SemaphoreType.DMA((7,)),
        ],
        compiler_params=params(24),
        cost_estimate=cost(4 * total * width * hidden, 9 * 1024 * 1024, total * hidden),
        name="ffn_fwd",
    )(*operands, *earlier)


def ffn_bwd_kernel(part, forward, *refs):
    pieces, refs = refs[:4], refs[4:]
    if forward:
        normed_refs, (bu_ref, wd_ref, wu_ref), refs = refs[:4], refs[4:7], refs[7:]
        *outs, bias_out, rows_out, grad_out, normed_out, active_out = refs[-15:-6]
    else:
        (upper_ref, wd_ref, wu_ref), refs = refs[:3], refs[3:]
        *outs, bias_out, rows_out, grad_out = refs[-13:-6]
    rows_s, grad_s, out_s, normed_s, active_s, sems = refs[-6:]
    send = Sender(sems)
    total = rows_s.shape[0]
    here = pl.ds(part * total, total)
    load_pieces(rows_s, pieces, part)
    send(rows_s, rows_out.at[here])
    if forward:
        load_pieces(normed_s, normed_refs, part)
        send(normed_s, normed_out.at[here])
    sums = jnp.zeros((1, grad_s.shape[1]), f32)
    for span in two_spans(total):
        if forward:
            upper = dot(normed_s[span, :], wu_ref[...]) + bu_ref[...]
        else:
            upper = upper_ref[span, :].astype(f32)
        active_grad = dot_t(rows_s[span, :], wd_ref[...])
        active, slope = gelu_parts(upper)
        if forward:
            active_s[span, :] = active.astype(bf16)
        upper_grad = (active_grad * slope).astype(bf16)
        grad_s[span, :] = upper_grad
        sums = sums + jnp.sum(upper_grad.astype(f32), axis=0, keepdims=True)
    bias_out[...] = sums
    send(grad_s, grad_out.at[here])
    if forward:
        send(active_s, active_out.at[here])
    for span in two_spans(total)[::-1]:
        out_s[span, :] = dot_t(grad_s[span, :], wu_ref[...]).astype(bf16)
        send_rows(send, out_s, outs, span)
    send.wait()


def ffn_bwd(pieces, part, wd, wu, earlier, upper=None, normed=None, bu=None):
    forward = normed is not None
    width, hidden = wu.shape
    rows = min(a.shape[0] for a in (normed if forward else pieces))
    total = 4 * rows
    shape = lambda *dims: jax.ShapeDtypeStruct(dims, bf16)
    kept = [shape(2 * total, width), shape(2 * total, hidden)]
    outs = [shape(rows, width)] * 4 + [jax.ShapeDtypeStruct((1, hidden), f32)] + kept + (kept if forward else [])
    operands = (*pieces, *normed, bu, wd, wu) if forward else (*pieces, upper, wd, wu)
    specs = [whole_spec(a.shape) for a in operands]
    if not forward:
        specs[4] = rows_spec(upper, part, total)
    spare = (total, width) if forward else (8, lanes)
    return pl.pallas_call(
        functools.partial(ffn_bwd_kernel, part, forward),
        grid=(1,),
        in_specs=specs + [anywhere] * len(earlier),
        out_specs=[anywhere] * 4 + [whole_spec((1, hidden))] + [anywhere] * (len(outs) - 5),
        out_shape=outs,
        input_output_aliases={len(operands) + i: 5 + i for i in range(len(earlier))},
        scratch_shapes=[
            pltpu.VMEM((total, width), bf16),
            pltpu.VMEM((total, hidden), bf16),
            pltpu.VMEM((total, width), bf16),
            pltpu.VMEM(spare, bf16),
            pltpu.VMEM(spare, bf16),
            pltpu.SemaphoreType.DMA((8,)),
        ],
        compiler_params=params(36),
        cost_estimate=cost(4 * total * width * hidden, 9 * 1024 * 1024, total * hidden),
        name="ffn_bwd",
    )(*operands, *earlier)


def attn_grads_kernel(experts, head_width, *refs):
    sources, (out_ref, dproj_s, normed_s, mixed_s, rows_s, grad_s, loads, sems) = refs[:4], refs[4:]
    send = Sender(sems)
    fetch = Sender(loads)
    for source, target in zip(sources, (dproj_s, normed_s, mixed_s, rows_s)):
        fetch(source, target)

    def fill(start, left, right, counts):
        for pair in range(0, len(counts), 2):
            here = counts[pair : pair + 2]
            wide = t_dot(left[:, pair * lanes : (pair + len(here)) * lanes], right[...]).astype(bf16)
            for number, count in enumerate(here):
                grad_s[start : start + count, :] = wide[number * lanes : number * lanes + count]
                start += count
        return start

    fetch.copies[0].wait()
    fetch.copies[1].wait()
    pack = fill(0, dproj_s, normed_s, [head_width] * experts + [2 * out_lane] + [head_width] * 2)
    send(grad_s.at[pl.ds(0, pack)], out_ref.at[pl.ds(0, pack)])
    fetch.copies[2].wait()
    fetch.copies[3].wait()
    total = fill(pack, mixed_s, rows_s, [head_width] * experts)
    send(grad_s.at[pl.ds(pack, total - pack)], out_ref.at[pl.ds(pack, total - pack)])
    send.wait()


def attn_grads(dproj, normed, mixed, rows, experts, head_width):
    count = (2 * experts + 2) * head_width + 2 * out_lane
    width = normed.shape[1]
    operands = (dproj, normed, mixed, rows)
    return pl.pallas_call(
        functools.partial(attn_grads_kernel, experts, head_width),
        in_specs=[anywhere] * len(operands),
        out_specs=anywhere,
        out_shape=jax.ShapeDtypeStruct((count, width), bf16),
        scratch_shapes=[pltpu.VMEM(a.shape, a.dtype) for a in operands]
        + [pltpu.VMEM((count, width), bf16), pltpu.SemaphoreType.DMA((4,)), pltpu.SemaphoreType.DMA((2,))],
        compiler_params=params(28),
        cost_estimate=cost(0, 0),
        name="attn_grads",
    )(*operands)


class Chunk:
    def __init__(self, own, moving):
        self.own, self.moving, self.step, self.end = own, moving, 0, None


class Turns:
    def __init__(self):
        self.token = ()
        self.direct = lax.axis_size(dp_axis) != 4
        place = lax.axis_index(dp_axis)
        self.middle = (place == 1) | (place == 2)

    def __call__(self, *chunks):
        for chunk in chunks:
            self.turn(chunk)

    def turn(self, chunk):
        step = chunk.step
        chunk.step += 1
        if self.direct:
            if step == 0:
                chunk.end = lax.psum(plus(chunk.own, chunk.moving), dp_axis)
            return
        got = after(chunk.moving, self.token)
        if step == 3:
            chunk.end = jax.tree.map(lambda full, far: jnp.where(self.middle, full, far), chunk.own, got)
            return
        chunk.own = self.token = plus(chunk.own, got)
        pairs = ([(0, 1), (3, 2)], [(1, 2), (2, 1)], [(1, 0), (2, 3)])[step]
        chunk.moving = jax.tree.map(lambda a: lax.ppermute(a, dp_axis, pairs), chunk.own)


def order_turns(chunks):
    lags = (0, 1.5, 2.5, 3.5)
    left = [(number + lags[step], step, number) for number, chunk in enumerate(chunks) for step in range(chunk.step, 4)]
    return [chunks[number] for _, _, number in sorted(left)]


def split_tiles(rows):
    size = rows // 32 * 16
    return [rows - size, size]


def cut(a, pieces):
    rows = a.shape[0] // pieces
    return [a[i * rows : (i + 1) * rows] for i in range(pieces)]


def padded_rows(a, rows):
    return jnp.pad(a, ((0, rows - a.shape[0]), (0, 0)))


def swap_weights(weights, start_after):
    size = lax.axis_size(dp_axis)
    odd = lax.axis_index(dp_axis) % 2
    results, gots = [], []
    for a in weights:
        a = after(a, start_after, *gots[: max(0, len(gots) - 1)])
        if size % 2:
            gots.append(swap_section(a))
            results.append(gots[-1])
            continue
        rows = a.shape[0] // 2
        got = swap_section(lax.dynamic_slice_in_dim(a, odd * rows, rows, 0))
        gots.append(got)
        other = lax.ppermute(got, dp_axis, [(i, i ^ 1) for i in range(size)])
        results.append(jnp.concatenate([jnp.where(odd == 0, got, other), jnp.where(odd == 0, other, got)], axis=0))
    return results


def route_mask(value_ids, out_ids, experts, memory_len):
    lane = jnp.arange(lanes, dtype=jnp.int32)[None, :]
    out_full = jnp.pad(out_ids, ((0, 0), (memory_len, 0)), constant_values=-1)
    hit = jnp.zeros((value_ids.shape[1], lanes), jnp.bool_)
    for k in range(value_ids.shape[0]):
        hit = hit | (lane == value_ids[k][:, None])
        hit = hit | ((lane == out_full[k][:, None] + out_lane) & (out_full[k][:, None] >= 0))
    return hit.astype(f32)


def on_device(
    inputs,
    memory,
    value_routes,
    out_routes,
    ln1_gain,
    ln1_bias,
    query_weight,
    key_weight,
    value_weight,
    value_router,
    out_router,
    output_weight,
    ln2_gain,
    ln2_bias,
    up_weight,
    up_bias,
    down_weight,
    down_bias,
    out_cot,
):
    experts = value_router.shape[-1]
    head_width = query_weight.shape[-1]
    sec = lax.axis_index(section_axis)
    head = lax.axis_index(head_axis)
    me = head.astype(jnp.int32).reshape(1)
    first = sec == 0
    pick = lambda a, index: lax.dynamic_index_in_dim(a, index, 0, keepdims=False)
    memory_len = memory.shape[2] * lax.axis_size(head_axis)

    value_rows = experts * head_width
    router_rows = [padded_rows(a[0, 0].T, out_lane) for a in (value_router, out_router)]
    kqr = jnp.concatenate([key_weight[0, 0].T, query_weight[0, 0].T, *router_rows])
    weights = [value_weight[0, 0].T, kqr, output_weight[0, 0], up_weight[0], down_weight[0]]

    small = jnp.concatenate([ln1_gain, ln1_bias, ln2_gain, ln2_bias, up_bias, down_bias, ln1_gain, ln1_bias], axis=0)
    route_rows = jnp.concatenate(
        [
            jnp.transpose(value_routes[0, :, :, 0, :], (0, 2, 1)),
            jnp.pad(jnp.transpose(out_routes[0, :, :, 0, :], (0, 2, 1)), ((0, 0), (0, 0), (memory_len, 0)), constant_values=-1),
        ],
        axis=1,
    )
    sends = [small, pick(memory[0], 1 - sec), pick(route_rows, 1 - sec)]
    small_got, memory_got, routes_got = [swap_section(a) for a in sends]

    def both_layers(own, got):
        return jnp.where(first, own, got), jnp.where(first, got, own)

    smalls = both_layers(small, small_got)
    route_sets = both_layers(pick(route_rows, sec), routes_got)
    memories = both_layers(pick(memory[0], sec), memory_got)
    weight_sets = [both_layers(a, got) for a, got in zip(weights, swap_weights(weights, sends))]

    x = pick(inputs, sec)
    cot = pick(out_cot, sec)
    own_norm = norm_only(x, smalls[0][0:1], smalls[0][1:2])
    slots = gather_slots(own_norm)
    route_sets = after(route_sets, own_norm)
    topk = value_routes.shape[-1]

    layers = []
    for number in range(2):
        layer = SimpleNamespace(mem=memories[number], w=[a[number] for a in weight_sets[:3]])
        layer.wu, layer.wd = [a[number] for a in weight_sets[3:]]
        vec = smalls[number]
        layer.gain1, layer.shift1, layer.gain2, layer.shift2, layer.up_b, layer.down_b = (vec[i : i + 1] for i in range(6))
        routes = route_sets[number]
        layer.mask = route_mask(routes[:topk], routes[topk:, memory_len:], experts, memory_len)
        layers.append(layer)
    one, two = layers
    no_add = jnp.zeros_like(one.gain1)
    for layer in layers:
        layer.mem_slots = gather_slots(norm_only(after(layer.mem, own_norm), layer.gain1, layer.shift1))
    cot_slots = gather_slots(after(cot, slots[2], one.mem_slots[2]))
    slots[3] = after(slots[3], one.mask, two.mask)

    def attention(layer, slots):
        *out, layer.normed, q, k, v, ev, gate, att, layer.mixed = attn_fwd(
            me, layer.mem_slots, slots, layer.w, layer.mask, experts, head_width
        )
        layer.saved = (q, k, v, ev, gate, att)
        if layer is one:
            out[3] = after(out[3], cot_slots[2], two.mem_slots[2])
        terms, _ = scatter_halves(out)
        layer.hidden, halves = [], []
        for part in range(2):
            hidden, normed = add_norm(layer.rows[part], terms[part], part, no_add, layer.gain2, layer.shift2, f32)
            layer.hidden.append(hidden)
            halves.append(send_half(normed))
        return [receive_half(half) for half in halves]

    one.rows = [x, x]
    halves = attention(one, slots)
    kept = ()
    two.rows, sent = [], []
    for part in range(2):
        pieces = halves[part]
        *out, n2, upper, active = ffn_fwd(pieces, part, one.wu, one.up_b, one.wd, kept)
        kept = (n2, upper, active)
        terms, _ = scatter_slots(out)
        rows, normed = add_norm(one.hidden[part], terms, part, one.down_b, two.gain1, two.shift1, bf16)
        two.rows.append(rows)
        sent.append(send_half(normed))
    one.n2, one.upper, one.active = kept
    sent = [receive_half(half) for half in sent]
    halves = attention(two, [half[slot] for slot in range(4) for half in sent])

    def by_layer(one, two):
        got = swap_section(jnp.where(first, two, one))
        kept = jnp.where(first, one, two)
        return jnp.stack([jnp.where(first, kept, got), jnp.where(first, got, kept)])[None]

    def send_chunks(one, two, sizes):
        start = 0
        for size in sizes:
            part_one, part_two = one[start : start + size], two[start : start + size]
            start += size
            send = jnp.where(first, part_two, part_one)
            if chunks:
                send = after(send, chunks[-1].moving)
            chunks.append(Chunk(jnp.where(first, part_one, part_two), swap_section(send)))

    chunks = []
    turns = Turns()
    for number in (1, 0):
        layer = layers[number]
        if number == 1:
            g_rows = [cot, cot]
        kept = ()
        terms, layer.bias = [], []
        for part in range(2):
            pieces = halves[part]
            if number == 1:
                *out, sums_here, g_all, upper_grad, n2, active = ffn_bwd(
                    cot_slots, part, layer.wd, layer.wu, kept, normed=pieces, bu=layer.up_b
                )
                kept = (g_all, upper_grad, n2, active)
            else:
                *out, sums_here, g_all, upper_grad = ffn_bwd(pieces, part, layer.wd, layer.wu, kept, upper=layer.upper)
                kept = (g_all, upper_grad)
                n2, active = layer.n2, layer.active
            layer.bias.append(sums_here)
            terms_here, token = scatter_slots(out)
            terms.append(terms_here)
        layer.down = t_dot(active, after(g_all, token)).astype(bf16)
        layer.up = t_dot(after(n2, token), upper_grad).astype(bf16)
        if number == 1:
            layer.up = after(layer.up, layer.down)
        if number == 0:
            quarter = layer.down.shape[0] // 4
            send_chunks(layer.down, two.down, [quarter, quarter, 2 * quarter])
            send_chunks(layer.up, two.up, [layer.up.shape[0] // 2] * 2)
        terms[1] = (*terms[1][0:2], after(terms[1][2], layer.up))
        hidden_grads, layer.small2, sent = [], [], []
        for part in range(2):
            dx, low, small_here = norm_back(layer.hidden[part], terms[part], part, layer.gain2, g_rows[part])
            hidden_grads.append(dx)
            layer.small2.append(small_here)
            sent.append(send_half(low))
        sent = [receive_half(half) for half in sent]
        slots = [half[slot] for slot in range(4) for half in sent]
        if number == 0:
            turns(chunks[0])
            slots[7] = after(slots[7], turns.token)
        else:
            down_out = dot(active, after(layer.wd, sent[1][2])).astype(bf16)
            rows = down_out.shape[0] // 8
            last_parts = [
                jnp.concatenate([down_out[s * rows : (s + 1) * rows], down_out[(4 + s) * rows : (5 + s) * rows]])
                for s in range(4)
            ]
            last_terms, _ = scatter_halves(last_parts, sent[1][2])
        *ngs, ngm, dproj, a_all = attn_bwd(me, slots, layer.w, layer.saved, experts, head_width)
        if number == 1:
            ngs[3] = after(ngs[3], [here[2] for here in last_terms])
            near, from_core, _ = last_terms[0]
            last_out = jnp.concatenate(layer.hidden) + layer.down_b + near.astype(f32) + from_core.astype(f32)
            last_out = (last_out + jnp.concatenate([here[2] for here in last_terms]).astype(f32)).astype(bf16)
            layer_out = by_layer(jnp.concatenate(layer.rows), last_out)
        terms, token = scatter_halves(ngs)
        layer.dproj, layer.a_all = dproj, a_all
        for here in (two, one) if number == 0 else ():
            here.attn = attn_grads(after(here.dproj, token), here.normed, here.mixed, here.a_all, experts, head_width)
            token = here.attn
        if number == 0:
            pack = (experts + 2) * head_width + 2 * out_lane
            send_chunks(layer.attn, two.attn, split_tiles(pack) + split_tiles(value_rows))
            turns.token = layer.attn
            turns(chunks[0], chunks[1])
            token = turns.token
        if number == 0:
            terms[1] = (*terms[1][0:2], after(terms[1][2], token))
        rows_grads, low_grads, layer.small1, halves = [], [], [], []
        for part in range(2):
            here = in_order(terms[part], halves)
            dx, low, small_here = norm_back(layer.rows[part], here, part, layer.gain1, hidden_grads[part])
            rows_grads.append(dx)
            low_grads.append(low)
            layer.small1.append(small_here)
            halves.append(send_half(low) if number == 1 else (low,))
        if number == 1:
            halves = [receive_half(half) for half in halves]
        g_rows = low_grads
        layer.mem_grads = cut(ngm, 4)
        layer.input_grad = jnp.concatenate(low_grads)

    mem_terms, _ = scatter_slots([jnp.concatenate(pair) for pair in zip(one.mem_grads, two.mem_grads)])
    rows = one.mem.shape[0]
    vecs = []
    for number, layer in enumerate(layers):
        small_mem = norm_back_small(layer.mem, [a[number * rows : (number + 1) * rows] for a in mem_terms])
        vecs.append((layer.small1[0] + layer.small1[1] + small_mem)[0:2])
        vecs.append((layer.small2[0] + layer.small2[1])[0:6])
    vec = jnp.concatenate(vecs)
    vec = vec + to_core(vec)
    vec = vec + to_chip(vec)
    vecs = [
        jnp.concatenate([part[0:5], layer.bias[0] + layer.bias[1], part[6:8]]) for part, layer in zip(cut(vec, 2), layers)
    ]
    down0, down1, down2, up0, up1, pack0, pack1, out0, out1 = chunks
    pack1.own = (pack1.own, jnp.where(first, vecs[0], vecs[1]))
    pack1.moving = (pack1.moving, swap_section(jnp.where(first, vecs[1], vecs[0])))
    for chunk in order_turns(chunks):
        turns(chunk)
        if chunk is out1 and chunk.step == 1:
            last_sum = turns.token
    pack_end, vec = pack1.end
    input_grad = by_layer(*[after(layer.input_grad, last_sum) for layer in layers])
    join = lambda *parts: jnp.concatenate(parts).astype(f32)
    pack_sum = join(pack0.end, pack_end)

    def take(start, count):
        return pack_sum[start : start + count].T[None, None]

    keys = value_rows + 2 * out_lane

    return (
        layer_out,
        input_grad,
        vec[0:1],
        vec[1:2],
        take(keys + head_width, head_width),
        take(keys, head_width),
        take(0, value_rows),
        take(value_rows, experts),
        take(value_rows + out_lane, experts),
        join(out0.end, out1.end)[None, None],
        vec[2:3],
        vec[3:4],
        join(up0.end, up1.end)[None],
        vec[5:6],
        join(down0.end, down1.end, down2.end)[None],
        vec[4:5],
    )


def solution(mesh):
    rows = P(dp_axis, head_axis, None)
    layer_rows = P(section_axis, dp_axis, head_axis, None)
    routes = P(section_axis, dp_axis, None, head_axis, None)
    by_layer = P(section_axis, None)
    by_head = P(section_axis, head_axis, None, None)
    up, up_shift, down = P(section_axis, None, head_axis), P(section_axis, head_axis), P(section_axis, head_axis, None)
    params = [by_layer] * 2 + [by_head] * 6 + [by_layer] * 2 + [up, up_shift, down, by_layer]
    return jax.shard_map(
        on_device,
        mesh=mesh,
        in_specs=(rows, layer_rows, routes, routes, *params, rows),
        out_specs=(layer_rows, layer_rows, *params),
        check_vma=False,
    )
```
